32 devices in a mesh: section: 2 (over y), dp: 16 (over z, x, core).
Axes of the slice: x: 2, y: 2, z: 4, core: 2. Of those that a mesh axis runs over, the one named last changes fastest.
Arguments:
- queries: bfloat16 [4096, 3584], P(('section', 'dp')), may hold values from -1 to 1
- passages: bfloat16 [128, 16, 3584], P('dp'), may hold values from -1 to 1
- candidates: int32 [32, 3], P('section'), may hold values from 0 to 15, as said below
- counts: int32 [32], P('section'), may hold values from 1 to 3, 64 in all
- teacher: float32 [4096, 384], P(('section', 'dp')), may hold values from -20 to 450
- section_weights: bfloat16 [2, 3584, 3584], P('section', 'dp'), may hold values from -0.09375 to 0.09375
- section_inputs: bfloat16 [2, 16, 3584], P('section', None, 'dp'), may hold values from -1.5 to 1.5
- pre_acts: bfloat16 [2, 16, 3584], P('section', None, 'dp'), may hold values from -8 to 8
Outputs:
- query_grads: bfloat16 [4096, 3584], P(('section', 'dp'))
- passage_grads: bfloat16 [128, 16, 3584], P('dp')
- grad_inputs: float32 [2, 16, 3584], P('section', None, 'dp')
- weight_grads: bfloat16 [2, 3584, 3584], P('section', 'dp')
The draws below stay inside these ranges and needn't reach their ends.
Inputs may be any that keep to these rules, and one draw needn't show every extreme that they name: `candidates`: each row names 3 different passage blocks. A query block uses the first counts[b] entries of its row of candidates.
All inputs are finite; a program needn't handle non-finite values.
Results may differ from the reference program's by a relative error of at most 0.0085.
Values may be sent and summed in bfloat16 or wider, within the bound.
A program may use at most 64 MiB of HBM per device.

```python
import math
import jax
import jax.numpy as jnp
import numpy as np
from jax import lax

D = 3584
BLOCK = 128
C_MAX = 3
QB_DEV = 1
MB_DEV = 1
NQB = 32
NQ = 4096
NPB = 16
M = 16
N_SECTION = 2
N_DP = 16


def embed_scale():
    return 0.387 * float(D) ** (-0.25)


def passage_row(key, row_pos, block_pos):
    inner_key = jax.random.fold_in(jax.random.fold_in(jax.random.fold_in(key, 301), row_pos), block_pos)
    return jax.random.truncated_normal(inner_key, -6.0, 6.0, (D,), jnp.float32) * embed_scale()


def row_block_count(key, row_pos):
    blocks = jnp.arange(NPB, dtype=jnp.int32)
    return jax.vmap(lambda block_pos: passage_row(key, row_pos, block_pos))(blocks)


def passage_table(key):
    rows = jnp.arange(BLOCK, dtype=jnp.int32)
    return jax.vmap(lambda row_pos: row_block_count(key, row_pos))(rows)


def candidate_table(key):
    weight_matrices = jax.random.randint(jax.random.fold_in(key, 401), (NPB,), 1, 5)
    draws = jax.random.randint(jax.random.fold_in(key, 402), (NQB, NPB), 0, 4096)
    ranks = jnp.arange(NPB, dtype=jnp.int32)
    row_ids = jnp.arange(NQB, dtype=jnp.int32)[:, None]
    scores = draws * weight_matrices[None, :] * NPB + ranks[None, :]
    scores = scores + jnp.where((row_ids == 0) & (ranks[None, :] == NPB - 1), 1 << 29, 0)
    scores = scores + jnp.where((row_ids == 1) & (ranks[None, :] == 0), 1 << 29, 0)
    return lax.top_k(scores, C_MAX)[1].astype(jnp.int32)


def draw_candidates(key, part):
    return candidate_table(key)


def draw_passages(key, part):
    table = passage_table(key)
    return jnp.clip(table, -1.0, 1.0).astype(jnp.bfloat16)


def draw_queries(key, part):
    values = jax.random.truncated_normal(jax.random.fold_in(key, 601), -6.0, 6.0, (NQ, D), jnp.float32)
    values = values * embed_scale()
    return jnp.clip(values, -1.0, 1.0).astype(jnp.bfloat16)


def draw_teacher(key, part):
    values = jax.random.truncated_normal(jax.random.fold_in(key, 703), -6.0, 6.0, (NQ, C_MAX * BLOCK), jnp.float32) * 3.0
    return values.astype(jnp.float32)


def level_of(key, extent, split, least, largest):
    factor_of, own = 1.0, jax.random.fold_in(key, 6)
    for axis_at, blocks in split:
        steps = jnp.exp(jax.random.uniform(jax.random.fold_in(own, axis_at), (blocks,), jnp.float32, least / len(split), largest / len(split)))
        factor_of = factor_of * jnp.repeat(steps, extent[axis_at] // blocks).reshape([-1 if axis == axis_at else 1 for axis in range(len(extent))])
    return factor_of


def length_profile(amount, total, limit, skew):
    loads = [(1 << 20) // math.isqrt(rank ** skew) + 1 for rank in range(2, amount + 1)]
    surplus, given = total - limit - (amount - 1), [1] * (amount - 1)
    while surplus > 0:
        free = [i for i in range(amount - 1) if given[i] < limit]
        mass, budget = sum([loads[i] for i in free]), surplus
        for i in free:
            more = min(limit - given[i], max(1, budget * loads[i] // mass), surplus)
            given[i] = given[i] + more
            surplus = surplus - more
    return np.array([limit] + given)


def ragged(key, amount, total, reach, slope):
    if amount == 2:
        one = jax.random.randint(key, (), max(1, total - reach), min(reach, total - 1) + 1)
        return jnp.stack([one, total - one])
    sizes = jnp.asarray(length_profile(amount, total, reach, slope), jnp.int32)
    couples = (amount - 1) // 2
    giver, sink = sizes[1:1 + 2 * couples:2], sizes[2:2 + 2 * couples:2]
    slack = jnp.minimum(giver - 1, reach - sink)
    moved = jax.random.randint(jax.random.fold_in(key, 1), (couples,), 0, 1 << 20) % (slack + 1)
    sizes = sizes.at[1:1 + 2 * couples:2].set(giver - moved).at[2:2 + 2 * couples:2].set(sink + moved)
    return sizes[jax.random.permutation(jax.random.fold_in(key, 2), amount)]


def gaussian(rng, shape, scale, limit, cuts=(), kind=jnp.bfloat16):
    drawn = jax.random.normal(rng, shape, jnp.float32) * scale
    if len(cuts) > 0:
        drawn = level_of(rng, shape, cuts, -0.22, 0.18) * drawn
    return jnp.clip(drawn, min=-limit, max=limit).astype(kind)


def setup_inputs(seed: int = 0) -> dict:
    seeds = jax.random.split(jax.random.key(seed), 9)
    return {
        "queries": draw_queries(jax.random.fold_in(seeds[8], 71), 0),
        "passages": draw_passages(jax.random.fold_in(seeds[8], 71), 0),
        "candidates": draw_candidates(jax.random.fold_in(seeds[8], 71), 0),
        "counts": ragged(seeds[3], NQB, 2 * NQB, C_MAX, 2).astype(jnp.int32),
        "teacher": draw_teacher(jax.random.fold_in(seeds[8], 71), 0),
        "section_weights": gaussian(seeds[5], (N_SECTION, D, D), D ** -0.5, 0.09375, ((0, 2), (1, 16))),
        "section_inputs": gaussian(seeds[6], (N_SECTION, M, D), 0.25, 1.5, ((0, 2), (2, 16))),
        "pre_acts": gaussian(seeds[7], (N_SECTION, M, D), 1.5, 8.0, ((0, 2), (2, 16))),
    }


INVERSE_TEMP = 20.0


def soft_weights(logits, valid):
    masked = jnp.where(valid, logits, -1e30)
    highest = jnp.max(masked, axis=-1, keepdims=True)
    expons = jnp.where(valid, jnp.exp(masked - highest), 0.0)
    return expons / jnp.sum(expons, axis=-1, keepdims=True)


def reference(queries, passages, candidates, counts, teacher, section_weights, section_inputs, pre_acts):
    query_blocks = queries.reshape(NQB, BLOCK, D)
    teacher_blocks = teacher.reshape(NQB, BLOCK, C_MAX * BLOCK)
    slot_index = jnp.arange(C_MAX, dtype=jnp.int32)

    def one_block(dense, item):
        query_row_items, teacher_rows, chosen, how_many = item
        pulled_rows = jnp.take(passages, chosen, axis=1)
        columns = jnp.transpose(pulled_rows, (1, 0, 2)).reshape(C_MAX * BLOCK, D)
        logits = jnp.dot(query_row_items, columns.T, preferred_element_type=jnp.float32) * INVERSE_TEMP
        valid = jnp.repeat(slot_index < how_many, BLOCK)[None, :]
        weight_matrices = (soft_weights(logits, valid) - soft_weights(teacher_rows, valid)).astype(jnp.bfloat16)
        query_sums = jnp.dot(weight_matrices, columns, preferred_element_type=jnp.float32) * INVERSE_TEMP
        passage_sums = jnp.dot(weight_matrices.T, query_row_items, preferred_element_type=jnp.float32) * INVERSE_TEMP
        rounded = lax.optimization_barrier(passage_sums.astype(jnp.bfloat16))
        passage_sums = rounded.astype(jnp.float32)
        passage_sums = jnp.transpose(passage_sums.reshape(C_MAX, BLOCK, D), (1, 0, 2))
        dense = dense.at[:, chosen, :].add(passage_sums)
        return dense, (query_sums.astype(jnp.bfloat16), query_sums[:MB_DEV])

    start_dense = jnp.zeros((BLOCK, NPB, D), jnp.float32)
    dense, (query_grads, micro_rows) = lax.scan(
        one_block, start_dense, (query_blocks, teacher_blocks, candidates, counts))
    top = micro_rows.reshape(N_SECTION, N_DP, QB_DEV, MB_DEV, D)[N_SECTION - 1, :, 0].reshape(N_DP * MB_DEV, D)

    cotangent = top
    input_grads = []
    weight_list = []
    for section_pos in range(N_SECTION - 1, -1, -1):
        pre = pre_acts[section_pos].astype(jnp.float32)
        sigma = jax.nn.sigmoid(pre)
        inner = (cotangent * (sigma * (1.0 + pre * (1.0 - sigma)))).astype(jnp.bfloat16)
        weight_list.append(
            jnp.dot(section_inputs[section_pos].T, inner, preferred_element_type=jnp.float32).astype(jnp.bfloat16))
        cotangent = cotangent + jnp.dot(inner, section_weights[section_pos].T, preferred_element_type=jnp.float32)
        input_grads.append(cotangent)
    return (query_grads.reshape(NQ, D), dense.astype(jnp.bfloat16),
            jnp.stack(input_grads[::-1]), jnp.stack(weight_list[::-1]))
```

```python
import functools

import jax
import jax.numpy as jnp
from jax import lax
from jax.experimental import pallas as pl
from jax.experimental.pallas import tpu as pltpu
from jax.sharding import PartitionSpec as P

INVERSE_TEMP = 20.0


def passed_along(value, axis, steps):
    count = lax.axis_size(axis)
    initial, last = (max(0, -steps), min(count, count - steps))
    return lax.ppermute(value, axis, [(source, source + steps) for source in range(initial, last)])


def soft_weights(logits, valid):
    masked = jnp.where(valid, logits, -1e30)
    highest = jnp.max(masked, axis=-1, keepdims=True)
    expons = jnp.where(valid, jnp.exp(masked - highest), 0.0)
    return expons / jnp.sum(expons, axis=-1, keepdims=True)


def general_body(queries, passages, candidates, counts, teacher, section_weights, section_inputs, pre_acts):
    dp_count = lax.axis_size("dp")
    dp_index = lax.axis_index("dp")
    stripe, block_total, width = passages.shape
    row_block_count = stripe * dp_count
    blocks_here = candidates.shape[0] // dp_count
    slot_count = candidates.shape[1]
    requests = blocks_here * slot_count
    all_slots = candidates.reshape(-1)
    outgoing = jnp.take(passages, all_slots, axis=1)
    pulled_rows = lax.all_to_all(outgoing, "dp", split_axis=1, concat_axis=0, tiled=True)
    pulled_rows = pulled_rows.reshape(row_block_count, blocks_here, slot_count, width)
    own_counts = lax.dynamic_slice_in_dim(counts, dp_index * blocks_here, blocks_here)
    slot_valid = jnp.arange(slot_count, dtype=jnp.int32)[None, :] < own_counts[:, None]
    column_valid = jnp.repeat(slot_valid, row_block_count, axis=1)[:, None, :]
    query_row_items = queries.reshape(blocks_here, row_block_count, width)
    logits = (
        jnp.einsum(
            "ixp,wifp->ixfw", query_row_items, pulled_rows, preferred_element_type=jnp.float32
        )
        * INVERSE_TEMP
    )
    logits = logits.reshape(blocks_here, row_block_count, slot_count * row_block_count)
    target_logits = soft_weights(
        teacher.reshape(blocks_here, row_block_count, slot_count * row_block_count), column_valid
    )
    weight_matrices = (soft_weights(logits, column_valid) - target_logits).astype(jnp.bfloat16)
    weight_matrices = weight_matrices.reshape(
        blocks_here, row_block_count, slot_count, row_block_count
    )
    query_sums = (
        jnp.einsum(
            "geal,lgay->gey", weight_matrices, pulled_rows, preferred_element_type=jnp.float32
        )
        * INVERSE_TEMP
    )
    passage_sums = (
        jnp.einsum(
            "fnyw,fnj->wfyj", weight_matrices, query_row_items, preferred_element_type=jnp.float32
        )
        * INVERSE_TEMP
    )
    block_terms = passage_sums.reshape(row_block_count, requests, width).astype(jnp.bfloat16)
    micro_count = section_inputs.shape[1] // dp_count
    col_width = width // dp_count
    micro_cols = jnp.transpose(
        query_sums[0, :micro_count].reshape(micro_count, dp_count, col_width), (1, 0, 2)
    )
    incoming_piece = lax.all_to_all(block_terms, "dp", split_axis=0, concat_axis=1, tiled=True)
    entry = lax.all_to_all(micro_cols, "dp", split_axis=0, concat_axis=1, tiled=True)
    onehot = (all_slots[:, None] == jnp.arange(block_total, dtype=jnp.int32)[None, :]).astype(
        jnp.float32
    )
    dense = jnp.einsum(
        "sjd,jn->snd",
        incoming_piece.astype(jnp.float32),
        onehot,
        precision=lax.Precision.HIGHEST,
        preferred_element_type=jnp.float32,
    )
    passage_out = lax.psum(dense, "section").astype(jnp.bfloat16)
    weight_rows = section_weights[0]
    input_cols = section_inputs[0]
    pre = pre_acts[0].astype(jnp.float32)
    sigma = jax.nn.sigmoid(pre)
    slope = sigma * (1.0 + pre * (1.0 - sigma))
    carry = entry.reshape(dp_count * micro_count, col_width)
    section_count = lax.axis_size("section")
    section_index = lax.axis_index("section")
    grad_cols = jnp.zeros_like(carry)
    grad_weight = jnp.zeros((col_width, width), jnp.float32)
    for section_turn in range(section_count):
        active_flag = section_count - 1 - section_turn
        inner = (carry * slope).astype(jnp.bfloat16)
        piece = lax.all_gather(inner, "dp", axis=1, tiled=True)
        back_sum = jnp.einsum("mj,ij->mi", piece, weight_rows, preferred_element_type=jnp.float32)
        weight_part = jnp.einsum("mi,mj->ij", input_cols, piece, preferred_element_type=jnp.float32)
        back_sum, layer_weight = (back_sum, weight_part)
        updated = carry + back_sum
        is_active = section_index == active_flag
        grad_cols = jnp.where(is_active, updated, grad_cols)
        grad_weight = jnp.where(is_active, layer_weight, grad_weight)
        if section_turn + 1 < section_count:
            carry = passed_along(updated, "section", -1)
    return (
        query_sums.reshape(blocks_here * row_block_count, width).astype(jnp.bfloat16),
        passage_out,
        grad_cols[None],
        grad_weight[None].astype(jnp.bfloat16),
    )


PLANE = 8
GROUP = 4


def cells(width, ref, index):
    return ref.at[:, :, pl.ds(pl.multiple_of(index * width, width), width)]


def relay_kernel(
    q_ref, p_ref, cand_ref, teacher_ref, w_ref, inp_ref, pre_ref,
    qg_ref, pg_ref, gi_ref, wg_ref,
    candx, shard, up_in, down_in, sel, sel_t, stage, cols, target, terms, tin,
    up_out, up_sum, down_out, down_sum, fin, final_in, prebuf, topbuf, cbuf, cot,
    cand_s, cand_r, half_s, half_r, line_s, line_r, pull_s, pull_r, push_s, push_r,
    sum_s, sum_r, fin_s, fin_r, pre_s, pre_r, top_s, top_r, cot_s, cot_r,
):
    dp_count = lax.axis_size("dp")
    section = lax.axis_index("section")
    dp = lax.axis_index("dp")
    z = dp // GROUP
    x = (dp // 2) % 2
    core = dp % 2
    me = x * 4 + section * 2 + core
    quarter = section * 2 + core
    z_count = dp_count // GROUP
    stripe, block_total, width = p_ref.shape
    part = width // 4
    rows = 2 * stripe
    block = q_ref.shape[0]
    slots = teacher_ref.shape[1] // block
    col = inp_ref.shape[1]
    micro = inp_ref.shape[0]
    f32, bf16 = jnp.float32, jnp.bfloat16

    def remote(source, dest, send, recv, device):
        return pltpu.make_async_remote_copy(
            src_ref=source, dst_ref=dest, send_sem=send, recv_sem=recv,
            device_id=device, device_id_type=pl.DeviceIdType.MESH,
        )

    def member(g):
        return ((g // 2) % 2, z * GROUP + (g // 4) * 2 + g % 2)

    def others(count, own, act):
        def step(i, carry):
            @pl.when(i != own)
            def _():
                act(i)
            return carry
        lax.fori_loop(0, count, step, 0)

    barrier = pltpu.get_barrier_semaphore()
    everyone = 2 * dp_count

    def greet(i):
        pl.semaphore_signal(
            barrier, inc=1, device_id=(i // dp_count, i % dp_count),
            device_id_type=pl.DeviceIdType.MESH,
        )

    others(everyone, section * dp_count + dp, greet)
    pl.semaphore_wait(barrier, everyone - 1)

    cand_copy = remote(cand_ref, candx, cand_s.at[0], cand_r.at[0], (1 - section, dp))
    cand_copy.start()
    partner = dp + 1 - 2 * core
    half_copy = remote(
        cells(part, p_ref, section * 2 + 1 - core), shard.at[pl.ds(core * stripe, stripe)],
        half_s.at[0], half_r.at[0], (section, partner),
    )
    half_copy.start()
    shard[pl.ds(core * stripe, stripe)] = p_ref[
        :, :, pl.ds(pl.multiple_of(quarter * part, part), part)
    ]
    half_wait = remote(
        cells(part, p_ref, quarter), shard.at[pl.ds((1 - core) * stripe, stripe)],
        half_s.at[0], half_r.at[0], (section, partner),
    )
    half_wait.wait_recv()

    def line_copy(source, ref, sems, h, step):
        return remote(source, ref.at[h], line_s.at[sems, h], line_r.at[sems, h], (section, dp + step * GROUP))

    @pl.when(z < z_count - 1)
    def _():
        line_copy(shard, up_in, 0, 0, 1).start()

    @pl.when(z > 0)
    def _():
        line_copy(shard, down_in, 1, 0, -1).start()

    cand_copy.wait_recv()
    pieces = []
    for g in range(PLANE):
        at = z * GROUP + (g // 4) * 2 + g % 2
        mine = cand_ref[pl.ds(at, 1), :]
        away = candx[pl.ds(at, 1), :]
        row = jnp.where(section == (g // 2) % 2, mine, away)
        pieces.append(jnp.broadcast_to(row.astype(f32), (slots * rows, row.shape[1])))
    listed = jnp.concatenate(pieces, axis=0)
    total = PLANE * slots * rows
    slot_of = (lax.broadcasted_iota(jnp.int32, listed.shape, 0) // rows) % slots
    lane = lax.broadcasted_iota(jnp.int32, listed.shape, 1)
    wanted = jnp.sum(jnp.where(lane == slot_of, listed, 0.0), axis=1, keepdims=True)
    shape = (total, rows * block_total)
    row_of = lax.broadcasted_iota(jnp.int32, shape, 0) % rows
    place = lax.broadcasted_iota(jnp.int32, shape, 1)
    hit = (place // block_total == row_of) & ((place % block_total).astype(f32) == wanted)
    onehot = jnp.where(hit, 1.0, 0.0)
    sel[...] = onehot.astype(bf16)
    sel_t[...] = jnp.transpose(onehot).astype(bf16)

    def own_rows(zs, at_x):
        return pl.ds(pl.multiple_of(zs * GROUP * stripe + at_x * rows, rows), rows)

    def pull_copy(zs, g):
        return remote(
            stage.at[zs, g], cols.at[quarter, :, own_rows(zs, x), :],
            pull_s.at[zs, g], pull_r.at[zs, me], member(g),
        )

    def pull_wait(zs, g):
        return remote(
            stage.at[zs, g], cols.at[g % 4, :, own_rows(zs, g // 4), :],
            pull_s.at[zs, g], pull_r.at[zs, g], member(g),
        )

    def spread(ref, zs):
        picked = jnp.dot(
            sel[...], ref[...].reshape(rows * block_total, part), preferred_element_type=f32
        )
        stage[zs] = picked.astype(bf16).reshape(PLANE, slots, rows, part)
        others(PLANE, me, lambda g: pull_copy(zs, g).start())
        cols[quarter, :, own_rows(zs, x), :] = stage[zs, me]

    spread(shard, z)

    prebuf[dp, :, :] = pre_ref[...]

    def pre_copy(j):
        return remote(prebuf.at[dp], prebuf.at[dp], pre_s.at[j], pre_r.at[dp], (section, j))

    others(dp_count, dp, lambda j: pre_copy(j).start())

    def soft(values, valid):
        masked = jnp.where(valid, values, -1e30)
        highest = jnp.max(masked, axis=-1, keepdims=True)
        expons = jnp.where(valid, jnp.exp(masked - highest), 0.0)
        return expons / jnp.sum(expons, axis=-1, keepdims=True)

    own_row = cand_ref[pl.ds(dp, 1), :].astype(f32)
    own_lane = lax.broadcasted_iota(jnp.int32, own_row.shape, 1)
    how_many = jnp.sum(jnp.where(own_lane == slots, own_row, 0.0), axis=1, keepdims=True)
    slot_lane = lax.broadcasted_iota(jnp.int32, teacher_ref.shape, 1) // block
    valid = slot_lane.astype(f32) < how_many
    target[...] = soft(teacher_ref[...], valid)

    for h in range(z_count - 1):
        @pl.when(z >= h + 1)
        def _():
            line_copy(shard, up_in, 0, h, -1).wait_recv()
            if h + 1 < z_count - 1:
                @pl.when(z < z_count - 1)
                def _():
                    line_copy(up_in.at[h], up_in, 0, h + 1, 1).start()

        @pl.when(z + h + 1 < z_count)
        def _():
            line_copy(shard, down_in, 1, h, 1).wait_recv()
            if h + 1 < z_count - 1:
                @pl.when(z > 0)
                def _():
                    line_copy(down_in.at[h], down_in, 1, h + 1, -1).start()

        @pl.when(z >= h + 1)
        def _():
            spread(up_in.at[h], z - h - 1)

        @pl.when(z + h + 1 < z_count)
        def _():
            spread(down_in.at[h], z + h + 1)

    for zs in range(z_count):
        others(PLANE, me, lambda g: pull_wait(zs, g).wait_recv())

    contract_last = (((1,), (1,)), ((), ()))
    contract_first = (((0,), (0,)), ((), ()))
    logits = jnp.zeros((block, slots * block), f32)
    for f in range(4):
        logits += lax.dot_general(
            q_ref[:, f * part:(f + 1) * part], cols[f].reshape(slots * block, part),
            contract_last, preferred_element_type=f32,
        )
    weights32 = soft(logits * INVERSE_TEMP, valid) - target[...]
    weights = weights32.astype(bf16)
    weights_t = jnp.transpose(weights32).astype(bf16)
    for f in range(4):
        sums = jnp.dot(weights, cols[f].reshape(slots * block, part), preferred_element_type=f32)
        sums = sums * INVERSE_TEMP
        qg_ref[:, f * part:(f + 1) * part] = sums.astype(bf16)
        topbuf[dp, :, f * part:(f + 1) * part] = sums[0:1]

    def top_copy(j):
        return remote(topbuf.at[dp], topbuf.at[dp], top_s.at[j], top_r.at[dp], (section, j))

    @pl.when(section == 1)
    def _():
        others(dp_count, dp, lambda j: top_copy(j).start())

    for f in range(4):
        sums = jnp.dot(
            weights_t, q_ref[:, f * part:(f + 1) * part], preferred_element_type=f32
        )
        terms[f] = (sums * INVERSE_TEMP).astype(bf16).reshape(slots, block, part)

    def push_copy(zt, g):
        return remote(
            terms.at[g % 4, :, own_rows(zt, g // 4), :], tin.at[zt, me],
            push_s.at[zt, g], push_r.at[zt, me], member(g),
        )

    def push_wait(zt, g):
        return remote(
            terms.at[quarter, :, own_rows(zt, x), :], tin.at[zt, g],
            push_s.at[zt, g], push_r.at[zt, g], member(g),
        )

    def push(zt):
        others(PLANE, me, lambda g: push_copy(zt, g).start())
        tin[zt, me] = terms[quarter, :, own_rows(zt, x), :]

    for h in range(z_count - 1, 0, -1):
        @pl.when(z + h < z_count)
        def _():
            push(z + h)

        @pl.when(z >= h)
        def _():
            push(z - h)

    push(z)

    def cot_copy(j):
        return remote(cbuf.at[dp], cbuf.at[dp], cot_s.at[j], cot_r.at[dp], (1 - section, j))

    def layer(own):
        others(dp_count, dp, lambda j: remote(
            prebuf.at[j], prebuf.at[j], pre_s.at[j], pre_r.at[j], (section, j)).wait_recv())
        pre = jnp.concatenate([prebuf[j].astype(f32)[:, :col] for j in range(dp_count)], axis=1)
        sigma = 1.0 / (1.0 + jnp.exp(-pre))
        slope = sigma * (1.0 + pre * (1.0 - sigma))
        inner = (cot[...] * slope).astype(bf16)
        back = lax.dot_general(inner, w_ref[...], contract_last, preferred_element_type=f32)
        updated = own + back
        gi_ref[...] = updated
        inner_parts = [(f, inner[:, f * part:(f + 1) * part]) for f in range(4)]

        def outer():
            for f, piece in inner_parts:
                wg_ref[:, f * part:(f + 1) * part] = lax.dot_general(
                    inp_ref[...], piece, contract_first, preferred_element_type=f32
                ).astype(bf16)

        return updated, outer

    @pl.when(section == 1)
    def _():
        others(dp_count, dp, lambda j: remote(
            topbuf.at[j], topbuf.at[j], top_s.at[j], top_r.at[j], (section, j)).wait_recv())
        own = jnp.zeros((micro, col), f32)
        for j in range(dp_count):
            cot[j:j + 1, :] = topbuf[j]
        for j in range(dp_count):
            own = jnp.where(dp == j, cot[:, j * col:(j + 1) * col], own)
        updated, outer = layer(own)
        cbuf[dp, :, :col] = updated
        others(dp_count, dp_count, lambda j: cot_copy(j).start())
        outer()

    def summed(zt):
        others(PLANE, me, lambda g: push_wait(zt, g).wait_recv())
        return jnp.dot(
            sel_t[...], tin[zt].reshape(total, part), preferred_element_type=f32
        )

    def sum_copy(source, dest, sems, h, step):
        return remote(
            source.at[h], dest.at[h], sum_s.at[sems, h], sum_r.at[sems, h],
            (section, dp + step * GROUP),
        )

    def line_sum(h, zt, step, sems, out, incoming, beyond):
        value = summed(zt)
        fin_shape = (rows, block_total, part)
        out[h - 1] = value.astype(bf16).reshape(fin_shape)
        if h < z_count - 1:
            @pl.when(beyond)
            def _():
                sum_copy(out, incoming, sems, h, -step).wait_recv()
                out[h - 1] = (value.reshape(fin_shape) + incoming[h].astype(f32)).astype(bf16)
        sum_copy(out, incoming, sems, h - 1, step).start()

    for h in range(z_count - 1, 0, -1):
        @pl.when(z + h < z_count)
        def _():
            line_sum(h, z + h, 1, 0, up_out, up_sum, z > 0)

        @pl.when(z >= h)
        def _():
            line_sum(h, z - h, -1, 1, down_out, down_sum, z < z_count - 1)

    value = summed(z).reshape(rows, block_total, part)

    zero = jnp.zeros_like(value)
    fin_acc = cot_like = None
    @pl.when(z > 0)
    def _():
        sum_copy(up_out, up_sum, 0, 0, -1).wait_recv()

    @pl.when(z < z_count - 1)
    def _():
        sum_copy(down_out, down_sum, 1, 0, 1).wait_recv()

    below = jnp.where(z > 0, up_sum[0].astype(f32), zero)
    above = jnp.where(z < z_count - 1, down_sum[0].astype(f32), zero)
    fin[...] = (value + below + above).astype(bf16)

    def fin_copy(i):
        return remote(
            fin.at[pl.ds((i % 2) * stripe, stripe)], final_in.at[quarter],
            fin_s.at[i], fin_r.at[quarter], (i // 2, z * GROUP + x * 2 + i % 2),
        )

    def fin_wait(i):
        return remote(
            fin.at[pl.ds(core * stripe, stripe)], final_in.at[i],
            fin_s.at[i], fin_r.at[i], (i // 2, z * GROUP + x * 2 + i % 2),
        )

    others(4, quarter, lambda i: fin_copy(i).start())
    final_in[quarter] = fin[pl.ds(core * stripe, stripe)]

    @pl.when(section == 0)
    def _():
        def wait(j, carry):
            remote(cbuf.at[j], cbuf.at[j], cot_s.at[j], cot_r.at[j], (1 - section, j)).wait_recv()
            return carry
        lax.fori_loop(0, dp_count, wait, 0)
        cot[...] = jnp.concatenate([cbuf[j][:, :col] for j in range(dp_count)], axis=1)
        updated, outer = layer(cbuf[dp][:, :col])
        outer()

    others(4, quarter, lambda i: fin_wait(i).wait_recv())
    for f in range(4):
        pg_ref[:, :, f * part:(f + 1) * part] = final_in[f]

    cand_copy.wait_send()
    half_copy.wait_send()
    for h in range(z_count - 1):
        @pl.when((z >= h) & (z < z_count - 1))
        def _():
            line_copy(up_in.at[h], up_in, 0, h, 1).wait_send()

        @pl.when((z + h < z_count) & (z > 0))
        def _():
            line_copy(down_in.at[h], down_in, 1, h, -1).wait_send()

        @pl.when(z + h + 1 < z_count)
        def _():
            sum_copy(up_out, up_sum, 0, h, 1).wait_send()

        @pl.when(z >= h + 1)
        def _():
            sum_copy(down_out, down_sum, 1, h, -1).wait_send()

    for zs in range(z_count):
        others(PLANE, me, lambda g: pull_copy(zs, g).wait_send())
        others(PLANE, me, lambda g: push_copy(zs, g).wait_send())
    others(dp_count, dp, lambda j: pre_copy(j).wait_send())

    @pl.when(section == 1)
    def _():
        others(dp_count, dp, lambda j: top_copy(j).wait_send())
        others(dp_count, dp_count, lambda j: cot_copy(j).wait_send())

    others(4, quarter, lambda i: fin_copy(i).wait_send())


def plane_body(queries, passages, candidates, counts, teacher, section_weights, section_inputs, pre_acts):
    dp_count = lax.axis_size("dp")
    z_count = dp_count // GROUP
    stripe, block_total, width = passages.shape
    block = queries.shape[0]
    slots = candidates.shape[1]
    part = width // 4
    rows = 2 * stripe
    micro, col = section_inputs.shape[1:]
    wide = -(-col // 128) * 128
    f32, bf16, i32 = jnp.float32, jnp.bfloat16, jnp.int32
    table = jnp.concatenate([candidates, counts[:, None]], axis=1)
    table = jnp.pad(table, ((0, 0), (0, 128 - slots - 1)))
    pre = jnp.pad(pre_acts[0], ((0, 0), (0, wide - col)))
    vmem, dma = pltpu.VMEM, pltpu.SemaphoreType.DMA
    hop = z_count - 1
    scratch = [
        vmem(table.shape, i32),
        vmem((rows, block_total, part), bf16),
        vmem((hop, rows, block_total, part), bf16),
        vmem((hop, rows, block_total, part), bf16),
        vmem((PLANE * slots * rows, rows * block_total), bf16),
        vmem((rows * block_total, PLANE * slots * rows), bf16),
        vmem((z_count, PLANE, slots, rows, part), bf16),
        vmem((4, slots, block, part), bf16),
        vmem((block, slots * block), f32),
        vmem((4, slots, block, part), bf16),
        vmem((z_count, PLANE, slots, rows, part), bf16),
        vmem((hop, rows, block_total, part), bf16),
        vmem((hop, rows, block_total, part), bf16),
        vmem((hop, rows, block_total, part), bf16),
        vmem((hop, rows, block_total, part), bf16),
        vmem((rows, block_total, part), bf16),
        vmem((4, stripe, block_total, part), bf16),
        vmem((dp_count, micro, wide), bf16),
        vmem((dp_count, 1, width), f32),
        vmem((dp_count, micro, wide), f32),
        vmem((micro, width), f32),
        dma((1,)), dma((1,)), dma((1,)), dma((1,)),
        dma((2, hop)), dma((2, hop)),
        dma((z_count, PLANE)), dma((z_count, PLANE)),
        dma((z_count, PLANE)), dma((z_count, PLANE)),
        dma((2, hop)), dma((2, hop)),
        dma((4,)), dma((4,)),
        dma((dp_count,)), dma((dp_count,)),
        dma((dp_count,)), dma((dp_count,)),
        dma((dp_count,)), dma((dp_count,)),
    ]
    here = pl.BlockSpec(memory_space=vmem)
    query_grads, passage_grads, grad_inputs, weight_grads = pl.pallas_call(
        relay_kernel,
        out_shape=(
            jax.ShapeDtypeStruct(queries.shape, bf16),
            jax.ShapeDtypeStruct(passages.shape, bf16),
            jax.ShapeDtypeStruct((micro, col), f32),
            jax.ShapeDtypeStruct(section_weights.shape[1:], bf16),
        ),
        in_specs=[here] * 7,
        out_specs=(here,) * 4,
        scratch_shapes=scratch,
        compiler_params=pltpu.CompilerParams(
            collective_id=0, has_side_effects=True, vmem_limit_bytes=56 * 1024 * 1024
        ),
    )(queries, passages, table, teacher, section_weights[0], section_inputs[0], pre)
    return query_grads, passage_grads, grad_inputs[None], weight_grads[None]


def body(queries, passages, candidates, counts, teacher, section_weights, section_inputs, pre_acts):
    sections, dp_count = lax.axis_size("section"), lax.axis_size("dp")
    stripe, block_total, width = passages.shape
    by_planes = (
        sections == 2
        and dp_count == 16
        and stripe == 8
        and block_total == 16
        and width % 512 == 0
        and candidates.shape[0] == dp_count
        and candidates.shape[1] * dp_count * stripe == teacher.shape[1]
        and section_inputs.shape[1] == dp_count
    )
    chosen = plane_body if by_planes else general_body
    return chosen(
        queries, passages, candidates, counts, teacher, section_weights, section_inputs, pre_acts
    )


def solution(mesh):
    placed = (
        P(("section", "dp"), None),
        P("dp", None, None),
        P("section", None),
        P("section"),
        P(("section", "dp"), None),
        P("section", "dp", None),
        P("section", None, "dp"),
        P("section", None, "dp"),
    )
    return jax.shard_map(
        body,
        mesh=mesh,
        in_specs=placed,
        out_specs=(
            P(("section", "dp"), None),
            P("dp", None, None),
            P("section", None, "dp"),
            P("section", "dp", None),
        ),
        check_vma=False,
    )
```

```python
import functools

import jax
import jax.numpy as jnp
from jax import lax
from jax.experimental import pallas as pl
from jax.experimental.pallas import tpu as pltpu
from jax.sharding import PartitionSpec as P

INVERSE_TEMP = 20.0


def passed_along(value, axis, steps):
    count = lax.axis_size(axis)
    initial, last = (max(0, -steps), min(count, count - steps))
    return lax.ppermute(value, axis, [(source, source + steps) for source in range(initial, last)])


def soft_weights(logits, valid):
    masked = jnp.where(valid, logits, -1e30)
    highest = jnp.max(masked, axis=-1, keepdims=True)
    expons = jnp.where(valid, jnp.exp(masked - highest), 0.0)
    return expons / jnp.sum(expons, axis=-1, keepdims=True)


def general_body(queries, passages, candidates, counts, teacher, section_weights, section_inputs, pre_acts):
    dp_count = lax.axis_size("dp")
    dp_index = lax.axis_index("dp")
    stripe, block_total, width = passages.shape
    row_block_count = stripe * dp_count
    blocks_here = candidates.shape[0] // dp_count
    slot_count = candidates.shape[1]
    requests = blocks_here * slot_count
    all_slots = candidates.reshape(-1)
    outgoing = jnp.take(passages, all_slots, axis=1)
    pulled_rows = lax.all_to_all(outgoing, "dp", split_axis=1, concat_axis=0, tiled=True)
    pulled_rows = pulled_rows.reshape(row_block_count, blocks_here, slot_count, width)
    own_counts = lax.dynamic_slice_in_dim(counts, dp_index * blocks_here, blocks_here)
    slot_valid = jnp.arange(slot_count, dtype=jnp.int32)[None, :] < own_counts[:, None]
    column_valid = jnp.repeat(slot_valid, row_block_count, axis=1)[:, None, :]
    query_row_items = queries.reshape(blocks_here, row_block_count, width)
    logits = (
        jnp.einsum(
            "ixp,wifp->ixfw", query_row_items, pulled_rows, preferred_element_type=jnp.float32
        )
        * INVERSE_TEMP
    )
    logits = logits.reshape(blocks_here, row_block_count, slot_count * row_block_count)
    target_logits = soft_weights(
        teacher.reshape(blocks_here, row_block_count, slot_count * row_block_count), column_valid
    )
    weight_matrices = (soft_weights(logits, column_valid) - target_logits).astype(jnp.bfloat16)
    weight_matrices = weight_matrices.reshape(
        blocks_here, row_block_count, slot_count, row_block_count
    )
    query_sums = (
        jnp.einsum(
            "geal,lgay->gey", weight_matrices, pulled_rows, preferred_element_type=jnp.float32
        )
        * INVERSE_TEMP
    )
    passage_sums = (
        jnp.einsum(
            "fnyw,fnj->wfyj", weight_matrices, query_row_items, preferred_element_type=jnp.float32
        )
        * INVERSE_TEMP
    )
    block_terms = passage_sums.reshape(row_block_count, requests, width).astype(jnp.bfloat16)
    micro_count = section_inputs.shape[1] // dp_count
    col_width = width // dp_count
    micro_cols = jnp.transpose(
        query_sums[0, :micro_count].reshape(micro_count, dp_count, col_width), (1, 0, 2)
    )
    incoming_piece = lax.all_to_all(block_terms, "dp", split_axis=0, concat_axis=1, tiled=True)
    entry = lax.all_to_all(micro_cols, "dp", split_axis=0, concat_axis=1, tiled=True)
    onehot = (all_slots[:, None] == jnp.arange(block_total, dtype=jnp.int32)[None, :]).astype(
        jnp.float32
    )
    dense = jnp.einsum(
        "sjd,jn->snd",
        incoming_piece.astype(jnp.float32),
        onehot,
        precision=lax.Precision.HIGHEST,
        preferred_element_type=jnp.float32,
    )
    passage_out = lax.psum(dense, "section").astype(jnp.bfloat16)
    weight_rows = section_weights[0]
    input_cols = section_inputs[0]
    pre = pre_acts[0].astype(jnp.float32)
    sigma = jax.nn.sigmoid(pre)
    slope = sigma * (1.0 + pre * (1.0 - sigma))
    carry = entry.reshape(dp_count * micro_count, col_width)
    section_count = lax.axis_size("section")
    section_index = lax.axis_index("section")
    grad_cols = jnp.zeros_like(carry)
    grad_weight = jnp.zeros((col_width, width), jnp.float32)
    for section_turn in range(section_count):
        active_flag = section_count - 1 - section_turn
        inner = (carry * slope).astype(jnp.bfloat16)
        piece = lax.all_gather(inner, "dp", axis=1, tiled=True)
        back_sum = jnp.einsum("mj,ij->mi", piece, weight_rows, preferred_element_type=jnp.float32)
        weight_part = jnp.einsum("mi,mj->ij", input_cols, piece, preferred_element_type=jnp.float32)
        back_sum, layer_weight = (back_sum, weight_part)
        updated = carry + back_sum
        is_active = section_index == active_flag
        grad_cols = jnp.where(is_active, updated, grad_cols)
        grad_weight = jnp.where(is_active, layer_weight, grad_weight)
        if section_turn + 1 < section_count:
            carry = passed_along(updated, "section", -1)
    return (
        query_sums.reshape(blocks_here * row_block_count, width).astype(jnp.bfloat16),
        passage_out,
        grad_cols[None],
        grad_weight[None].astype(jnp.bfloat16),
    )


PLANE = 8
GROUP = 4


def cells(width, ref, index):
    return ref.at[:, :, pl.ds(pl.multiple_of(index * width, width), width)]


def relay_kernel(
    q_hbm, p_ref, cand_ref, count_ref, teacher_hbm, w_hbm, pre_ref,
    qg_hbm, pg_ref, gi_ref, inner_ref,
    q_ref, teacher_ref, w_ref, qg_ref, load_s, store_s,
    candx, shard, up_in, down_in, sel, sel_t, stage, cols, target, terms, tin,
    up_out, up_sum, down_out, down_sum, fin, final_in, prebuf, topbuf, cbuf, cot,
    cand_s, cand_r, half_s, half_r, line_s, line_r, pull_s, pull_r, push_s, push_r,
    sum_s, sum_r, fin_s, fin_r, pre_s, pre_r, top_s, top_r, cot_s, cot_r,
):
    dp_count = lax.axis_size("dp")
    section = lax.axis_index("section")
    dp = lax.axis_index("dp")
    z = dp // GROUP
    x = (dp // 2) % 2
    core = dp % 2
    me = x * 4 + section * 2 + core
    quarter = section * 2 + core
    z_count = dp_count // GROUP
    stripe, block_total, width = p_ref.shape
    part = width // 4
    rows = 2 * stripe
    block = q_ref.shape[0]
    slots = teacher_ref.shape[1] // block
    micro, col = pre_ref.shape
    f32, bf16 = jnp.float32, jnp.bfloat16

    def remote(source, dest, send, recv, device):
        return pltpu.make_async_remote_copy(
            src_ref=source, dst_ref=dest, send_sem=send, recv_sem=recv,
            device_id=device, device_id_type=pl.DeviceIdType.MESH,
        )

    def member(g):
        return ((g // 2) % 2, z * GROUP + (g // 4) * 2 + g % 2)

    def others(count, own, act):
        def step(i, carry):
            @pl.when(i != own)
            def _():
                act(i)
            return carry
        lax.fori_loop(0, count, step, 0)

    loads = [
        pltpu.make_async_copy(source, dest, load_s.at[i])
        for i, (source, dest) in enumerate(
            ((q_hbm, q_ref), (teacher_hbm, teacher_ref), (w_hbm, w_ref))
        )
    ]
    for load in loads:
        load.start()

    barrier = pltpu.get_barrier_semaphore()
    everyone = 2 * dp_count

    def greet(i):
        pl.semaphore_signal(
            barrier, inc=1, device_id=(i // dp_count, i % dp_count),
            device_id_type=pl.DeviceIdType.MESH,
        )

    others(everyone, section * dp_count + dp, greet)
    pl.semaphore_wait(barrier, everyone - 1)

    cand_copy = remote(cand_ref, candx, cand_s.at[0], cand_r.at[0], (1 - section, dp))
    cand_copy.start()
    partner = dp + 1 - 2 * core
    half_copy = remote(
        cells(part, p_ref, section * 2 + 1 - core), shard.at[pl.ds(core * stripe, stripe)],
        half_s.at[0], half_r.at[0], (section, partner),
    )
    half_copy.start()
    shard[pl.ds(core * stripe, stripe)] = p_ref[
        :, :, pl.ds(pl.multiple_of(quarter * part, part), part)
    ]
    half_wait = remote(
        cells(part, p_ref, quarter), shard.at[pl.ds((1 - core) * stripe, stripe)],
        half_s.at[0], half_r.at[0], (section, partner),
    )
    half_wait.wait_recv()

    def line_copy(source, ref, sems, h, step):
        return remote(source, ref.at[h], line_s.at[sems, h], line_r.at[sems, h], (section, dp + step * GROUP))

    @pl.when(z < z_count - 1)
    def _():
        line_copy(shard, up_in, 0, 0, 1).start()

    @pl.when(z > 0)
    def _():
        line_copy(shard, down_in, 1, 0, -1).start()

    cand_copy.wait_recv()
    total = PLANE * slots * rows
    listed_shape = (total, dp_count)
    at_row = lax.broadcasted_iota(jnp.int32, listed_shape, 0)
    lane = lax.broadcasted_iota(jnp.int32, listed_shape, 1)
    g_of = at_row // (slots * rows)
    slot_of = (at_row // rows) % slots
    here = (g_of // 2) % 2 == section
    listed = jnp.zeros(listed_shape, f32)
    for slot in range(slots):
        mine = cand_ref[slot:slot + 1, :].astype(f32)
        away = candx[slot:slot + 1, :].astype(f32)
        listed = jnp.where(slot_of == slot, jnp.where(here, mine, away), listed)
    picked_lane = lane == z * GROUP + (g_of // 4) * 2 + g_of % 2
    wanted = jnp.sum(jnp.where(picked_lane, listed, 0.0), axis=1, keepdims=True)
    shape = (total, rows * block_total)
    row_of = lax.broadcasted_iota(jnp.int32, shape, 0) % rows
    place = lax.broadcasted_iota(jnp.int32, shape, 1)
    hit = (place // block_total == row_of) & ((place % block_total).astype(f32) == wanted)
    onehot = jnp.where(hit, 1.0, 0.0)
    sel[...] = onehot.astype(bf16)
    sel_t[...] = jnp.transpose(onehot).astype(bf16)

    def own_rows(zs, at_x):
        return pl.ds(pl.multiple_of(zs * GROUP * stripe + at_x * rows, rows), rows)

    def pull_copy(zs, g):
        return remote(
            stage.at[zs, g], cols.at[quarter, :, own_rows(zs, x), :],
            pull_s.at[zs, g], pull_r.at[zs, me], member(g),
        )

    def pull_wait(zs, g):
        return remote(
            stage.at[zs, g], cols.at[g % 4, :, own_rows(zs, g // 4), :],
            pull_s.at[zs, g], pull_r.at[zs, g], member(g),
        )

    def spread(ref, zs):
        picked = jnp.dot(
            sel[...], ref[...].reshape(rows * block_total, part), preferred_element_type=f32
        )
        stage[zs] = picked.astype(bf16).reshape(PLANE, slots, rows, part)
        others(PLANE, me, lambda g: pull_copy(zs, g).start())
        cols[quarter, :, own_rows(zs, x), :] = stage[zs, me]

    spread(shard, z)

    prebuf[dp, :, :col] = pre_ref[...]

    def pre_copy(j):
        return remote(prebuf.at[dp], prebuf.at[dp], pre_s.at[j], pre_r.at[dp], (section, j))

    others(dp_count, dp, lambda j: pre_copy(j).start())

    def soft(values, valid):
        masked = jnp.where(valid, values, -1e30)
        highest = jnp.max(masked, axis=-1, keepdims=True)
        expons = jnp.where(valid, jnp.exp(masked - highest), 0.0)
        return expons / jnp.sum(expons, axis=-1, keepdims=True)

    own_row = count_ref[...].astype(f32)
    own_lane = lax.broadcasted_iota(jnp.int32, own_row.shape, 1)
    how_many = jnp.sum(jnp.where(own_lane == dp, own_row, 0.0), axis=1, keepdims=True)
    slot_lane = lax.broadcasted_iota(jnp.int32, teacher_ref.shape, 1) // block
    valid = slot_lane.astype(f32) < how_many
    loads[1].wait()
    target[...] = soft(teacher_ref[...], valid)
    loads[0].wait()

    for h in range(z_count - 1):
        @pl.when(z >= h + 1)
        def _():
            line_copy(shard, up_in, 0, h, -1).wait_recv()
            if h + 1 < z_count - 1:
                @pl.when(z < z_count - 1)
                def _():
                    line_copy(up_in.at[h], up_in, 0, h + 1, 1).start()

        @pl.when(z + h + 1 < z_count)
        def _():
            line_copy(shard, down_in, 1, h, 1).wait_recv()
            if h + 1 < z_count - 1:
                @pl.when(z > 0)
                def _():
                    line_copy(down_in.at[h], down_in, 1, h + 1, -1).start()

        @pl.when(z >= h + 1)
        def _():
            spread(up_in.at[h], z - h - 1)

        @pl.when(z + h + 1 < z_count)
        def _():
            spread(down_in.at[h], z + h + 1)

    for zs in range(z_count):
        others(PLANE, me, lambda g: pull_wait(zs, g).wait_recv())

    contract_last = (((1,), (1,)), ((), ()))
    contract_first = (((0,), (0,)), ((), ()))
    logits = jnp.zeros((block, slots * block), f32)
    for f in range(4):
        logits += lax.dot_general(
            q_ref[:, f * part:(f + 1) * part], cols[f].reshape(slots * block, part),
            contract_last, preferred_element_type=f32,
        )
    weights32 = soft(logits * INVERSE_TEMP, valid) - target[...]
    weights = weights32.astype(bf16)
    weights_t = jnp.transpose(weights32).astype(bf16)
    for f in range(4):
        sums = jnp.dot(
            weights_t, q_ref[:, f * part:(f + 1) * part], preferred_element_type=f32
        )
        terms[f] = (sums * INVERSE_TEMP).astype(bf16).reshape(slots, block, part)

    def push_copy(zt, g):
        return remote(
            terms.at[g % 4, :, own_rows(zt, g // 4), :], tin.at[zt, me],
            push_s.at[zt, g], push_r.at[zt, me], member(g),
        )

    def push_wait(zt, g):
        return remote(
            terms.at[quarter, :, own_rows(zt, x), :], tin.at[zt, g],
            push_s.at[zt, g], push_r.at[zt, g], member(g),
        )

    def push(zt):
        others(PLANE, me, lambda g: push_copy(zt, g).start())
        tin[zt, me] = terms[quarter, :, own_rows(zt, x), :]

    bits = max(1, (z_count - 1).bit_length())
    orders = [sorted(range(z_count), key=lambda t: (-abs(t - own), -t)) for own in range(z_count)]

    def target_at(i):
        code = sum(orders[own][i] << (bits * own) for own in range(z_count))
        return lax.shift_right_logical(jnp.int32(code), (bits * z).astype(jnp.int32)) % (1 << bits)

    push(target_at(0))
    for f in range(4):
        sums = jnp.dot(weights, cols[f].reshape(slots * block, part), preferred_element_type=f32)
        sums = sums * INVERSE_TEMP
        qg_ref[:, f * part:(f + 1) * part] = sums.astype(bf16)
        topbuf[dp, :, f * part:(f + 1) * part] = sums[0:1]

    qg_copy = pltpu.make_async_copy(qg_ref, qg_hbm, store_s.at[0])
    qg_copy.start()

    def top_copy(j):
        return remote(topbuf.at[dp], topbuf.at[dp], top_s.at[j], top_r.at[dp], (section, j))

    @pl.when(section == 1)
    def _():
        others(dp_count, dp, lambda j: top_copy(j).start())

    def cot_copy(j):
        return remote(cbuf.at[dp], cbuf.at[dp], cot_s.at[j], cot_r.at[dp], (1 - section, j))

    def layer(own):
        others(dp_count, dp, lambda j: remote(
            prebuf.at[j], prebuf.at[j], pre_s.at[j], pre_r.at[j], (section, j)).wait_recv())
        pre = jnp.concatenate([prebuf[j].astype(f32)[:, :col] for j in range(dp_count)], axis=1)
        sigma = 1.0 / (1.0 + jnp.exp(-pre))
        slope = sigma * (1.0 + pre * (1.0 - sigma))
        inner = (cot[...] * slope).astype(bf16)
        loads[2].wait()
        back = lax.dot_general(inner, w_ref[...], contract_last, preferred_element_type=f32)
        updated = own + back
        gi_ref[...] = updated
        inner_ref[...] = inner
        return updated

    def last_section():
        others(dp_count, dp, lambda j: remote(
            topbuf.at[j], topbuf.at[j], top_s.at[j], top_r.at[j], (section, j)).wait_recv())
        own = jnp.zeros((micro, col), f32)
        for j in range(dp_count):
            cot[j:j + 1, :] = topbuf[j]
        for j in range(dp_count):
            own = jnp.where(dp == j, cot[:, j * col:(j + 1) * col], own)
        updated = layer(own)
        cbuf[dp, :, :col] = updated
        others(dp_count, dp_count, lambda j: cot_copy(j).start())

    def summed(zt):
        others(PLANE, me, lambda g: push_wait(zt, g).wait_recv())
        return jnp.dot(
            sel_t[...], tin[zt].reshape(total, part), preferred_element_type=f32
        )

    def sum_copy(source, dest, sems, h, step):
        return remote(
            source.at[h], dest.at[h], sum_s.at[sems, h], sum_r.at[sems, h],
            (section, dp + step * GROUP),
        )

    def line_sum(value, h, step, sems, out, incoming, beyond):
        out[h - 1] = value.astype(bf16)

        @pl.when(beyond)
        def _():
            sum_copy(out, incoming, sems, h, -step).wait_recv()
            out[h - 1] = (value + incoming[h].astype(f32)).astype(bf16)

        sum_copy(out, incoming, sems, h - 1, step).start()

    for i in range(z_count - 1):
        zt = target_at(i)
        value = summed(zt).reshape(rows, block_total, part)
        push(target_at(i + 1))

        @pl.when(zt > z)
        def _():
            line_sum(value, zt - z, 1, 0, up_out, up_sum, z > 0)

        @pl.when(zt < z)
        def _():
            line_sum(value, z - zt, -1, 1, down_out, down_sum, z < z_count - 1)

        if i == 0:
            pl.when(section == 1)(last_section)

    value = summed(z).reshape(rows, block_total, part)

    zero = jnp.zeros_like(value)

    @pl.when(z > 0)
    def _():
        sum_copy(up_out, up_sum, 0, 0, -1).wait_recv()

    @pl.when(z < z_count - 1)
    def _():
        sum_copy(down_out, down_sum, 1, 0, 1).wait_recv()

    below = jnp.where(z > 0, up_sum[0].astype(f32), zero)
    above = jnp.where(z < z_count - 1, down_sum[0].astype(f32), zero)
    fin[...] = (value + below + above).astype(bf16)

    def fin_copy(i):
        return remote(
            fin.at[pl.ds((i % 2) * stripe, stripe)], final_in.at[quarter],
            fin_s.at[i], fin_r.at[quarter], (i // 2, z * GROUP + x * 2 + i % 2),
        )

    def fin_wait(i):
        return remote(
            fin.at[pl.ds(core * stripe, stripe)], final_in.at[i],
            fin_s.at[i], fin_r.at[i], (i // 2, z * GROUP + x * 2 + i % 2),
        )

    others(4, quarter, lambda i: fin_copy(i).start())
    final_in[quarter] = fin[pl.ds(core * stripe, stripe)]

    @pl.when(section == 0)
    def _():
        def wait(j, carry):
            remote(cbuf.at[j], cbuf.at[j], cot_s.at[j], cot_r.at[j], (1 - section, j)).wait_recv()
            return carry
        lax.fori_loop(0, dp_count, wait, 0)
        cot[...] = jnp.concatenate([cbuf[j][:, :col] for j in range(dp_count)], axis=1)
        layer(cbuf[dp][:, :col])

    others(4, quarter, lambda i: fin_wait(i).wait_recv())
    for f in range(4):
        pg_ref[:, :, f * part:(f + 1) * part] = final_in[f]

    qg_copy.wait()
    cand_copy.wait_send()
    half_copy.wait_send()
    for h in range(z_count - 1):
        @pl.when((z >= h) & (z < z_count - 1))
        def _():
            line_copy(up_in.at[h], up_in, 0, h, 1).wait_send()

        @pl.when((z + h < z_count) & (z > 0))
        def _():
            line_copy(down_in.at[h], down_in, 1, h, -1).wait_send()

        @pl.when(z + h + 1 < z_count)
        def _():
            sum_copy(up_out, up_sum, 0, h, 1).wait_send()

        @pl.when(z >= h + 1)
        def _():
            sum_copy(down_out, down_sum, 1, h, -1).wait_send()

    for zs in range(z_count):
        others(PLANE, me, lambda g: pull_copy(zs, g).wait_send())
        others(PLANE, me, lambda g: push_copy(zs, g).wait_send())
    others(dp_count, dp, lambda j: pre_copy(j).wait_send())

    @pl.when(section == 1)
    def _():
        others(dp_count, dp, lambda j: top_copy(j).wait_send())
        others(dp_count, dp_count, lambda j: cot_copy(j).wait_send())

    others(4, quarter, lambda i: fin_copy(i).wait_send())


def plane_body(queries, passages, candidates, counts, teacher, section_weights, section_inputs, pre_acts):
    dp_count = lax.axis_size("dp")
    z_count = dp_count // GROUP
    stripe, block_total, width = passages.shape
    block = queries.shape[0]
    slots = candidates.shape[1]
    part = width // 4
    rows = 2 * stripe
    micro, col = section_inputs.shape[1:]
    wide = -(-col // 128) * 128
    f32, bf16, i32 = jnp.float32, jnp.bfloat16, jnp.int32
    table = candidates.T
    vmem, dma = pltpu.VMEM, pltpu.SemaphoreType.DMA
    hop = z_count - 1
    scratch = [
        vmem(queries.shape, bf16),
        vmem(teacher.shape, f32),
        vmem(section_weights.shape[1:], bf16),
        vmem(queries.shape, bf16),
        dma((3,)), dma((1,)),
        vmem(table.shape, i32),
        vmem((rows, block_total, part), bf16),
        vmem((hop, rows, block_total, part), bf16),
        vmem((hop, rows, block_total, part), bf16),
        vmem((PLANE * slots * rows, rows * block_total), bf16),
        vmem((rows * block_total, PLANE * slots * rows), bf16),
        vmem((z_count, PLANE, slots, rows, part), bf16),
        vmem((4, slots, block, part), bf16),
        vmem((block, slots * block), f32),
        vmem((4, slots, block, part), bf16),
        vmem((z_count, PLANE, slots, rows, part), bf16),
        vmem((hop, rows, block_total, part), bf16),
        vmem((hop, rows, block_total, part), bf16),
        vmem((hop, rows, block_total, part), bf16),
        vmem((hop, rows, block_total, part), bf16),
        vmem((rows, block_total, part), bf16),
        vmem((4, stripe, block_total, part), bf16),
        vmem((dp_count, micro, wide), bf16),
        vmem((dp_count, 1, width), f32),
        vmem((dp_count, micro, wide), f32),
        vmem((micro, width), f32),
        dma((1,)), dma((1,)), dma((1,)), dma((1,)),
        dma((2, hop)), dma((2, hop)),
        dma((z_count, PLANE)), dma((z_count, PLANE)),
        dma((z_count, PLANE)), dma((z_count, PLANE)),
        dma((2, hop)), dma((2, hop)),
        dma((4,)), dma((4,)),
        dma((dp_count,)), dma((dp_count,)),
        dma((dp_count,)), dma((dp_count,)),
        dma((dp_count,)), dma((dp_count,)),
    ]
    here, there = pl.BlockSpec(memory_space=vmem), pl.BlockSpec(memory_space=pl.ANY)
    query_grads, passage_grads, grad_inputs, inner = pl.pallas_call(
        relay_kernel,
        out_shape=(
            jax.ShapeDtypeStruct(queries.shape, bf16),
            jax.ShapeDtypeStruct(passages.shape, bf16),
            jax.ShapeDtypeStruct((micro, col), f32),
            jax.ShapeDtypeStruct((micro, width), bf16),
        ),
        in_specs=[there, here, here, here, there, there, here],
        out_specs=(there, here, here, here),
        scratch_shapes=scratch,
        compiler_params=pltpu.CompilerParams(
            collective_id=0, has_side_effects=True, vmem_limit_bytes=56 * 1024 * 1024
        ),
    )(queries, passages, table, counts[None], teacher, section_weights[0], pre_acts[0])
    weight_grads = jnp.einsum(
        "mi,mj->ij", section_inputs[0], inner, preferred_element_type=f32
    ).astype(bf16)
    return query_grads, passage_grads, grad_inputs[None], weight_grads[None]


def body(queries, passages, candidates, counts, teacher, section_weights, section_inputs, pre_acts):
    sections, dp_count = lax.axis_size("section"), lax.axis_size("dp")
    stripe, block_total, width = passages.shape
    by_planes = (
        sections == 2
        and dp_count == 16
        and stripe == 8
        and block_total == 16
        and width % 512 == 0
        and candidates.shape[0] == dp_count
        and candidates.shape[1] * dp_count * stripe == teacher.shape[1]
        and section_inputs.shape[1] == dp_count
    )
    chosen = plane_body if by_planes else general_body
    return chosen(
        queries, passages, candidates, counts, teacher, section_weights, section_inputs, pre_acts
    )


def solution(mesh):
    placed = (
        P(("section", "dp"), None),
        P("dp", None, None),
        P("section", None),
        P("section"),
        P(("section", "dp"), None),
        P("section", "dp", None),
        P("section", None, "dp"),
        P("section", None, "dp"),
    )
    return jax.shard_map(
        body,
        mesh=mesh,
        in_specs=placed,
        out_specs=(
            P(("section", "dp"), None),
            P("dp", None, None),
            P("section", None, "dp"),
            P("section", "dp", None),
        ),
        check_vma=False,
    )
```

```python
import functools

import jax
import jax.numpy as jnp
from jax import lax
from jax.experimental import pallas as pl
from jax.experimental.pallas import tpu as pltpu
from jax.sharding import PartitionSpec as P

INVERSE_TEMP = 20.0


def passed_along(value, axis, steps):
    count = lax.axis_size(axis)
    initial, last = (max(0, -steps), min(count, count - steps))
    return lax.ppermute(value, axis, [(source, source + steps) for source in range(initial, last)])


def soft_weights(logits, valid):
    masked = jnp.where(valid, logits, -1e30)
    highest = jnp.max(masked, axis=-1, keepdims=True)
    expons = jnp.where(valid, jnp.exp(masked - highest), 0.0)
    return expons / jnp.sum(expons, axis=-1, keepdims=True)


def general_body(queries, passages, candidates, counts, teacher, section_weights, section_inputs, pre_acts):
    dp_count = lax.axis_size("dp")
    dp_index = lax.axis_index("dp")
    stripe, block_total, width = passages.shape
    row_block_count = stripe * dp_count
    blocks_here = candidates.shape[0] // dp_count
    slot_count = candidates.shape[1]
    requests = blocks_here * slot_count
    all_slots = candidates.reshape(-1)
    outgoing = jnp.take(passages, all_slots, axis=1)
    pulled_rows = lax.all_to_all(outgoing, "dp", split_axis=1, concat_axis=0, tiled=True)
    pulled_rows = pulled_rows.reshape(row_block_count, blocks_here, slot_count, width)
    own_counts = lax.dynamic_slice_in_dim(counts, dp_index * blocks_here, blocks_here)
    slot_valid = jnp.arange(slot_count, dtype=jnp.int32)[None, :] < own_counts[:, None]
    column_valid = jnp.repeat(slot_valid, row_block_count, axis=1)[:, None, :]
    query_row_items = queries.reshape(blocks_here, row_block_count, width)
    logits = (
        jnp.einsum(
            "ixp,wifp->ixfw", query_row_items, pulled_rows, preferred_element_type=jnp.float32
        )
        * INVERSE_TEMP
    )
    logits = logits.reshape(blocks_here, row_block_count, slot_count * row_block_count)
    target_logits = soft_weights(
        teacher.reshape(blocks_here, row_block_count, slot_count * row_block_count), column_valid
    )
    weight_matrices = (soft_weights(logits, column_valid) - target_logits).astype(jnp.bfloat16)
    weight_matrices = weight_matrices.reshape(
        blocks_here, row_block_count, slot_count, row_block_count
    )
    query_sums = (
        jnp.einsum(
            "geal,lgay->gey", weight_matrices, pulled_rows, preferred_element_type=jnp.float32
        )
        * INVERSE_TEMP
    )
    passage_sums = (
        jnp.einsum(
            "fnyw,fnj->wfyj", weight_matrices, query_row_items, preferred_element_type=jnp.float32
        )
        * INVERSE_TEMP
    )
    block_terms = passage_sums.reshape(row_block_count, requests, width).astype(jnp.bfloat16)
    micro_count = section_inputs.shape[1] // dp_count
    col_width = width // dp_count
    micro_cols = jnp.transpose(
        query_sums[0, :micro_count].reshape(micro_count, dp_count, col_width), (1, 0, 2)
    )
    incoming_piece = lax.all_to_all(block_terms, "dp", split_axis=0, concat_axis=1, tiled=True)
    entry = lax.all_to_all(micro_cols, "dp", split_axis=0, concat_axis=1, tiled=True)
    onehot = (all_slots[:, None] == jnp.arange(block_total, dtype=jnp.int32)[None, :]).astype(
        jnp.float32
    )
    dense = jnp.einsum(
        "sjd,jn->snd",
        incoming_piece.astype(jnp.float32),
        onehot,
        precision=lax.Precision.HIGHEST,
        preferred_element_type=jnp.float32,
    )
    passage_out = lax.psum(dense, "section").astype(jnp.bfloat16)
    weight_rows = section_weights[0]
    input_cols = section_inputs[0]
    pre = pre_acts[0].astype(jnp.float32)
    sigma = jax.nn.sigmoid(pre)
    slope = sigma * (1.0 + pre * (1.0 - sigma))
    carry = entry.reshape(dp_count * micro_count, col_width)
    section_count = lax.axis_size("section")
    section_index = lax.axis_index("section")
    grad_cols = jnp.zeros_like(carry)
    grad_weight = jnp.zeros((col_width, width), jnp.float32)
    for section_turn in range(section_count):
        active_flag = section_count - 1 - section_turn
        inner = (carry * slope).astype(jnp.bfloat16)
        piece = lax.all_gather(inner, "dp", axis=1, tiled=True)
        back_sum = jnp.einsum("mj,ij->mi", piece, weight_rows, preferred_element_type=jnp.float32)
        weight_part = jnp.einsum("mi,mj->ij", input_cols, piece, preferred_element_type=jnp.float32)
        back_sum, layer_weight = (back_sum, weight_part)
        updated = carry + back_sum
        is_active = section_index == active_flag
        grad_cols = jnp.where(is_active, updated, grad_cols)
        grad_weight = jnp.where(is_active, layer_weight, grad_weight)
        if section_turn + 1 < section_count:
            carry = passed_along(updated, "section", -1)
    return (
        query_sums.reshape(blocks_here * row_block_count, width).astype(jnp.bfloat16),
        passage_out,
        grad_cols[None],
        grad_weight[None].astype(jnp.bfloat16),
    )


PLANE = 8
GROUP = 4


def chunks_of(width, count):
    lanes, edges = width // 128, [0]
    for i in range(count):
        edges.append(edges[-1] + -(-(lanes - edges[-1]) // (count - i)))
    return [(128 * a, 128 * (b - a)) for a, b in zip(edges, edges[1:])]


CHUNKS = 2
AHEAD = 2


def cells(width, ref, index):
    return ref.at[:, :, pl.ds(pl.multiple_of(index * width, width), width)]


def relay_kernel(
    q_hbm, p_ref, cand_ref, count_ref, teacher_hbm, w_hbm, pre_ref,
    qg_hbm, pg_ref, gi_ref, inner_ref,
    q_ref, teacher_ref, w_ref, qg_ref, slope_ref, load_s, store_s,
    candx, shard, up_in, down_in, sel, sel_t, stage, cols, target, terms, tin,
    up_out, up_sum, down_out, down_sum, fin, final_in, prebuf, topbuf, cbuf, cot,
    cand_s, cand_r, half_s, half_r, line_s, line_r, pull_s, pull_r, push_s, push_r,
    sum_s, sum_r, fin_s, fin_r, pre_s, pre_r, top_s, top_r, cot_s, cot_r,
):
    dp_count = lax.axis_size("dp")
    section = lax.axis_index("section")
    dp = lax.axis_index("dp")
    z = dp // GROUP
    x = (dp // 2) % 2
    core = dp % 2
    me = x * 4 + section * 2 + core
    quarter = section * 2 + core
    z_count = dp_count // GROUP
    stripe, block_total, width = p_ref.shape
    part = width // 4
    rows = 2 * stripe
    block = q_ref.shape[0]
    slots = teacher_ref.shape[1] // block
    micro, col = pre_ref.shape
    f32, bf16 = jnp.float32, jnp.bfloat16
    chunks = chunks_of(part, CHUNKS)

    def lanes(c):
        return pl.ds(*chunks[c])

    def remote(source, dest, send, recv, device):
        return pltpu.make_async_remote_copy(
            src_ref=source, dst_ref=dest, send_sem=send, recv_sem=recv,
            device_id=device, device_id_type=pl.DeviceIdType.MESH,
        )

    def member(g):
        return ((g // 2) % 2, z * GROUP + (g // 4) * 2 + g % 2)

    def others(count, own, act):
        def step(i, carry):
            @pl.when(i != own)
            def _():
                act(i)
            return carry
        lax.fori_loop(0, count, step, 0)

    loads = [
        pltpu.make_async_copy(source, dest, load_s.at[i])
        for i, (source, dest) in enumerate(
            ((q_hbm, q_ref), (teacher_hbm, teacher_ref), (w_hbm, w_ref))
        )
    ]
    for load in loads:
        load.start()

    barrier = pltpu.get_barrier_semaphore()
    everyone = 2 * dp_count

    def greet(i):
        pl.semaphore_signal(
            barrier, inc=1, device_id=(i // dp_count, i % dp_count),
            device_id_type=pl.DeviceIdType.MESH,
        )

    others(everyone, section * dp_count + dp, greet)
    pl.semaphore_wait(barrier, everyone - 1)

    cand_copy = remote(cand_ref, candx, cand_s.at[0], cand_r.at[0], (1 - section, dp))
    cand_copy.start()
    partner = dp + 1 - 2 * core
    half_copy = remote(
        cells(part, p_ref, section * 2 + 1 - core), shard.at[pl.ds(core * stripe, stripe)],
        half_s.at[0], half_r.at[0], (section, partner),
    )
    half_copy.start()
    shard[pl.ds(core * stripe, stripe)] = p_ref[
        :, :, pl.ds(pl.multiple_of(quarter * part, part), part)
    ]
    half_wait = remote(
        cells(part, p_ref, quarter), shard.at[pl.ds((1 - core) * stripe, stripe)],
        half_s.at[0], half_r.at[0], (section, partner),
    )
    half_wait.wait_recv()

    def line_copy(source, ref, sems, h, c, step):
        return remote(
            source.at[:, :, lanes(c)], ref.at[h, :, :, lanes(c)],
            line_s.at[sems, h, c], line_r.at[sems, h, c], (section, dp + step * GROUP),
        )

    @pl.when(z < z_count - 1)
    def _():
        for c in range(CHUNKS):
            line_copy(shard, up_in, 0, 0, c, 1).start()

    @pl.when(z > 0)
    def _():
        for c in range(CHUNKS):
            line_copy(shard, down_in, 1, 0, c, -1).start()

    cand_copy.wait_recv()
    total = PLANE * slots * rows
    listed_shape = (total, dp_count)
    at_row = lax.broadcasted_iota(jnp.int32, listed_shape, 0)
    lane = lax.broadcasted_iota(jnp.int32, listed_shape, 1)
    g_of = at_row // (slots * rows)
    slot_of = (at_row // rows) % slots
    here = (g_of // 2) % 2 == section
    listed = jnp.zeros(listed_shape, f32)
    for slot in range(slots):
        mine = cand_ref[slot:slot + 1, :].astype(f32)
        away = candx[slot:slot + 1, :].astype(f32)
        listed = jnp.where(slot_of == slot, jnp.where(here, mine, away), listed)
    picked_lane = lane == z * GROUP + (g_of // 4) * 2 + g_of % 2
    wanted = jnp.sum(jnp.where(picked_lane, listed, 0.0), axis=1, keepdims=True)
    shape = (total, rows * block_total)
    row_of = lax.broadcasted_iota(jnp.int32, shape, 0) % rows
    place = lax.broadcasted_iota(jnp.int32, shape, 1)
    hit = (place // block_total == row_of) & ((place % block_total).astype(f32) == wanted)
    onehot = jnp.where(hit, 1.0, 0.0)
    sel[...] = onehot.astype(bf16)
    sel_t[...] = jnp.transpose(onehot).astype(bf16)

    def own_rows(zs, at_x):
        return pl.ds(pl.multiple_of(zs * GROUP * stripe + at_x * rows, rows), rows)

    def pull_copy(zs, g, c):
        return remote(
            stage.at[zs, g, :, :, lanes(c)], cols.at[quarter, :, own_rows(zs, x), lanes(c)],
            pull_s.at[zs, g, c], pull_r.at[zs, me, c], member(g),
        )

    def pull_wait(zs, g, c):
        return remote(
            stage.at[zs, g, :, :, lanes(c)], cols.at[g % 4, :, own_rows(zs, g // 4), lanes(c)],
            pull_s.at[zs, g, c], pull_r.at[zs, g, c], member(g),
        )

    def spread(ref, zs, c):
        size = chunks[c][1]
        picked = jnp.dot(
            sel[...], ref[:, :, lanes(c)].reshape(rows * block_total, size),
            preferred_element_type=f32,
        )
        stage[zs, :, :, :, lanes(c)] = picked.astype(bf16).reshape(PLANE, slots, rows, size)
        others(PLANE, me, lambda g: pull_copy(zs, g, c).start())
        cols[quarter, :, own_rows(zs, x), lanes(c)] = stage[zs, me, :, :, lanes(c)]

    for c in range(CHUNKS):
        spread(shard, z, c)

    prebuf[dp, :, :col] = pre_ref[...]

    def pre_copy(j):
        return remote(prebuf.at[dp], prebuf.at[dp], pre_s.at[j], pre_r.at[dp], (section, j))

    others(dp_count, dp, lambda j: pre_copy(j).start())

    def soft(values, valid):
        masked = jnp.where(valid, values, -1e30)
        highest = jnp.max(masked, axis=-1, keepdims=True)
        expons = jnp.where(valid, jnp.exp(masked - highest), 0.0)
        return expons / jnp.sum(expons, axis=-1, keepdims=True)

    own_row = count_ref[...].astype(f32)
    own_lane = lax.broadcasted_iota(jnp.int32, own_row.shape, 1)
    how_many = jnp.sum(jnp.where(own_lane == dp, own_row, 0.0), axis=1, keepdims=True)
    slot_lane = lax.broadcasted_iota(jnp.int32, teacher_ref.shape, 1) // block
    valid = slot_lane.astype(f32) < how_many
    loads[1].wait()
    target[...] = soft(teacher_ref[...], valid)
    loads[0].wait()

    def slopes():
        others(dp_count, dp, lambda j: remote(
            prebuf.at[j], prebuf.at[j], pre_s.at[j], pre_r.at[j], (section, j)).wait_recv())
        pre = jnp.concatenate([prebuf[j].astype(f32)[:, :col] for j in range(dp_count)], axis=1)
        sigma = 1.0 / (1.0 + jnp.exp(-pre))
        slope_ref[...] = sigma * (1.0 + pre * (1.0 - sigma))

    def hop(h, c):
        @pl.when(z >= h + 1)
        def _():
            line_copy(shard, up_in, 0, h, c, -1).wait_recv()
            if h + 1 < z_count - 1:
                @pl.when(z < z_count - 1)
                def _():
                    line_copy(up_in.at[h], up_in, 0, h + 1, c, 1).start()

        @pl.when(z + h + 1 < z_count)
        def _():
            line_copy(shard, down_in, 1, h, c, 1).wait_recv()
            if h + 1 < z_count - 1:
                @pl.when(z > 0)
                def _():
                    line_copy(down_in.at[h], down_in, 1, h + 1, c, -1).start()

        @pl.when(z >= h + 1)
        def _():
            spread(up_in.at[h], z - h - 1, c)

        @pl.when(z + h + 1 < z_count)
        def _():
            spread(down_in.at[h], z + h + 1, c)

    for h in range(z_count - 1):
        if h == z_count - 2:
            slopes()
        for c in range(CHUNKS):
            hop(h, c)

    contract_last = (((1,), (1,)), ((), ()))
    logits = jnp.zeros((block, slots * block), f32)
    for c, (offset, size) in enumerate(chunks):
        for zs in range(z_count):
            others(PLANE, me, lambda g: pull_wait(zs, g, c).wait_recv())
        for f in range(4):
            logits += lax.dot_general(
                q_ref[:, f * part + offset:f * part + offset + size],
                cols[f, :, :, lanes(c)].reshape(slots * block, size),
                contract_last, preferred_element_type=f32,
            )
    weights32 = soft(logits * INVERSE_TEMP, valid) - target[...]
    weights = weights32.astype(bf16)
    weights_t = jnp.transpose(weights32).astype(bf16)
    def push_copy(zt, g, c):
        return remote(
            terms.at[g % 4, :, own_rows(zt, g // 4), lanes(c)], tin.at[zt, me, :, :, lanes(c)],
            push_s.at[zt, g, c], push_r.at[zt, me, c], member(g),
        )

    def push_wait(zt, g, c):
        return remote(
            terms.at[quarter, :, own_rows(zt, x), lanes(c)], tin.at[zt, g, :, :, lanes(c)],
            push_s.at[zt, g, c], push_r.at[zt, g, c], member(g),
        )

    def push(zt, c):
        others(PLANE, me, lambda g: push_copy(zt, g, c).start())
        tin[zt, me, :, :, lanes(c)] = terms[quarter, :, own_rows(zt, x), lanes(c)]

    bits = max(1, (z_count - 1).bit_length())
    orders = [sorted(range(z_count), key=lambda t: (-abs(t - own), -abs(2 * t - z_count + 1))) for own in range(z_count)]

    def target_at(i):
        code = sum(orders[own][i] << (bits * own) for own in range(z_count))
        return lax.shift_right_logical(jnp.int32(code), (bits * z).astype(jnp.int32)) % (1 << bits)

    turns = [(i, c) for i in range(z_count) for c in range(CHUNKS)]
    for c, (offset, size) in enumerate(chunks):
        for f in range(4):
            sums = jnp.dot(
                weights_t, q_ref[:, f * part + offset:f * part + offset + size],
                preferred_element_type=f32,
            )
            terms[f, :, :, lanes(c)] = (
                (sums * INVERSE_TEMP).astype(bf16).reshape(slots, block, size)
            )
        if c < AHEAD:
            push(target_at(0), c)
    for f in range(4):
        sums = jnp.dot(weights, cols[f].reshape(slots * block, part), preferred_element_type=f32)
        sums = sums * INVERSE_TEMP
        qg_ref[:, f * part:(f + 1) * part] = sums.astype(bf16)
        topbuf[dp, :, f * part:(f + 1) * part] = sums[0:1]

    qg_copy = pltpu.make_async_copy(qg_ref, qg_hbm, store_s.at[0])
    qg_copy.start()

    def top_copy(j):
        return remote(topbuf.at[dp], topbuf.at[dp], top_s.at[j], top_r.at[dp], (section, j))

    @pl.when(section == 1)
    def _():
        others(dp_count, dp, lambda j: top_copy(j).start())

    def cot_copy(j):
        return remote(cbuf.at[dp], cbuf.at[dp], cot_s.at[j], cot_r.at[dp], (1 - section, j))

    def layer(own):
        inner = (cot[...] * slope_ref[...]).astype(bf16)
        loads[2].wait()
        back = lax.dot_general(inner, w_ref[...], contract_last, preferred_element_type=f32)
        updated = own + back
        gi_ref[...] = updated
        inner_ref[...] = inner
        return updated

    def last_section():
        others(dp_count, dp, lambda j: remote(
            topbuf.at[j], topbuf.at[j], top_s.at[j], top_r.at[j], (section, j)).wait_recv())
        own = jnp.zeros((micro, col), f32)
        for j in range(dp_count):
            cot[j:j + 1, :] = topbuf[j]
        for j in range(dp_count):
            own = jnp.where(dp == j, cot[:, j * col:(j + 1) * col], own)
        updated = layer(own)
        cbuf[dp, :, :col] = updated
        others(dp_count, dp_count, lambda j: cot_copy(j).start())

    def summed(zt, c):
        others(PLANE, me, lambda g: push_wait(zt, g, c).wait_recv())
        size = chunks[c][1]
        return jnp.dot(
            sel_t[...], tin[zt, :, :, :, lanes(c)].reshape(total, size),
            preferred_element_type=f32,
        ).reshape(rows, block_total, size)

    def sum_copy(source, dest, sems, h, c, step):
        return remote(
            source.at[h, :, :, lanes(c)], dest.at[h, :, :, lanes(c)],
            sum_s.at[sems, h, c], sum_r.at[sems, h, c], (section, dp + step * GROUP),
        )

    def line_sum(value, h, c, step, sems, out, incoming, beyond):
        out[h - 1, :, :, lanes(c)] = value.astype(bf16)

        @pl.when(beyond)
        def _():
            sum_copy(out, incoming, sems, h, c, -step).wait_recv()
            both = value + incoming[h, :, :, lanes(c)].astype(f32)
            out[h - 1, :, :, lanes(c)] = both.astype(bf16)

        sum_copy(out, incoming, sems, h - 1, c, step).start()

    def fin_copy(i, c):
        return remote(
            fin.at[pl.ds((i % 2) * stripe, stripe), :, lanes(c)],
            final_in.at[quarter, :, :, lanes(c)],
            fin_s.at[i, c], fin_r.at[quarter, c], (i // 2, z * GROUP + x * 2 + i % 2),
        )

    def fin_wait(i, c):
        return remote(
            fin.at[pl.ds(core * stripe, stripe), :, lanes(c)], final_in.at[i, :, :, lanes(c)],
            fin_s.at[i, c], fin_r.at[i, c], (i // 2, z * GROUP + x * 2 + i % 2),
        )

    def own_sum(value, c):
        zero = jnp.zeros_like(value)

        @pl.when(z > 0)
        def _():
            sum_copy(up_out, up_sum, 0, 0, c, -1).wait_recv()

        @pl.when(z < z_count - 1)
        def _():
            sum_copy(down_out, down_sum, 1, 0, c, 1).wait_recv()

        below = jnp.where(z > 0, up_sum[0, :, :, lanes(c)].astype(f32), zero)
        above = jnp.where(z < z_count - 1, down_sum[0, :, :, lanes(c)].astype(f32), zero)
        fin[:, :, lanes(c)] = (value + below + above).astype(bf16)
        others(4, quarter, lambda i: fin_copy(i, c).start())
        final_in[quarter, :, :, lanes(c)] = fin[pl.ds(core * stripe, stripe), :, lanes(c)]

    for turn, (i, c) in enumerate(turns):
        zt = target_at(i)
        value = summed(zt, c)
        if turn + AHEAD < len(turns):
            push(target_at(turns[turn + AHEAD][0]), turns[turn + AHEAD][1])
        if i == z_count - 1:
            own_sum(value, c)
            continue

        @pl.when(zt > z)
        def _():
            line_sum(value, zt - z, c, 1, 0, up_out, up_sum, z > 0)

        @pl.when(zt < z)
        def _():
            line_sum(value, z - zt, c, -1, 1, down_out, down_sum, z < z_count - 1)

        if turn == CHUNKS:
            pl.when(section == 1)(last_section)

    @pl.when(section == 0)
    def _():
        def wait(j, carry):
            remote(cbuf.at[j], cbuf.at[j], cot_s.at[j], cot_r.at[j], (1 - section, j)).wait_recv()
            return carry
        lax.fori_loop(0, dp_count, wait, 0)
        cot[...] = jnp.concatenate([cbuf[j][:, :col] for j in range(dp_count)], axis=1)
        layer(cbuf[dp][:, :col])

    for c in range(CHUNKS):
        others(4, quarter, lambda i: fin_wait(i, c).wait_recv())
    for f in range(4):
        pg_ref[:, :, f * part:(f + 1) * part] = final_in[f]

    qg_copy.wait()
    cand_copy.wait_send()
    half_copy.wait_send()
    for h in range(z_count - 1):
        for c in range(CHUNKS):
            @pl.when((z >= h) & (z < z_count - 1))
            def _():
                line_copy(up_in.at[h], up_in, 0, h, c, 1).wait_send()

            @pl.when((z + h < z_count) & (z > 0))
            def _():
                line_copy(down_in.at[h], down_in, 1, h, c, -1).wait_send()

            @pl.when(z + h + 1 < z_count)
            def _():
                sum_copy(up_out, up_sum, 0, h, c, 1).wait_send()

            @pl.when(z >= h + 1)
            def _():
                sum_copy(down_out, down_sum, 1, h, c, -1).wait_send()

    def sent(zs, carry):
        for c in range(CHUNKS):
            others(PLANE, me, lambda g: pull_copy(zs, g, c).wait_send())
            others(PLANE, me, lambda g: push_copy(zs, g, c).wait_send())
        return carry

    lax.fori_loop(0, z_count, sent, 0)
    others(dp_count, dp, lambda j: pre_copy(j).wait_send())

    @pl.when(section == 1)
    def _():
        others(dp_count, dp, lambda j: top_copy(j).wait_send())
        others(dp_count, dp_count, lambda j: cot_copy(j).wait_send())

    for c in range(CHUNKS):
        others(4, quarter, lambda i: fin_copy(i, c).wait_send())


def finish_kernel(qg_in, pg_in, gi_in, inner_ref, inp_ref, qg_ref, pg_ref, gi_ref, wg_ref, sems):
    copies = [
        pltpu.make_async_copy(qg_in, qg_ref, sems.at[0]),
        pltpu.make_async_copy(pg_in, pg_ref, sems.at[1]),
    ]
    for copy in copies:
        copy.start()
    gi_ref[...] = gi_in[...]
    part = inner_ref.shape[1] // 4
    for f in range(4):
        wg_ref[:, f * part:(f + 1) * part] = lax.dot_general(
            inp_ref[...], inner_ref[:, f * part:(f + 1) * part],
            (((0,), (0,)), ((), ())), preferred_element_type=jnp.float32,
        ).astype(wg_ref.dtype)
    for copy in copies:
        copy.wait()


def plane_body(queries, passages, candidates, counts, teacher, section_weights, section_inputs, pre_acts):
    dp_count = lax.axis_size("dp")
    z_count = dp_count // GROUP
    stripe, block_total, width = passages.shape
    block = queries.shape[0]
    slots = candidates.shape[1]
    part = width // 4
    rows = 2 * stripe
    micro, col = section_inputs.shape[1:]
    wide = -(-col // 128) * 128
    f32, bf16, i32 = jnp.float32, jnp.bfloat16, jnp.int32
    table = candidates.T
    vmem, dma = pltpu.VMEM, pltpu.SemaphoreType.DMA
    hop = z_count - 1
    scratch = [
        vmem(queries.shape, bf16),
        vmem(teacher.shape, f32),
        vmem(section_weights.shape[1:], bf16),
        vmem(queries.shape, bf16),
        vmem((micro, width), f32),
        dma((3,)), dma((1,)),
        vmem(table.shape, i32),
        vmem((rows, block_total, part), bf16),
        vmem((hop, rows, block_total, part), bf16),
        vmem((hop, rows, block_total, part), bf16),
        vmem((PLANE * slots * rows, rows * block_total), bf16),
        vmem((rows * block_total, PLANE * slots * rows), bf16),
        vmem((z_count, PLANE, slots, rows, part), bf16),
        vmem((4, slots, block, part), bf16),
        vmem((block, slots * block), f32),
        vmem((4, slots, block, part), bf16),
        vmem((z_count, PLANE, slots, rows, part), bf16),
        vmem((hop, rows, block_total, part), bf16),
        vmem((hop, rows, block_total, part), bf16),
        vmem((hop, rows, block_total, part), bf16),
        vmem((hop, rows, block_total, part), bf16),
        vmem((rows, block_total, part), bf16),
        vmem((4, stripe, block_total, part), bf16),
        vmem((dp_count, micro, wide), bf16),
        vmem((dp_count, 1, width), f32),
        vmem((dp_count, micro, wide), f32),
        vmem((micro, width), f32),
        dma((1,)), dma((1,)), dma((1,)), dma((1,)),
        dma((2, hop, CHUNKS)), dma((2, hop, CHUNKS)),
        dma((z_count, PLANE, CHUNKS)), dma((z_count, PLANE, CHUNKS)),
        dma((z_count, PLANE, CHUNKS)), dma((z_count, PLANE, CHUNKS)),
        dma((2, hop, CHUNKS)), dma((2, hop, CHUNKS)),
        dma((4, CHUNKS)), dma((4, CHUNKS)),
        dma((dp_count,)), dma((dp_count,)),
        dma((dp_count,)), dma((dp_count,)),
        dma((dp_count,)), dma((dp_count,)),
    ]
    here, there = pl.BlockSpec(memory_space=vmem), pl.BlockSpec(memory_space=pl.ANY)
    query_grads, passage_grads, grad_inputs, inner = pl.pallas_call(
        relay_kernel,
        out_shape=(
            jax.ShapeDtypeStruct(queries.shape, bf16),
            jax.ShapeDtypeStruct(passages.shape, bf16),
            jax.ShapeDtypeStruct((micro, col), f32),
            jax.ShapeDtypeStruct((micro, width), bf16),
        ),
        in_specs=[there, here, here, here, there, there, here],
        out_specs=(there, here, here, here),
        scratch_shapes=scratch,
        compiler_params=pltpu.CompilerParams(
            collective_id=0, has_side_effects=True, vmem_limit_bytes=56 * 1024 * 1024
        ),
    )(queries, passages, table, counts[None], teacher, section_weights[0], pre_acts[0])
    query_grads, passage_grads, grad_inputs, weight_grads = pl.pallas_call(
        finish_kernel,
        out_shape=(
            jax.ShapeDtypeStruct(queries.shape, bf16),
            jax.ShapeDtypeStruct(passages.shape, bf16),
            jax.ShapeDtypeStruct((micro, col), f32),
            jax.ShapeDtypeStruct(section_weights.shape[1:], bf16),
        ),
        in_specs=[there, there, here, here, here],
        out_specs=(there, there, here, here),
        scratch_shapes=[dma((2,))],
        compiler_params=pltpu.CompilerParams(vmem_limit_bytes=60 * 1024 * 1024),
    )(query_grads, passage_grads, grad_inputs, inner, section_inputs[0])
    return query_grads, passage_grads, grad_inputs[None], weight_grads[None]


def body(queries, passages, candidates, counts, teacher, section_weights, section_inputs, pre_acts):
    sections, dp_count = lax.axis_size("section"), lax.axis_size("dp")
    stripe, block_total, width = passages.shape
    by_planes = (
        sections == 2
        and dp_count == 16
        and stripe == 8
        and block_total == 16
        and width % 512 == 0
        and candidates.shape[0] == dp_count
        and candidates.shape[1] * dp_count * stripe == teacher.shape[1]
        and section_inputs.shape[1] == dp_count
    )
    chosen = plane_body if by_planes else general_body
    return chosen(
        queries, passages, candidates, counts, teacher, section_weights, section_inputs, pre_acts
    )


def solution(mesh):
    placed = (
        P(("section", "dp"), None),
        P("dp", None, None),
        P("section", None),
        P("section"),
        P(("section", "dp"), None),
        P("section", "dp", None),
        P("section", None, "dp"),
        P("section", None, "dp"),
    )
    return jax.shard_map(
        body,
        mesh=mesh,
        in_specs=placed,
        out_specs=(
            P(("section", "dp"), None),
            P("dp", None, None),
            P("section", None, "dp"),
            P("section", "dp", None),
        ),
        check_vma=False,
    )
```

```python
import functools

import jax
import jax.numpy as jnp
from jax import lax
from jax.experimental import pallas as pl
from jax.experimental.pallas import tpu as pltpu
from jax.sharding import PartitionSpec as P

INVERSE_TEMP = 20.0


def passed_along(value, axis, steps):
    count = lax.axis_size(axis)
    initial, last = (max(0, -steps), min(count, count - steps))
    return lax.ppermute(value, axis, [(source, source + steps) for source in range(initial, last)])


def soft_weights(logits, valid):
    masked = jnp.where(valid, logits, -1e30)
    highest = jnp.max(masked, axis=-1, keepdims=True)
    expons = jnp.where(valid, jnp.exp(masked - highest), 0.0)
    return expons / jnp.sum(expons, axis=-1, keepdims=True)


def general_body(queries, passages, candidates, counts, teacher, section_weights, section_inputs, pre_acts):
    dp_count = lax.axis_size("dp")
    dp_index = lax.axis_index("dp")
    stripe, block_total, width = passages.shape
    row_block_count = stripe * dp_count
    blocks_here = candidates.shape[0] // dp_count
    slot_count = candidates.shape[1]
    requests = blocks_here * slot_count
    all_slots = candidates.reshape(-1)
    outgoing = jnp.take(passages, all_slots, axis=1)
    pulled_rows = lax.all_to_all(outgoing, "dp", split_axis=1, concat_axis=0, tiled=True)
    pulled_rows = pulled_rows.reshape(row_block_count, blocks_here, slot_count, width)
    own_counts = lax.dynamic_slice_in_dim(counts, dp_index * blocks_here, blocks_here)
    slot_valid = jnp.arange(slot_count, dtype=jnp.int32)[None, :] < own_counts[:, None]
    column_valid = jnp.repeat(slot_valid, row_block_count, axis=1)[:, None, :]
    query_row_items = queries.reshape(blocks_here, row_block_count, width)
    logits = (
        jnp.einsum(
            "ixp,wifp->ixfw", query_row_items, pulled_rows, preferred_element_type=jnp.float32
        )
        * INVERSE_TEMP
    )
    logits = logits.reshape(blocks_here, row_block_count, slot_count * row_block_count)
    target_logits = soft_weights(
        teacher.reshape(blocks_here, row_block_count, slot_count * row_block_count), column_valid
    )
    weight_matrices = (soft_weights(logits, column_valid) - target_logits).astype(jnp.bfloat16)
    weight_matrices = weight_matrices.reshape(
        blocks_here, row_block_count, slot_count, row_block_count
    )
    query_sums = (
        jnp.einsum(
            "geal,lgay->gey", weight_matrices, pulled_rows, preferred_element_type=jnp.float32
        )
        * INVERSE_TEMP
    )
    passage_sums = (
        jnp.einsum(
            "fnyw,fnj->wfyj", weight_matrices, query_row_items, preferred_element_type=jnp.float32
        )
        * INVERSE_TEMP
    )
    block_terms = passage_sums.reshape(row_block_count, requests, width).astype(jnp.bfloat16)
    micro_count = section_inputs.shape[1] // dp_count
    col_width = width // dp_count
    micro_cols = jnp.transpose(
        query_sums[0, :micro_count].reshape(micro_count, dp_count, col_width), (1, 0, 2)
    )
    incoming_piece = lax.all_to_all(block_terms, "dp", split_axis=0, concat_axis=1, tiled=True)
    entry = lax.all_to_all(micro_cols, "dp", split_axis=0, concat_axis=1, tiled=True)
    onehot = (all_slots[:, None] == jnp.arange(block_total, dtype=jnp.int32)[None, :]).astype(
        jnp.float32
    )
    dense = jnp.einsum(
        "sjd,jn->snd",
        incoming_piece.astype(jnp.float32),
        onehot,
        precision=lax.Precision.HIGHEST,
        preferred_element_type=jnp.float32,
    )
    passage_out = lax.psum(dense, "section").astype(jnp.bfloat16)
    weight_rows = section_weights[0]
    input_cols = section_inputs[0]
    pre = pre_acts[0].astype(jnp.float32)
    sigma = jax.nn.sigmoid(pre)
    slope = sigma * (1.0 + pre * (1.0 - sigma))
    carry = entry.reshape(dp_count * micro_count, col_width)
    section_count = lax.axis_size("section")
    section_index = lax.axis_index("section")
    grad_cols = jnp.zeros_like(carry)
    grad_weight = jnp.zeros((col_width, width), jnp.float32)
    for section_turn in range(section_count):
        active_flag = section_count - 1 - section_turn
        inner = (carry * slope).astype(jnp.bfloat16)
        piece = lax.all_gather(inner, "dp", axis=1, tiled=True)
        back_sum = jnp.einsum("mj,ij->mi", piece, weight_rows, preferred_element_type=jnp.float32)
        weight_part = jnp.einsum("mi,mj->ij", input_cols, piece, preferred_element_type=jnp.float32)
        back_sum, layer_weight = (back_sum, weight_part)
        updated = carry + back_sum
        is_active = section_index == active_flag
        grad_cols = jnp.where(is_active, updated, grad_cols)
        grad_weight = jnp.where(is_active, layer_weight, grad_weight)
        if section_turn + 1 < section_count:
            carry = passed_along(updated, "section", -1)
    return (
        query_sums.reshape(blocks_here * row_block_count, width).astype(jnp.bfloat16),
        passage_out,
        grad_cols[None],
        grad_weight[None].astype(jnp.bfloat16),
    )


PLANE = 8
GROUP = 4


def chunks_of(width, count):
    lanes, edges = width // 128, [0]
    for i in range(count):
        edges.append(edges[-1] + -(-(lanes - edges[-1]) // (count - i)))
    return [(128 * a, 128 * (b - a)) for a, b in zip(edges, edges[1:])]


CHUNKS = 3
AHEAD = 3


def cells(width, ref, index):
    return ref.at[:, :, pl.ds(pl.multiple_of(index * width, width), width)]


def relay_kernel(
    q_hbm, p_ref, cand_ref, count_ref, teacher_hbm, w_hbm, pre_ref,
    qg_hbm, pg_ref, gi_ref, inner_ref,
    q_ref, teacher_ref, w_ref, qg_ref, slope_ref, load_s, store_s,
    candx, shard, up_in, down_in, sel, sel_t, stage, cols, target, terms, tin,
    up_out, up_sum, down_out, down_sum, fin, final_in, prebuf, topbuf, cbuf, cot,
    cand_s, cand_r, half_s, half_r, line_s, line_r, pull_s, pull_r, push_s, push_r,
    sum_s, sum_r, fin_s, fin_r, pre_s, pre_r, top_s, top_r, cot_s, cot_r,
):
    dp_count = lax.axis_size("dp")
    section = lax.axis_index("section")
    dp = lax.axis_index("dp")
    z = dp // GROUP
    x = (dp // 2) % 2
    core = dp % 2
    me = x * 4 + section * 2 + core
    quarter = section * 2 + core
    z_count = dp_count // GROUP
    stripe, block_total, width = p_ref.shape
    part = width // 4
    rows = 2 * stripe
    block = q_ref.shape[0]
    slots = teacher_ref.shape[1] // block
    micro, col = pre_ref.shape
    f32, bf16 = jnp.float32, jnp.bfloat16
    chunks = chunks_of(part, CHUNKS)

    def lanes(c):
        return pl.ds(*chunks[c])

    def remote(source, dest, send, recv, device):
        return pltpu.make_async_remote_copy(
            src_ref=source, dst_ref=dest, send_sem=send, recv_sem=recv,
            device_id=device, device_id_type=pl.DeviceIdType.MESH,
        )

    def member(g):
        return ((g // 2) % 2, z * GROUP + (g // 4) * 2 + g % 2)

    def others(count, own, act):
        def step(i, carry):
            act((own + i) % count)
            return carry
        lax.fori_loop(1, count, step, 0)

    def peers(act):
        def step(j, carry):
            i = (j * 5) % PLANE
            act(
                (x + i // 4) % 2 * 4
                + (section + (i // 2) % 2) % 2 * 2
                + (core + i % 2) % 2
            )
            return carry
        lax.fori_loop(1, PLANE, step, 0)

    def each(count, act):
        def step(i, carry):
            act(i)
            return carry
        lax.fori_loop(0, count, step, 0)

    loads = [
        pltpu.make_async_copy(source, dest, load_s.at[i])
        for i, (source, dest) in enumerate(
            ((q_hbm, q_ref), (teacher_hbm, teacher_ref), (w_hbm, w_ref))
        )
    ]
    for load in loads:
        load.start()

    barrier = pltpu.get_barrier_semaphore()
    everyone = 2 * dp_count

    def greet(i):
        pl.semaphore_signal(
            barrier, inc=1, device_id=(i // dp_count, i % dp_count),
            device_id_type=pl.DeviceIdType.MESH,
        )

    others(everyone, section * dp_count + dp, greet)
    pl.semaphore_wait(barrier, everyone - 1)

    cand_copy = remote(cand_ref, candx, cand_s.at[0], cand_r.at[0], (1 - section, dp))
    cand_copy.start()
    partner = dp + 1 - 2 * core
    half_copy = remote(
        cells(part, p_ref, section * 2 + 1 - core), shard.at[pl.ds(core * stripe, stripe)],
        half_s.at[0], half_r.at[0], (section, partner),
    )
    half_copy.start()
    shard[pl.ds(core * stripe, stripe)] = p_ref[
        :, :, pl.ds(pl.multiple_of(quarter * part, part), part)
    ]
    half_wait = remote(
        cells(part, p_ref, quarter), shard.at[pl.ds((1 - core) * stripe, stripe)],
        half_s.at[0], half_r.at[0], (section, partner),
    )
    half_wait.wait_recv()

    def line_copy(source, ref, sems, h, c, step):
        return remote(
            source.at[:, :, lanes(c)], ref.at[h, :, :, lanes(c)],
            line_s.at[sems, h, c], line_r.at[sems, h, c], (section, dp + step * GROUP),
        )

    @pl.when(z < z_count - 1)
    def _():
        for c in range(CHUNKS):
            line_copy(shard, up_in, 0, 0, c, 1).start()

    @pl.when(z > 0)
    def _():
        for c in range(CHUNKS):
            line_copy(shard, down_in, 1, 0, c, -1).start()

    cand_copy.wait_recv()
    total = PLANE * slots * rows
    listed_shape = (total, dp_count)
    at_row = lax.broadcasted_iota(jnp.int32, listed_shape, 0)
    lane = lax.broadcasted_iota(jnp.int32, listed_shape, 1)
    g_of = at_row // (slots * rows)
    slot_of = (at_row // rows) % slots
    here = (g_of // 2) % 2 == section
    listed = jnp.zeros(listed_shape, f32)
    for slot in range(slots):
        mine = cand_ref[slot:slot + 1, :].astype(f32)
        away = candx[slot:slot + 1, :].astype(f32)
        listed = jnp.where(slot_of == slot, jnp.where(here, mine, away), listed)
    picked_lane = lane == z * GROUP + (g_of // 4) * 2 + g_of % 2
    wanted = jnp.sum(jnp.where(picked_lane, listed, 0.0), axis=1, keepdims=True)
    shape = (total, rows * block_total)
    row_of = lax.broadcasted_iota(jnp.int32, shape, 0) % rows
    place = lax.broadcasted_iota(jnp.int32, shape, 1)
    hit = (place // block_total == row_of) & ((place % block_total).astype(f32) == wanted)
    onehot = jnp.where(hit, 1.0, 0.0)
    sel[...] = onehot.astype(bf16)
    sel_t[...] = jnp.transpose(onehot).astype(bf16)

    def own_rows(zs, at_x):
        return pl.ds(pl.multiple_of(zs * GROUP * stripe + at_x * rows, rows), rows)

    def pull_copy(zs, g, c):
        return remote(
            stage.at[zs, g, :, :, lanes(c)], cols.at[quarter, :, own_rows(zs, x), lanes(c)],
            pull_s.at[zs, g, c], pull_r.at[zs, me, c], member(g),
        )

    def pull_wait(zs, g, c):
        return remote(
            stage.at[zs, g, :, :, lanes(c)], cols.at[g % 4, :, own_rows(zs, g // 4), lanes(c)],
            pull_s.at[zs, g, c], pull_r.at[zs, g, c], member(g),
        )

    def spread(ref, zs, c):
        size = chunks[c][1]
        picked = jnp.dot(
            sel[...], ref[:, :, lanes(c)].reshape(rows * block_total, size),
            preferred_element_type=f32,
        )
        stage[zs, :, :, :, lanes(c)] = picked.astype(bf16).reshape(PLANE, slots, rows, size)
        peers(lambda g: pull_copy(zs, g, c).start())
        cols[quarter, :, own_rows(zs, x), lanes(c)] = stage[zs, me, :, :, lanes(c)]

    for c in range(CHUNKS):
        spread(shard, z, c)

    prebuf[dp, :, :col] = pre_ref[...]

    def pre_copy(j):
        return remote(prebuf.at[dp], prebuf.at[dp], pre_s.at[j], pre_r.at[dp], (section, j))

    others(dp_count, dp, lambda j: pre_copy(j).start())

    def soft(values, valid):
        masked = jnp.where(valid, values, -1e30)
        highest = jnp.max(masked, axis=-1, keepdims=True)
        expons = jnp.where(valid, jnp.exp(masked - highest), 0.0)
        return expons / jnp.sum(expons, axis=-1, keepdims=True)

    own_row = count_ref[...].astype(f32)
    own_lane = lax.broadcasted_iota(jnp.int32, own_row.shape, 1)
    how_many = jnp.sum(jnp.where(own_lane == dp, own_row, 0.0), axis=1, keepdims=True)
    slot_lane = lax.broadcasted_iota(jnp.int32, teacher_ref.shape, 1) // block
    valid = slot_lane.astype(f32) < how_many
    loads[1].wait()
    target[...] = soft(teacher_ref[...], valid)
    loads[0].wait()

    def slopes():
        others(dp_count, dp, lambda j: remote(
            prebuf.at[j], prebuf.at[j], pre_s.at[j], pre_r.at[j], (section, j)).wait_recv())
        pre = jnp.concatenate([prebuf[j].astype(f32)[:, :col] for j in range(dp_count)], axis=1)
        sigma = 1.0 / (1.0 + jnp.exp(-pre))
        slope_ref[...] = sigma * (1.0 + pre * (1.0 - sigma))

    def hop(h, c):
        @pl.when(z >= h + 1)
        def _():
            line_copy(shard, up_in, 0, h, c, -1).wait_recv()
            if h + 1 < z_count - 1:
                @pl.when(z < z_count - 1)
                def _():
                    line_copy(up_in.at[h], up_in, 0, h + 1, c, 1).start()

        @pl.when(z + h + 1 < z_count)
        def _():
            line_copy(shard, down_in, 1, h, c, 1).wait_recv()
            if h + 1 < z_count - 1:
                @pl.when(z > 0)
                def _():
                    line_copy(down_in.at[h], down_in, 1, h + 1, c, -1).start()

        @pl.when(z >= h + 1)
        def _():
            spread(up_in.at[h], z - h - 1, c)

        @pl.when(z + h + 1 < z_count)
        def _():
            spread(down_in.at[h], z + h + 1, c)

    for h in range(z_count - 1):
        if h == z_count - 2:
            slopes()
        for c in range(CHUNKS):
            hop(h, c)

    contract_last = (((1,), (1,)), ((), ()))
    logits = jnp.zeros((block, slots * block), f32)
    for c, (offset, size) in enumerate(chunks):
        for zs in range(z_count):
            peers(lambda g: pull_wait(zs, g, c).wait_recv())
        for f in range(4):
            logits += lax.dot_general(
                q_ref[:, f * part + offset:f * part + offset + size],
                cols[f, :, :, lanes(c)].reshape(slots * block, size),
                contract_last, preferred_element_type=f32,
            )
    weights32 = soft(logits * INVERSE_TEMP, valid) - target[...]
    weights = weights32.astype(bf16)
    weights_t = jnp.transpose(weights32).astype(bf16)
    def push_copy(zt, g, c):
        return remote(
            terms.at[g % 4, :, own_rows(zt, g // 4), lanes(c)], tin.at[zt, me, :, :, lanes(c)],
            push_s.at[zt, g, c], push_r.at[zt, me, c], member(g),
        )

    def push_wait(zt, g, c):
        return remote(
            terms.at[quarter, :, own_rows(zt, x), lanes(c)], tin.at[zt, g, :, :, lanes(c)],
            push_s.at[zt, g, c], push_r.at[zt, g, c], member(g),
        )

    def push(zt, c):
        peers(lambda g: push_copy(zt, g, c).start())
        tin[zt, me, :, :, lanes(c)] = terms[quarter, :, own_rows(zt, x), lanes(c)]

    bits = max(1, (z_count - 1).bit_length())
    orders = [sorted(range(z_count), key=lambda t: (-abs(t - own), -abs(2 * t - z_count + 1))) for own in range(z_count)]

    def target_at(i):
        code = sum(orders[own][i] << (bits * own) for own in range(z_count))
        return lax.shift_right_logical(jnp.int32(code), (bits * z).astype(jnp.int32)) % (1 << bits)

    turns = [(i, c) for i in range(z_count) for c in range(CHUNKS)]
    for c, (offset, size) in enumerate(chunks):
        for f in range(4):
            sums = jnp.dot(
                weights_t, q_ref[:, f * part + offset:f * part + offset + size],
                preferred_element_type=f32,
            )
            terms[f, :, :, lanes(c)] = (
                (sums * INVERSE_TEMP).astype(bf16).reshape(slots, block, size)
            )
        if c < AHEAD:
            push(target_at(0), c)
    for f in range(4):
        sums = jnp.dot(weights, cols[f].reshape(slots * block, part), preferred_element_type=f32)
        sums = sums * INVERSE_TEMP
        qg_ref[:, f * part:(f + 1) * part] = sums.astype(bf16)
        topbuf[dp, :, f * part:(f + 1) * part] = sums[0:1]

    qg_copy = pltpu.make_async_copy(qg_ref, qg_hbm, store_s.at[0])
    qg_copy.start()

    def top_copy(j):
        return remote(topbuf.at[dp], topbuf.at[dp], top_s.at[j], top_r.at[dp], (section, j))

    @pl.when(section == 1)
    def _():
        others(dp_count, dp, lambda j: top_copy(j).start())

    def cot_copy(j):
        return remote(cbuf.at[dp], cbuf.at[dp], cot_s.at[j], cot_r.at[dp], (1 - section, j))

    def layer(own):
        inner = (cot[...] * slope_ref[...]).astype(bf16)
        loads[2].wait()
        back = lax.dot_general(inner, w_ref[...], contract_last, preferred_element_type=f32)
        updated = own + back
        gi_ref[...] = updated
        inner_ref[...] = inner
        return updated

    def last_section():
        others(dp_count, dp, lambda j: remote(
            topbuf.at[j], topbuf.at[j], top_s.at[j], top_r.at[j], (section, j)).wait_recv())
        own = jnp.zeros((micro, col), f32)
        for j in range(dp_count):
            cot[j:j + 1, :] = topbuf[j]
        for j in range(dp_count):
            own = jnp.where(dp == j, cot[:, j * col:(j + 1) * col], own)
        updated = layer(own)
        cbuf[dp, :, :col] = updated
        each(dp_count, lambda j: cot_copy(j).start())

    def summed(zt, c):
        peers(lambda g: push_wait(zt, g, c).wait_recv())
        size = chunks[c][1]
        return jnp.dot(
            sel_t[...], tin[zt, :, :, :, lanes(c)].reshape(total, size),
            preferred_element_type=f32,
        ).reshape(rows, block_total, size)

    def sum_copy(source, dest, sems, h, c, step):
        return remote(
            source.at[h, :, :, lanes(c)], dest.at[h, :, :, lanes(c)],
            sum_s.at[sems, h, c], sum_r.at[sems, h, c], (section, dp + step * GROUP),
        )

    def line_sum(value, h, c, step, sems, out, incoming, beyond):
        out[h - 1, :, :, lanes(c)] = value.astype(bf16)

        @pl.when(beyond)
        def _():
            sum_copy(out, incoming, sems, h, c, -step).wait_recv()
            both = value + incoming[h, :, :, lanes(c)].astype(f32)
            out[h - 1, :, :, lanes(c)] = both.astype(bf16)

        sum_copy(out, incoming, sems, h - 1, c, step).start()

    def fin_copy(i, c):
        return remote(
            fin.at[pl.ds((i % 2) * stripe, stripe), :, lanes(c)],
            final_in.at[quarter, :, :, lanes(c)],
            fin_s.at[i, c], fin_r.at[quarter, c], (i // 2, z * GROUP + x * 2 + i % 2),
        )

    def fin_wait(i, c):
        return remote(
            fin.at[pl.ds(core * stripe, stripe), :, lanes(c)], final_in.at[i, :, :, lanes(c)],
            fin_s.at[i, c], fin_r.at[i, c], (i // 2, z * GROUP + x * 2 + i % 2),
        )

    def own_sum(value, c):
        zero = jnp.zeros_like(value)

        @pl.when(z > 0)
        def _():
            sum_copy(up_out, up_sum, 0, 0, c, -1).wait_recv()

        @pl.when(z < z_count - 1)
        def _():
            sum_copy(down_out, down_sum, 1, 0, c, 1).wait_recv()

        below = jnp.where(z > 0, up_sum[0, :, :, lanes(c)].astype(f32), zero)
        above = jnp.where(z < z_count - 1, down_sum[0, :, :, lanes(c)].astype(f32), zero)
        fin[:, :, lanes(c)] = (value + below + above).astype(bf16)
        others(4, quarter, lambda i: fin_copy(i, c).start())
        final_in[quarter, :, :, lanes(c)] = fin[pl.ds(core * stripe, stripe), :, lanes(c)]

    for turn, (i, c) in enumerate(turns):
        zt = target_at(i)
        value = summed(zt, c)
        if turn + AHEAD < len(turns):
            push(target_at(turns[turn + AHEAD][0]), turns[turn + AHEAD][1])
        if i == z_count - 1:
            own_sum(value, c)
            continue

        @pl.when(zt > z)
        def _():
            line_sum(value, zt - z, c, 1, 0, up_out, up_sum, z > 0)

        @pl.when(zt < z)
        def _():
            line_sum(value, z - zt, c, -1, 1, down_out, down_sum, z < z_count - 1)

        if turn == CHUNKS:
            pl.when(section == 1)(last_section)

    @pl.when(section == 0)
    def _():
        def wait(j, carry):
            remote(cbuf.at[j], cbuf.at[j], cot_s.at[j], cot_r.at[j], (1 - section, j)).wait_recv()
            return carry
        lax.fori_loop(0, dp_count, wait, 0)
        cot[...] = jnp.concatenate([cbuf[j][:, :col] for j in range(dp_count)], axis=1)
        layer(cbuf[dp][:, :col])

    for c in range(CHUNKS):
        others(4, quarter, lambda i: fin_wait(i, c).wait_recv())
    for f in range(4):
        pg_ref[:, :, f * part:(f + 1) * part] = final_in[f]

    qg_copy.wait()
    cand_copy.wait_send()
    half_copy.wait_send()
    for h in range(z_count - 1):
        for c in range(CHUNKS):
            @pl.when((z >= h) & (z < z_count - 1))
            def _():
                line_copy(up_in.at[h], up_in, 0, h, c, 1).wait_send()

            @pl.when((z + h < z_count) & (z > 0))
            def _():
                line_copy(down_in.at[h], down_in, 1, h, c, -1).wait_send()

            @pl.when(z + h + 1 < z_count)
            def _():
                sum_copy(up_out, up_sum, 0, h, c, 1).wait_send()

            @pl.when(z >= h + 1)
            def _():
                sum_copy(down_out, down_sum, 1, h, c, -1).wait_send()

    def sent(zs, carry):
        for c in range(CHUNKS):
            peers(lambda g: pull_copy(zs, g, c).wait_send())
            peers(lambda g: push_copy(zs, g, c).wait_send())
        return carry

    lax.fori_loop(0, z_count, sent, 0)
    others(dp_count, dp, lambda j: pre_copy(j).wait_send())

    @pl.when(section == 1)
    def _():
        others(dp_count, dp, lambda j: top_copy(j).wait_send())
        each(dp_count, lambda j: cot_copy(j).wait_send())

    for c in range(CHUNKS):
        others(4, quarter, lambda i: fin_copy(i, c).wait_send())


def finish_kernel(
    qg_in, pg_in, gi_in, inner_ref, inp_ref, qg_out, pg_out, gi_ref, wg_out,
    qg, pg, wg, in_s, out_s,
):
    held = (qg, pg)
    takes = [
        pltpu.make_async_copy(source, ref, in_s.at[i])
        for i, (source, ref) in enumerate(zip((qg_in, pg_in), held))
    ]
    gives = [
        pltpu.make_async_copy(ref, dest, out_s.at[i])
        for i, (ref, dest) in enumerate(zip(held, (qg_out, pg_out)))
    ]
    for take in takes:
        take.start()
    gi_ref[...] = gi_in[...]
    part = inner_ref.shape[1] // 4
    for f in range(4):
        cut = pl.ds(f * part, part)
        wg[:, cut] = lax.dot_general(
            inp_ref[...], inner_ref[:, cut],
            (((0,), (0,)), ((), ())), preferred_element_type=jnp.float32,
        ).astype(wg.dtype)
        gives.append(pltpu.make_async_copy(wg.at[:, cut], wg_out.at[:, cut], out_s.at[2 + f]))
        gives[-1].start()
    for take, give in zip(takes, gives):
        take.wait()
        give.start()
    for give in gives:
        give.wait()


def plane_body(queries, passages, candidates, counts, teacher, section_weights, section_inputs, pre_acts):
    dp_count = lax.axis_size("dp")
    z_count = dp_count // GROUP
    stripe, block_total, width = passages.shape
    block = queries.shape[0]
    slots = candidates.shape[1]
    part = width // 4
    rows = 2 * stripe
    micro, col = section_inputs.shape[1:]
    wide = -(-col // 128) * 128
    f32, bf16, i32 = jnp.float32, jnp.bfloat16, jnp.int32
    table = candidates.T
    vmem, dma = pltpu.VMEM, pltpu.SemaphoreType.DMA
    hop = z_count - 1
    scratch = [
        vmem(queries.shape, bf16),
        vmem(teacher.shape, f32),
        vmem(section_weights.shape[1:], bf16),
        vmem(queries.shape, bf16),
        vmem((micro, width), f32),
        dma((3,)), dma((1,)),
        vmem(table.shape, i32),
        vmem((rows, block_total, part), bf16),
        vmem((hop, rows, block_total, part), bf16),
        vmem((hop, rows, block_total, part), bf16),
        vmem((PLANE * slots * rows, rows * block_total), bf16),
        vmem((rows * block_total, PLANE * slots * rows), bf16),
        vmem((z_count, PLANE, slots, rows, part), bf16),
        vmem((4, slots, block, part), bf16),
        vmem((block, slots * block), f32),
        vmem((4, slots, block, part), bf16),
        vmem((z_count, PLANE, slots, rows, part), bf16),
        vmem((hop, rows, block_total, part), bf16),
        vmem((hop, rows, block_total, part), bf16),
        vmem((hop, rows, block_total, part), bf16),
        vmem((hop, rows, block_total, part), bf16),
        vmem((rows, block_total, part), bf16),
        vmem((4, stripe, block_total, part), bf16),
        vmem((dp_count, micro, wide), bf16),
        vmem((dp_count, 1, width), f32),
        vmem((dp_count, micro, wide), f32),
        vmem((micro, width), f32),
        dma((1,)), dma((1,)), dma((1,)), dma((1,)),
        dma((2, hop, CHUNKS)), dma((2, hop, CHUNKS)),
        dma((z_count, PLANE, CHUNKS)), dma((z_count, PLANE, CHUNKS)),
        dma((z_count, PLANE, CHUNKS)), dma((z_count, PLANE, CHUNKS)),
        dma((2, hop, CHUNKS)), dma((2, hop, CHUNKS)),
        dma((4, CHUNKS)), dma((4, CHUNKS)),
        dma((dp_count,)), dma((dp_count,)),
        dma((dp_count,)), dma((dp_count,)),
        dma((dp_count,)), dma((dp_count,)),
    ]
    here, there = pl.BlockSpec(memory_space=vmem), pl.BlockSpec(memory_space=pl.ANY)
    query_grads, passage_grads, grad_inputs, inner = pl.pallas_call(
        relay_kernel,
        out_shape=(
            jax.ShapeDtypeStruct(queries.shape, bf16),
            jax.ShapeDtypeStruct(passages.shape, bf16),
            jax.ShapeDtypeStruct((micro, col), f32),
            jax.ShapeDtypeStruct((micro, width), bf16),
        ),
        in_specs=[there, here, here, here, there, there, here],
        out_specs=(there, here, here, here),
        scratch_shapes=scratch,
        compiler_params=pltpu.CompilerParams(
            collective_id=0, has_side_effects=True, vmem_limit_bytes=56 * 1024 * 1024
        ),
    )(queries, passages, table, counts[None], teacher, section_weights[0], pre_acts[0])
    query_grads, passage_grads, grad_inputs, weight_grads = pl.pallas_call(
        finish_kernel,
        out_shape=(
            jax.ShapeDtypeStruct(queries.shape, bf16),
            jax.ShapeDtypeStruct(passages.shape, bf16),
            jax.ShapeDtypeStruct((micro, col), f32),
            jax.ShapeDtypeStruct(section_weights.shape[1:], bf16),
        ),
        in_specs=[there, there, here, here, here],
        out_specs=(there, there, here, there),
        scratch_shapes=[
            vmem(queries.shape, bf16),
            vmem(passages.shape, bf16),
            vmem(section_weights.shape[1:], bf16),
            dma((2,)), dma((6,)),
        ],
        compiler_params=pltpu.CompilerParams(vmem_limit_bytes=60 * 1024 * 1024),
    )(query_grads, passage_grads, grad_inputs, inner, section_inputs[0])
    return query_grads, passage_grads, grad_inputs[None], weight_grads[None]


def body(queries, passages, candidates, counts, teacher, section_weights, section_inputs, pre_acts):
    sections, dp_count = lax.axis_size("section"), lax.axis_size("dp")
    stripe, block_total, width = passages.shape
    by_planes = (
        sections == 2
        and dp_count == 16
        and stripe == 8
        and block_total == 16
        and width % 512 == 0
        and candidates.shape[0] == dp_count
        and candidates.shape[1] * dp_count * stripe == teacher.shape[1]
        and section_inputs.shape[1] == dp_count
    )
    chosen = plane_body if by_planes else general_body
    return chosen(
        queries, passages, candidates, counts, teacher, section_weights, section_inputs, pre_acts
    )


def solution(mesh):
    placed = (
        P(("section", "dp"), None),
        P("dp", None, None),
        P("section", None),
        P("section"),
        P(("section", "dp"), None),
        P("section", "dp", None),
        P("section", None, "dp"),
        P("section", None, "dp"),
    )
    return jax.shard_map(
        body,
        mesh=mesh,
        in_specs=placed,
        out_specs=(
            P(("section", "dp"), None),
            P("dp", None, None),
            P("section", None, "dp"),
            P("section", "dp", None),
        ),
        check_vma=False,
    )
```

```python
import functools

import jax
import jax.numpy as jnp
from jax import lax
from jax.experimental import pallas as pl
from jax.experimental.pallas import tpu as pltpu
from jax.sharding import PartitionSpec as P

INVERSE_TEMP = 20.0


def passed_along(value, axis, steps):
    count = lax.axis_size(axis)
    initial, last = (max(0, -steps), min(count, count - steps))
    return lax.ppermute(value, axis, [(source, source + steps) for source in range(initial, last)])


def soft_weights(logits, valid):
    masked = jnp.where(valid, logits, -1e30)
    highest = jnp.max(masked, axis=-1, keepdims=True)
    expons = jnp.where(valid, jnp.exp(masked - highest), 0.0)
    return expons / jnp.sum(expons, axis=-1, keepdims=True)


def general_body(queries, passages, candidates, counts, teacher, section_weights, section_inputs, pre_acts):
    dp_count = lax.axis_size("dp")
    dp_index = lax.axis_index("dp")
    stripe, block_total, width = passages.shape
    row_block_count = stripe * dp_count
    blocks_here = candidates.shape[0] // dp_count
    slot_count = candidates.shape[1]
    requests = blocks_here * slot_count
    all_slots = candidates.reshape(-1)
    outgoing = jnp.take(passages, all_slots, axis=1)
    pulled_rows = lax.all_to_all(outgoing, "dp", split_axis=1, concat_axis=0, tiled=True)
    pulled_rows = pulled_rows.reshape(row_block_count, blocks_here, slot_count, width)
    own_counts = lax.dynamic_slice_in_dim(counts, dp_index * blocks_here, blocks_here)
    slot_valid = jnp.arange(slot_count, dtype=jnp.int32)[None, :] < own_counts[:, None]
    column_valid = jnp.repeat(slot_valid, row_block_count, axis=1)[:, None, :]
    query_row_items = queries.reshape(blocks_here, row_block_count, width)
    logits = (
        jnp.einsum(
            "ixp,wifp->ixfw", query_row_items, pulled_rows, preferred_element_type=jnp.float32
        )
        * INVERSE_TEMP
    )
    logits = logits.reshape(blocks_here, row_block_count, slot_count * row_block_count)
    target_logits = soft_weights(
        teacher.reshape(blocks_here, row_block_count, slot_count * row_block_count), column_valid
    )
    weight_matrices = (soft_weights(logits, column_valid) - target_logits).astype(jnp.bfloat16)
    weight_matrices = weight_matrices.reshape(
        blocks_here, row_block_count, slot_count, row_block_count
    )
    query_sums = (
        jnp.einsum(
            "geal,lgay->gey", weight_matrices, pulled_rows, preferred_element_type=jnp.float32
        )
        * INVERSE_TEMP
    )
    passage_sums = (
        jnp.einsum(
            "fnyw,fnj->wfyj", weight_matrices, query_row_items, preferred_element_type=jnp.float32
        )
        * INVERSE_TEMP
    )
    block_terms = passage_sums.reshape(row_block_count, requests, width).astype(jnp.bfloat16)
    micro_count = section_inputs.shape[1] // dp_count
    col_width = width // dp_count
    micro_cols = jnp.transpose(
        query_sums[0, :micro_count].reshape(micro_count, dp_count, col_width), (1, 0, 2)
    )
    incoming_piece = lax.all_to_all(block_terms, "dp", split_axis=0, concat_axis=1, tiled=True)
    entry = lax.all_to_all(micro_cols, "dp", split_axis=0, concat_axis=1, tiled=True)
    onehot = (all_slots[:, None] == jnp.arange(block_total, dtype=jnp.int32)[None, :]).astype(
        jnp.float32
    )
    dense = jnp.einsum(
        "sjd,jn->snd",
        incoming_piece.astype(jnp.float32),
        onehot,
        precision=lax.Precision.HIGHEST,
        preferred_element_type=jnp.float32,
    )
    passage_out = lax.psum(dense, "section").astype(jnp.bfloat16)
    weight_rows = section_weights[0]
    input_cols = section_inputs[0]
    pre = pre_acts[0].astype(jnp.float32)
    sigma = jax.nn.sigmoid(pre)
    slope = sigma * (1.0 + pre * (1.0 - sigma))
    carry = entry.reshape(dp_count * micro_count, col_width)
    section_count = lax.axis_size("section")
    section_index = lax.axis_index("section")
    grad_cols = jnp.zeros_like(carry)
    grad_weight = jnp.zeros((col_width, width), jnp.float32)
    for section_turn in range(section_count):
        active_flag = section_count - 1 - section_turn
        inner = (carry * slope).astype(jnp.bfloat16)
        piece = lax.all_gather(inner, "dp", axis=1, tiled=True)
        back_sum = jnp.einsum("mj,ij->mi", piece, weight_rows, preferred_element_type=jnp.float32)
        weight_part = jnp.einsum("mi,mj->ij", input_cols, piece, preferred_element_type=jnp.float32)
        back_sum, layer_weight = (back_sum, weight_part)
        updated = carry + back_sum
        is_active = section_index == active_flag
        grad_cols = jnp.where(is_active, updated, grad_cols)
        grad_weight = jnp.where(is_active, layer_weight, grad_weight)
        if section_turn + 1 < section_count:
            carry = passed_along(updated, "section", -1)
    return (
        query_sums.reshape(blocks_here * row_block_count, width).astype(jnp.bfloat16),
        passage_out,
        grad_cols[None],
        grad_weight[None].astype(jnp.bfloat16),
    )


PLANE = 8
GROUP = 4


def chunks_of(width, count):
    lanes, edges = width // 128, [0]
    for i in range(count):
        edges.append(edges[-1] + -(-(lanes - edges[-1]) // (count - i)))
    return [(128 * a, 128 * (b - a)) for a, b in zip(edges, edges[1:])]


CHUNKS = 2


def cells(width, ref, index):
    return ref.at[:, :, pl.ds(pl.multiple_of(index * width, width), width)]


def relay_kernel(
    q_hbm, p_ref, cand_ref, count_ref, teacher_hbm, w_hbm, pre_ref,
    qg_hbm, pg_ref, gi_ref, inner_ref,
    q_ref, teacher_ref, w_ref, qg_ref, slope_ref, load_s, store_s,
    candx, line_in, sel, sel_t, stage, cols, target, terms, tin,
    sum_out, sum_in, fin, final_in, prebuf, topbuf, cbuf, cot,
    cand_s, cand_r, half_s, half_r, line_s, line_r, pull_s, pull_r, push_s, push_r,
    sum_s, sum_r, fin_s, fin_r, pre_s, pre_r, top_s, top_r, cot_s, cot_r,
):
    dp_count = lax.axis_size("dp")
    section = lax.axis_index("section")
    dp = lax.axis_index("dp")
    z = dp // GROUP
    x = (dp // 2) % 2
    core = dp % 2
    me = x * 4 + section * 2 + core
    quarter = section * 2 + core
    z_count = dp_count // GROUP
    stripe, block_total, width = p_ref.shape
    part = width // 4
    rows = 2 * stripe
    block = q_ref.shape[0]
    slots = teacher_ref.shape[1] // block
    micro, col = pre_ref.shape
    f32, bf16 = jnp.float32, jnp.bfloat16
    chunks = chunks_of(part, CHUNKS)
    hops = z_count - 1
    own_slot = 2 * hops
    shard = line_in.at[own_slot]

    def lanes(c):
        return pl.ds(*chunks[c])

    def remote(source, dest, send, recv, device):
        return pltpu.make_async_remote_copy(
            src_ref=source, dst_ref=dest, send_sem=send, recv_sem=recv,
            device_id=device, device_id_type=pl.DeviceIdType.MESH,
        )

    def member(g):
        return ((g // 2) % 2, z * GROUP + (g // 4) * 2 + g % 2)

    def others(count, own, act):
        def step(i, carry):
            act((own + i) % count)
            return carry
        lax.fori_loop(1, count, step, 0)

    def peers(act):
        def step(j, carry):
            i = (j * 5) % PLANE
            act(
                (x + i // 4) % 2 * 4
                + (section + (i // 2) % 2) % 2 * 2
                + (core + i % 2) % 2
            )
            return carry
        lax.fori_loop(1, PLANE, step, 0)

    def each(count, act):
        def step(i, carry):
            act(i)
            return carry
        lax.fori_loop(0, count, step, 0)

    loads = [
        pltpu.make_async_copy(source, dest, load_s.at[i])
        for i, (source, dest) in enumerate(
            ((q_hbm, q_ref), (teacher_hbm, teacher_ref), (w_hbm, w_ref))
        )
    ]
    for load in loads:
        load.start()

    barrier = pltpu.get_barrier_semaphore()
    everyone = 2 * dp_count

    def greet(i):
        pl.semaphore_signal(
            barrier, inc=1, device_id=(i // dp_count, i % dp_count),
            device_id_type=pl.DeviceIdType.MESH,
        )

    others(everyone, section * dp_count + dp, greet)
    pl.semaphore_wait(barrier, everyone - 1)

    cand_copy = remote(cand_ref, candx, cand_s.at[0], cand_r.at[0], (1 - section, dp))
    cand_copy.start()
    partner = dp + 1 - 2 * core
    half_copy = remote(
        cells(part, p_ref, section * 2 + 1 - core), shard.at[pl.ds(core * stripe, stripe)],
        half_s.at[0], half_r.at[0], (section, partner),
    )
    half_copy.start()
    shard[pl.ds(core * stripe, stripe)] = p_ref[
        :, :, pl.ds(pl.multiple_of(quarter * part, part), part)
    ]
    half_wait = remote(
        cells(part, p_ref, quarter), shard.at[pl.ds((1 - core) * stripe, stripe)],
        half_s.at[0], half_r.at[0], (section, partner),
    )
    half_wait.wait_recv()

    def line_copy(source, d, h, c):
        return remote(
            line_in.at[source, :, :, lanes(c)], line_in.at[d * hops + h, :, :, lanes(c)],
            line_s.at[d, h, c], line_r.at[d, h, c], (section, dp + (1 - 2 * d) * GROUP),
        )

    def line_wait(d, h, c):
        return remote(
            line_in.at[own_slot, :, :, lanes(c)], line_in.at[d * hops + h, :, :, lanes(c)],
            line_s.at[d, h, c], line_r.at[d, h, c], (section, dp - (1 - 2 * d) * GROUP),
        )

    for d, further in enumerate((z < z_count - 1, z > 0)):
        @pl.when(further)
        def _():
            for c in range(CHUNKS):
                line_copy(own_slot, d, 0, c).start()

    cand_copy.wait_recv()
    total = PLANE * slots * rows
    listed_shape = (total, dp_count)
    at_row = lax.broadcasted_iota(jnp.int32, listed_shape, 0)
    lane = lax.broadcasted_iota(jnp.int32, listed_shape, 1)
    g_of = at_row // (slots * rows)
    slot_of = (at_row // rows) % slots
    here = (g_of // 2) % 2 == section
    listed = jnp.zeros(listed_shape, f32)
    for slot in range(slots):
        mine = cand_ref[slot:slot + 1, :].astype(f32)
        away = candx[slot:slot + 1, :].astype(f32)
        listed = jnp.where(slot_of == slot, jnp.where(here, mine, away), listed)
    picked_lane = lane == z * GROUP + (g_of // 4) * 2 + g_of % 2
    wanted = jnp.sum(jnp.where(picked_lane, listed, 0.0), axis=1, keepdims=True)
    shape = (total, rows * block_total)
    row_of = lax.broadcasted_iota(jnp.int32, shape, 0) % rows
    place = lax.broadcasted_iota(jnp.int32, shape, 1)
    hit = (place // block_total == row_of) & ((place % block_total).astype(f32) == wanted)
    onehot = jnp.where(hit, 1.0, 0.0)
    sel[...] = onehot.astype(bf16)
    sel_t[...] = jnp.transpose(onehot).astype(bf16)

    def own_rows(zs, at_x):
        return pl.ds(pl.multiple_of(zs * GROUP * stripe + at_x * rows, rows), rows)

    def pull_copy(zs, g, c):
        return remote(
            stage.at[zs, g, :, :, lanes(c)], cols.at[quarter, :, own_rows(zs, x), lanes(c)],
            pull_s.at[0], pull_r.at[c], member(g),
        )

    def spread(slot, zs, c):
        size = chunks[c][1]
        picked = jnp.dot(
            sel[...], line_in[slot, :, :, lanes(c)].reshape(rows * block_total, size),
            preferred_element_type=f32,
        )
        stage[zs, :, :, :, lanes(c)] = picked.astype(bf16).reshape(PLANE, slots, rows, size)
        peers(lambda g: pull_copy(zs, g, c).start())
        cols[quarter, :, own_rows(zs, x), lanes(c)] = stage[zs, me, :, :, lanes(c)]

    for c in range(CHUNKS):
        spread(own_slot, z, c)

    prebuf[dp, :, :col] = pre_ref[...]

    def pre_copy(j):
        return remote(prebuf.at[dp], prebuf.at[dp], pre_s.at[0], pre_r.at[0], (section, j))

    others(dp_count, dp, lambda j: pre_copy(j).start())

    def soft(values, valid):
        masked = jnp.where(valid, values, -1e30)
        highest = jnp.max(masked, axis=-1, keepdims=True)
        expons = jnp.where(valid, jnp.exp(masked - highest), 0.0)
        return expons / jnp.sum(expons, axis=-1, keepdims=True)

    own_row = count_ref[...].astype(f32)
    own_lane = lax.broadcasted_iota(jnp.int32, own_row.shape, 1)
    how_many = jnp.sum(jnp.where(own_lane == dp, own_row, 0.0), axis=1, keepdims=True)
    slot_lane = lax.broadcasted_iota(jnp.int32, teacher_ref.shape, 1) // block
    valid = slot_lane.astype(f32) < how_many
    loads[1].wait()
    target[...] = soft(teacher_ref[...], valid)
    loads[0].wait()

    beside = (section, dp + 1 - 2 * core)

    def all_but_one(ref, send, recv):
        return remote(ref, ref, send, recv, beside)

    def slopes():
        all_but_one(prebuf.at[pl.ds(0, dp_count - 1)], pre_s.at[0], pre_r.at[0]).wait_recv()
        pre = jnp.concatenate([prebuf[j].astype(f32)[:, :col] for j in range(dp_count)], axis=1)
        sigma = 1.0 / (1.0 + jnp.exp(-pre))
        slope_ref[...] = sigma * (1.0 + pre * (1.0 - sigma))

    def hop(h):
        pl.when(h == hops - 1)(slopes)
        for c in range(CHUNKS):
            for d, came, further in ((0, z >= h + 1, z < z_count - 1), (1, z + h + 1 < z_count, z > 0)):
                @pl.when(came)
                def _():
                    line_wait(d, h, c).wait_recv()

                    @pl.when(further & (h + 1 < hops))
                    def _():
                        line_copy(d * hops + h, d, h + 1, c).start()

            def both(d):
                zs = z - (1 - 2 * d) * (h + 1)

                @pl.when((zs >= 0) & (zs < z_count))
                def _():
                    spread(d * hops + h, zs, c)

            each(2, both)

    each(hops, hop)

    contract_last = (((1,), (1,)), ((), ()))
    logits = jnp.zeros((block, slots * block), f32)

    def lane_cut(f, c):
        return pl.ds(pl.multiple_of(f * part + chunks[c][0], 128), chunks[c][1])

    for c, (offset, size) in enumerate(chunks):
        all_but_one(
            stage.at[:, pl.ds(0, PLANE - 1), :, :, lanes(c)], pull_s.at[0], pull_r.at[c]
        ).wait_recv()

        def quarter_logits(f, carry):
            return carry + lax.dot_general(
                q_ref[:, lane_cut(f, c)], cols[f, :, :, lanes(c)].reshape(slots * block, size),
                contract_last, preferred_element_type=f32,
            )

        logits = lax.fori_loop(0, 4, quarter_logits, logits)
    weights32 = soft(logits * INVERSE_TEMP, valid) - target[...]
    weights = weights32.astype(bf16)
    weights_t = jnp.transpose(weights32).astype(bf16)
    def push_copy(zt, g, c):
        return remote(
            terms.at[g % 4, :, own_rows(zt, g // 4), lanes(c)], tin.at[zt, me, :, :, lanes(c)],
            push_s.at[0], push_r.at[zt, c], member(g),
        )

    def push(zt, c):
        peers(lambda g: push_copy(zt, g, c).start())
        tin[zt, me, :, :, lanes(c)] = terms[quarter, :, own_rows(zt, x), lanes(c)]

    bits = max(1, (z_count - 1).bit_length())
    orders = [sorted(range(z_count), key=lambda t: (-abs(t - own), -abs(2 * t - z_count + 1))) for own in range(z_count)]

    def target_at(i):
        code = sum(
            ((orders[own][at] - own) % z_count) << (bits * (at * z_count + own))
            for at in range(z_count - 1) for own in range(z_count)
        )
        moved = lax.shift_right_logical(jnp.int32(code), (bits * (i * z_count + z)).astype(jnp.int32))
        return (z + moved % (1 << bits)) % z_count

    for c, (offset, size) in enumerate(chunks):
        def quarter_terms(f):
            sums = jnp.dot(weights_t, q_ref[:, lane_cut(f, c)], preferred_element_type=f32)
            terms[f, :, :, lanes(c)] = (
                (sums * INVERSE_TEMP).astype(bf16).reshape(slots, block, size)
            )

        each(4, quarter_terms)
        push(target_at(z * 0), c)

    def quarter_sums(f):
        sums = jnp.dot(weights, cols[f].reshape(slots * block, part), preferred_element_type=f32)
        sums = sums * INVERSE_TEMP
        span = pl.ds(pl.multiple_of(f * part, 128), part)
        qg_ref[:, span] = sums.astype(bf16)
        topbuf[dp, :, span] = sums[0:1]

    each(4, quarter_sums)
    qg_copy = pltpu.make_async_copy(qg_ref, qg_hbm, store_s.at[0])
    qg_copy.start()

    def top_copy(j):
        return remote(topbuf.at[dp], topbuf.at[dp], top_s.at[0], top_r.at[0], (section, j))

    @pl.when(section == 1)
    def _():
        others(dp_count, dp, lambda j: top_copy(j).start())

    def cot_copy(j):
        return remote(cbuf.at[dp], cbuf.at[dp], cot_s.at[0], cot_r.at[0], (1 - section, j))

    def layer(own):
        inner = (cot[...] * slope_ref[...]).astype(bf16)
        loads[2].wait()
        back = lax.dot_general(inner, w_ref[...], contract_last, preferred_element_type=f32)
        updated = own + back
        gi_ref[...] = updated
        inner_ref[...] = inner
        return updated

    def last_section():
        all_but_one(topbuf.at[pl.ds(0, dp_count - 1)], top_s.at[0], top_r.at[0]).wait_recv()
        own = jnp.zeros((micro, col), f32)
        for j in range(dp_count):
            cot[j:j + 1, :] = topbuf[j]
        for j in range(dp_count):
            own = jnp.where(dp == j, cot[:, j * col:(j + 1) * col], own)
        updated = layer(own)
        cbuf[dp, :, :col] = updated
        each(dp_count, lambda j: cot_copy(j).start())

    def summed(zt, c):
        all_but_one(
            tin.at[zt, pl.ds(0, PLANE - 1), :, :, lanes(c)], push_s.at[0], push_r.at[zt, c]
        ).wait_recv()
        size = chunks[c][1]
        return jnp.dot(
            sel_t[...], tin[zt, :, :, :, lanes(c)].reshape(total, size),
            preferred_element_type=f32,
        ).reshape(rows, block_total, size)

    def sum_copy(d, h, c, step):
        return remote(
            sum_out.at[d, h, :, :, lanes(c)], sum_in.at[d, h, :, :, lanes(c)],
            sum_s.at[d, h, c], sum_r.at[d, h, c], (section, dp + step * GROUP),
        )

    def fin_copy(i, c):
        return remote(
            fin.at[pl.ds((i % 2) * stripe, stripe), :, lanes(c)],
            final_in.at[quarter, :, :, lanes(c)],
            fin_s.at[0], fin_r.at[c], (i // 2, z * GROUP + x * 2 + i % 2),
        )

    def own_sum(value, c):
        zero = jnp.zeros_like(value)

        @pl.when(z > 0)
        def _():
            sum_copy(0, 0, c, -1).wait_recv()

        @pl.when(z < z_count - 1)
        def _():
            sum_copy(1, 0, c, 1).wait_recv()

        below = jnp.where(z > 0, sum_in[0, 0, :, :, lanes(c)].astype(f32), zero)
        above = jnp.where(z < z_count - 1, sum_in[1, 0, :, :, lanes(c)].astype(f32), zero)
        fin[:, :, lanes(c)] = (value + below + above).astype(bf16)
        others(4, quarter, lambda i: fin_copy(i, c).start())
        final_in[quarter, :, :, lanes(c)] = fin[pl.ds(core * stripe, stripe), :, lanes(c)]

    def turn(i):
        zt = target_at(i)
        d = 1 - (zt - z - 1 + z_count) // z_count
        step = 1 - 2 * d
        h = (zt - z) * step
        for c in range(CHUNKS):
            value = summed(zt, c)
            push(target_at(i + 1), c)
            sum_out[d, h - 1, :, :, lanes(c)] = value.astype(bf16)

            @pl.when(z != d * (z_count - 1))
            def _():
                sum_copy(d, h, c, -step).wait_recv()
                both = value + sum_in[d, h, :, :, lanes(c)].astype(f32)
                sum_out[d, h - 1, :, :, lanes(c)] = both.astype(bf16)

            sum_copy(d, h - 1, c, step).start()

        pl.when((section == 1) & (i == 0))(last_section)

    each(z_count - 1, turn)
    for c in range(CHUNKS):
        own_sum(summed(z, c), c)

    @pl.when(section == 0)
    def _():
        remote(cbuf, cbuf, cot_s.at[0], cot_r.at[0], (1 - section, dp)).wait_recv()
        cot[...] = jnp.concatenate([cbuf[j][:, :col] for j in range(dp_count)], axis=1)
        layer(cbuf[dp][:, :col])

    qg_copy.wait()
    cand_copy.wait_send()
    half_copy.wait_send()

    def line_sent(h):
        for c in range(CHUNKS):
            for d, begun, further in ((0, z >= h, z < z_count - 1), (1, z + h < z_count, z > 0)):
                @pl.when(begun & further)
                def _():
                    line_copy(own_slot, d, h, c).wait_send()

            for d, held in ((0, z + h + 1 < z_count), (1, z >= h + 1)):
                @pl.when(held)
                def _():
                    sum_copy(d, h, c, 1 - 2 * d).wait_send()

    each(hops, line_sent)
    seven = pl.ds(0, PLANE - 1)
    all_but_one(stage.at[:, seven], pull_s.at[0], pull_r.at[0]).wait_send()
    all_but_one(tin.at[:, seven], push_s.at[0], pull_r.at[0]).wait_send()
    fifteen = pl.ds(0, dp_count - 1)
    all_but_one(prebuf.at[fifteen], pre_s.at[0], pre_r.at[0]).wait_send()

    @pl.when(section == 1)
    def _():
        all_but_one(topbuf.at[fifteen], top_s.at[0], top_r.at[0]).wait_send()
        all_but_one(cbuf, cot_s.at[0], cot_r.at[0]).wait_send()

    for c in range(CHUNKS):
        all_but_one(
            final_in.at[pl.ds(0, 3), :, :, lanes(c)], fin_s.at[0], fin_r.at[c]
        ).wait_recv()
    for f in range(4):
        pg_ref[:, :, f * part:(f + 1) * part] = final_in[f]
    all_but_one(final_in.at[pl.ds(0, 3)], fin_s.at[0], fin_r.at[0]).wait_send()


def finish_kernel(
    qg_in, pg_in, gi_in, inner_ref, inp_ref, qg_out, pg_out, gi_ref, wg_out,
    qg, pg, wg, in_s, out_s,
):
    held = (qg, pg)
    takes = [
        pltpu.make_async_copy(source, ref, in_s.at[i])
        for i, (source, ref) in enumerate(zip((qg_in, pg_in), held))
    ]
    gives = [
        pltpu.make_async_copy(ref, dest, out_s.at[i])
        for i, (ref, dest) in enumerate(zip(held, (qg_out, pg_out)))
    ]
    for take in takes:
        take.start()
    gi_ref[...] = gi_in[...]
    part = inner_ref.shape[1] // 4
    for f in range(4):
        cut = pl.ds(f * part, part)
        wg[:, cut] = lax.dot_general(
            inp_ref[...], inner_ref[:, cut],
            (((0,), (0,)), ((), ())), preferred_element_type=jnp.float32,
        ).astype(wg.dtype)
        gives.append(pltpu.make_async_copy(wg.at[:, cut], wg_out.at[:, cut], out_s.at[2 + f]))
        gives[-1].start()
    for take, give in zip(takes, gives):
        take.wait()
        give.start()
    for give in gives:
        give.wait()


def plane_body(queries, passages, candidates, counts, teacher, section_weights, section_inputs, pre_acts):
    dp_count = lax.axis_size("dp")
    z_count = dp_count // GROUP
    stripe, block_total, width = passages.shape
    block = queries.shape[0]
    slots = candidates.shape[1]
    part = width // 4
    rows = 2 * stripe
    micro, col = section_inputs.shape[1:]
    wide = -(-col // 128) * 128
    f32, bf16, i32 = jnp.float32, jnp.bfloat16, jnp.int32
    table = candidates.T
    vmem, dma = pltpu.VMEM, pltpu.SemaphoreType.DMA
    hop = z_count - 1
    scratch = [
        vmem(queries.shape, bf16),
        vmem(teacher.shape, f32),
        vmem(section_weights.shape[1:], bf16),
        vmem(queries.shape, bf16),
        vmem((micro, width), f32),
        dma((3,)), dma((1,)),
        vmem(table.shape, i32),
        vmem((2 * hop + 1, rows, block_total, part), bf16),
        vmem((PLANE * slots * rows, rows * block_total), bf16),
        vmem((rows * block_total, PLANE * slots * rows), bf16),
        vmem((z_count, PLANE, slots, rows, part), bf16),
        vmem((4, slots, block, part), bf16),
        vmem((block, slots * block), f32),
        vmem((4, slots, block, part), bf16),
        vmem((z_count, PLANE, slots, rows, part), bf16),
        vmem((2, hop, rows, block_total, part), bf16),
        vmem((2, hop, rows, block_total, part), bf16),
        vmem((rows, block_total, part), bf16),
        vmem((4, stripe, block_total, part), bf16),
        vmem((dp_count, micro, wide), bf16),
        vmem((dp_count, 1, width), f32),
        vmem((dp_count, micro, wide), f32),
        vmem((micro, width), f32),
        dma((1,)), dma((1,)), dma((1,)), dma((1,)),
        dma((2, hop, CHUNKS)), dma((2, hop, CHUNKS)),
        dma((1,)), dma((CHUNKS,)),
        dma((1,)), dma((z_count, CHUNKS)),
        dma((2, hop, CHUNKS)), dma((2, hop, CHUNKS)),
        dma((1,)), dma((CHUNKS,)),
        dma((1,)), dma((1,)),
        dma((1,)), dma((1,)),
        dma((1,)), dma((1,)),
    ]
    here, there = pl.BlockSpec(memory_space=vmem), pl.BlockSpec(memory_space=pl.ANY)
    query_grads, passage_grads, grad_inputs, inner = pl.pallas_call(
        relay_kernel,
        out_shape=(
            jax.ShapeDtypeStruct(queries.shape, bf16),
            jax.ShapeDtypeStruct(passages.shape, bf16),
            jax.ShapeDtypeStruct((micro, col), f32),
            jax.ShapeDtypeStruct((micro, width), bf16),
        ),
        in_specs=[there, here, here, here, there, there, here],
        out_specs=(there, here, here, here),
        scratch_shapes=scratch,
        compiler_params=pltpu.CompilerParams(
            collective_id=0, has_side_effects=True, vmem_limit_bytes=56 * 1024 * 1024
        ),
    )(queries, passages, table, counts[None], teacher, section_weights[0], pre_acts[0])
    query_grads, passage_grads, grad_inputs, weight_grads = pl.pallas_call(
        finish_kernel,
        out_shape=(
            jax.ShapeDtypeStruct(queries.shape, bf16),
            jax.ShapeDtypeStruct(passages.shape, bf16),
            jax.ShapeDtypeStruct((micro, col), f32),
            jax.ShapeDtypeStruct(section_weights.shape[1:], bf16),
        ),
        in_specs=[there, there, here, here, here],
        out_specs=(there, there, here, there),
        scratch_shapes=[
            vmem(queries.shape, bf16),
            vmem(passages.shape, bf16),
            vmem(section_weights.shape[1:], bf16),
            dma((2,)), dma((6,)),
        ],
        compiler_params=pltpu.CompilerParams(vmem_limit_bytes=60 * 1024 * 1024),
    )(query_grads, passage_grads, grad_inputs, inner, section_inputs[0])
    return query_grads, passage_grads, grad_inputs[None], weight_grads[None]


def body(queries, passages, candidates, counts, teacher, section_weights, section_inputs, pre_acts):
    sections, dp_count = lax.axis_size("section"), lax.axis_size("dp")
    stripe, block_total, width = passages.shape
    by_planes = (
        sections == 2
        and dp_count == 16
        and stripe == 8
        and block_total == 16
        and width % 512 == 0
        and candidates.shape[0] == dp_count
        and candidates.shape[1] * dp_count * stripe == teacher.shape[1]
        and section_inputs.shape[1] == dp_count
    )
    chosen = plane_body if by_planes else general_body
    return chosen(
        queries, passages, candidates, counts, teacher, section_weights, section_inputs, pre_acts
    )


def solution(mesh):
    placed = (
        P(("section", "dp"), None),
        P("dp", None, None),
        P("section", None),
        P("section"),
        P(("section", "dp"), None),
        P("section", "dp", None),
        P("section", None, "dp"),
        P("section", None, "dp"),
    )
    return jax.shard_map(
        body,
        mesh=mesh,
        in_specs=placed,
        out_specs=(
            P(("section", "dp"), None),
            P("dp", None, None),
            P("section", None, "dp"),
            P("section", "dp", None),
        ),
        check_vma=False,
    )
```

```python
import functools

import jax
import jax.numpy as jnp
from jax import lax
from jax.experimental import pallas as pl
from jax.experimental.pallas import tpu as pltpu
from jax.sharding import PartitionSpec as P

INVERSE_TEMP = 20.0


def passed_along(value, axis, steps):
    count = lax.axis_size(axis)
    initial, last = (max(0, -steps), min(count, count - steps))
    return lax.ppermute(value, axis, [(source, source + steps) for source in range(initial, last)])


def soft_weights(logits, valid):
    masked = jnp.where(valid, logits, -1e30)
    highest = jnp.max(masked, axis=-1, keepdims=True)
    expons = jnp.where(valid, jnp.exp(masked - highest), 0.0)
    return expons / jnp.sum(expons, axis=-1, keepdims=True)


def general_body(queries, passages, candidates, counts, teacher, section_weights, section_inputs, pre_acts):
    dp_count = lax.axis_size("dp")
    dp_index = lax.axis_index("dp")
    stripe, block_total, width = passages.shape
    row_block_count = stripe * dp_count
    blocks_here = candidates.shape[0] // dp_count
    slot_count = candidates.shape[1]
    requests = blocks_here * slot_count
    all_slots = candidates.reshape(-1)
    outgoing = jnp.take(passages, all_slots, axis=1)
    pulled_rows = lax.all_to_all(outgoing, "dp", split_axis=1, concat_axis=0, tiled=True)
    pulled_rows = pulled_rows.reshape(row_block_count, blocks_here, slot_count, width)
    own_counts = lax.dynamic_slice_in_dim(counts, dp_index * blocks_here, blocks_here)
    slot_valid = jnp.arange(slot_count, dtype=jnp.int32)[None, :] < own_counts[:, None]
    column_valid = jnp.repeat(slot_valid, row_block_count, axis=1)[:, None, :]
    query_row_items = queries.reshape(blocks_here, row_block_count, width)
    logits = (
        jnp.einsum(
            "ixp,wifp->ixfw", query_row_items, pulled_rows, preferred_element_type=jnp.float32
        )
        * INVERSE_TEMP
    )
    logits = logits.reshape(blocks_here, row_block_count, slot_count * row_block_count)
    target_logits = soft_weights(
        teacher.reshape(blocks_here, row_block_count, slot_count * row_block_count), column_valid
    )
    weight_matrices = (soft_weights(logits, column_valid) - target_logits).astype(jnp.bfloat16)
    weight_matrices = weight_matrices.reshape(
        blocks_here, row_block_count, slot_count, row_block_count
    )
    query_sums = (
        jnp.einsum(
            "geal,lgay->gey", weight_matrices, pulled_rows, preferred_element_type=jnp.float32
        )
        * INVERSE_TEMP
    )
    passage_sums = (
        jnp.einsum(
            "fnyw,fnj->wfyj", weight_matrices, query_row_items, preferred_element_type=jnp.float32
        )
        * INVERSE_TEMP
    )
    block_terms = passage_sums.reshape(row_block_count, requests, width).astype(jnp.bfloat16)
    micro_count = section_inputs.shape[1] // dp_count
    col_width = width // dp_count
    micro_cols = jnp.transpose(
        query_sums[0, :micro_count].reshape(micro_count, dp_count, col_width), (1, 0, 2)
    )
    incoming_piece = lax.all_to_all(block_terms, "dp", split_axis=0, concat_axis=1, tiled=True)
    entry = lax.all_to_all(micro_cols, "dp", split_axis=0, concat_axis=1, tiled=True)
    onehot = (all_slots[:, None] == jnp.arange(block_total, dtype=jnp.int32)[None, :]).astype(
        jnp.float32
    )
    dense = jnp.einsum(
        "sjd,jn->snd",
        incoming_piece.astype(jnp.float32),
        onehot,
        precision=lax.Precision.HIGHEST,
        preferred_element_type=jnp.float32,
    )
    passage_out = lax.psum(dense, "section").astype(jnp.bfloat16)
    weight_rows = section_weights[0]
    input_cols = section_inputs[0]
    pre = pre_acts[0].astype(jnp.float32)
    sigma = jax.nn.sigmoid(pre)
    slope = sigma * (1.0 + pre * (1.0 - sigma))
    carry = entry.reshape(dp_count * micro_count, col_width)
    section_count = lax.axis_size("section")
    section_index = lax.axis_index("section")
    grad_cols = jnp.zeros_like(carry)
    grad_weight = jnp.zeros((col_width, width), jnp.float32)
    for section_turn in range(section_count):
        active_flag = section_count - 1 - section_turn
        inner = (carry * slope).astype(jnp.bfloat16)
        piece = lax.all_gather(inner, "dp", axis=1, tiled=True)
        back_sum = jnp.einsum("mj,ij->mi", piece, weight_rows, preferred_element_type=jnp.float32)
        weight_part = jnp.einsum("mi,mj->ij", input_cols, piece, preferred_element_type=jnp.float32)
        back_sum, layer_weight = (back_sum, weight_part)
        updated = carry + back_sum
        is_active = section_index == active_flag
        grad_cols = jnp.where(is_active, updated, grad_cols)
        grad_weight = jnp.where(is_active, layer_weight, grad_weight)
        if section_turn + 1 < section_count:
            carry = passed_along(updated, "section", -1)
    return (
        query_sums.reshape(blocks_here * row_block_count, width).astype(jnp.bfloat16),
        passage_out,
        grad_cols[None],
        grad_weight[None].astype(jnp.bfloat16),
    )


PLANE = 8
GROUP = 4


def chunks_of(width, count):
    lanes, edges = width // 128, [0]
    for i in range(count):
        edges.append(edges[-1] + -(-(lanes - edges[-1]) // (count - i)))
    return [(128 * a, 128 * (b - a)) for a, b in zip(edges, edges[1:])]


CHUNKS = 3


def cells(width, ref, index):
    return ref.at[:, :, pl.ds(pl.multiple_of(index * width, width), width)]


def relay_kernel(
    q_hbm, p_hbm, cand_ref, count_ref, teacher_hbm, w_hbm, pre_ref,
    qg_hbm, pg_hbm, gi_ref, inner_ref,
    p_ref, q_ref, teacher_ref, w_ref, qg_ref, slope_ref, load_s, store_s,
    candx, line_in, sel, sel_t, stage, cols, target, terms, tin,
    sum_out, sum_in, fin, final_in, prebuf, topbuf, cbuf, cot,
    cand_s, cand_r, half_s, half_r, line_s, line_r, pull_s, pull_r, push_s, push_r,
    sum_s, sum_r, fin_s, fin_r, pre_s, pre_r, top_s, top_r, cot_s, cot_r,
):
    dp_count = lax.axis_size("dp")
    section = lax.axis_index("section")
    dp = lax.axis_index("dp")
    z = dp // GROUP
    x = (dp // 2) % 2
    core = dp % 2
    me = x * 4 + section * 2 + core
    quarter = section * 2 + core
    z_count = dp_count // GROUP
    stripe, block_total, width = p_ref.shape
    part = width // 4
    rows = 2 * stripe
    block = q_ref.shape[0]
    slots = teacher_ref.shape[1] // block
    micro, col = pre_ref.shape
    f32, bf16 = jnp.float32, jnp.bfloat16
    chunks = chunks_of(part, CHUNKS)
    hops = z_count - 1
    own_slot = 2 * hops
    shard = line_in.at[own_slot]

    def lanes(c):
        return pl.ds(*chunks[c])

    def remote(source, dest, send, recv, device):
        return pltpu.make_async_remote_copy(
            src_ref=source, dst_ref=dest, send_sem=send, recv_sem=recv,
            device_id=device, device_id_type=pl.DeviceIdType.MESH,
        )

    def member(g):
        return ((g // 2) % 2, z * GROUP + (g // 4) * 2 + g % 2)

    def others(count, own, act):
        def step(i, carry):
            act((own + i) % count)
            return carry
        lax.fori_loop(1, count, step, 0)

    def peers(act):
        def step(j, carry):
            i = (j * 5) % PLANE
            act(
                (x + i // 4) % 2 * 4
                + (section + (i // 2) % 2) % 2 * 2
                + (core + i % 2) % 2
            )
            return carry
        lax.fori_loop(1, PLANE, step, 0)

    def each(count, act):
        def step(i, carry):
            act(i)
            return carry
        lax.fori_loop(0, count, step, 0)

    loads = [
        pltpu.make_async_copy(source, dest, load_s.at[i])
        for i, (source, dest) in enumerate(
            ((q_hbm, q_ref), (teacher_hbm, teacher_ref), (w_hbm, w_ref))
        )
    ]
    rows_in = [
        pltpu.make_async_copy(
            p_hbm.at[:, :, pl.ds(f * part, part)], p_ref.at[:, :, pl.ds(f * part, part)],
            load_s.at[len(loads) + f],
        )
        for f in range(4)
    ]
    for load in rows_in + loads:
        load.start()

    barrier = pltpu.get_barrier_semaphore()
    everyone = 2 * dp_count

    def greet(i):
        pl.semaphore_signal(
            barrier, inc=1, device_id=(i // dp_count, i % dp_count),
            device_id_type=pl.DeviceIdType.MESH,
        )

    others(everyone, section * dp_count + dp, greet)
    pl.semaphore_wait(barrier, everyone - 1)

    cand_copy = remote(cand_ref, candx, cand_s.at[0], cand_r.at[0], (1 - section, dp))
    cand_copy.start()
    partner = dp + 1 - 2 * core
    for load in rows_in:
        load.wait()
    half_copy = remote(
        cells(part, p_ref, section * 2 + 1 - core), shard.at[pl.ds(core * stripe, stripe)],
        half_s.at[0], half_r.at[0], (section, partner),
    )
    half_copy.start()
    shard[pl.ds(core * stripe, stripe)] = p_ref[
        :, :, pl.ds(pl.multiple_of(quarter * part, part), part)
    ]
    half_wait = remote(
        cells(part, p_ref, quarter), shard.at[pl.ds((1 - core) * stripe, stripe)],
        half_s.at[0], half_r.at[0], (section, partner),
    )
    half_wait.wait_recv()

    def line_copy(source, d, h, c):
        return remote(
            line_in.at[source, :, :, lanes(c)], line_in.at[d * hops + h, :, :, lanes(c)],
            line_s.at[d, h, c], line_r.at[d, h, c], (section, dp + (1 - 2 * d) * GROUP),
        )

    def line_wait(d, h, c):
        return remote(
            line_in.at[own_slot, :, :, lanes(c)], line_in.at[d * hops + h, :, :, lanes(c)],
            line_s.at[d, h, c], line_r.at[d, h, c], (section, dp - (1 - 2 * d) * GROUP),
        )

    for d, further in enumerate((z < z_count - 1, z > 0)):
        @pl.when(further)
        def _():
            for c in range(CHUNKS):
                line_copy(own_slot, d, 0, c).start()

    cand_copy.wait_recv()
    total = PLANE * slots * rows
    listed_shape = (total, dp_count)
    at_row = lax.broadcasted_iota(jnp.int32, listed_shape, 0)
    lane = lax.broadcasted_iota(jnp.int32, listed_shape, 1)
    g_of = at_row // (slots * rows)
    slot_of = (at_row // rows) % slots
    here = (g_of // 2) % 2 == section
    listed = jnp.zeros(listed_shape, f32)
    for slot in range(slots):
        mine = cand_ref[slot:slot + 1, :].astype(f32)
        away = candx[slot:slot + 1, :].astype(f32)
        listed = jnp.where(slot_of == slot, jnp.where(here, mine, away), listed)
    picked_lane = lane == z * GROUP + (g_of // 4) * 2 + g_of % 2
    wanted = jnp.sum(jnp.where(picked_lane, listed, 0.0), axis=1, keepdims=True)
    shape = (total, rows * block_total)
    row_of = lax.broadcasted_iota(jnp.int32, shape, 0) % rows
    place = lax.broadcasted_iota(jnp.int32, shape, 1)
    hit = (place // block_total == row_of) & ((place % block_total).astype(f32) == wanted)
    onehot = jnp.where(hit, 1.0, 0.0)
    sel[...] = onehot.astype(bf16)
    sel_t[...] = jnp.transpose(onehot).astype(bf16)

    def own_rows(zs, at_x):
        return pl.ds(pl.multiple_of(zs * GROUP * stripe + at_x * rows, rows), rows)

    def pull_copy(zs, g, c):
        return remote(
            stage.at[zs, g, :, :, lanes(c)], cols.at[quarter, :, own_rows(zs, x), lanes(c)],
            pull_s.at[0], pull_r.at[c], member(g),
        )

    def spread(slot, zs, c):
        size = chunks[c][1]
        picked = jnp.dot(
            sel[...], line_in[slot, :, :, lanes(c)].reshape(rows * block_total, size),
            preferred_element_type=f32,
        )
        stage[zs, :, :, :, lanes(c)] = picked.astype(bf16).reshape(PLANE, slots, rows, size)
        peers(lambda g: pull_copy(zs, g, c).start())
        cols[quarter, :, own_rows(zs, x), lanes(c)] = stage[zs, me, :, :, lanes(c)]

    for c in range(CHUNKS):
        spread(own_slot, z, c)

    prebuf[dp, :, :col] = pre_ref[...]

    def pre_copy(j):
        return remote(prebuf.at[dp], prebuf.at[dp], pre_s.at[0], pre_r.at[0], (section, j))

    others(dp_count, dp, lambda j: pre_copy(j).start())

    def soft(values, valid):
        masked = jnp.where(valid, values, -1e30)
        highest = jnp.max(masked, axis=-1, keepdims=True)
        expons = jnp.where(valid, jnp.exp(masked - highest), 0.0)
        return expons / jnp.sum(expons, axis=-1, keepdims=True)

    own_row = count_ref[...].astype(f32)
    own_lane = lax.broadcasted_iota(jnp.int32, own_row.shape, 1)
    how_many = jnp.sum(jnp.where(own_lane == dp, own_row, 0.0), axis=1, keepdims=True)
    slot_lane = lax.broadcasted_iota(jnp.int32, teacher_ref.shape, 1) // block
    valid = slot_lane.astype(f32) < how_many
    loads[1].wait()
    target[...] = soft(teacher_ref[...], valid)
    loads[0].wait()

    beside = (section, dp + 1 - 2 * core)

    def all_but_one(ref, send, recv):
        return remote(ref, ref, send, recv, beside)

    def slopes():
        all_but_one(prebuf.at[pl.ds(0, dp_count - 1)], pre_s.at[0], pre_r.at[0]).wait_recv()
        pre = jnp.concatenate([prebuf[j].astype(f32)[:, :col] for j in range(dp_count)], axis=1)
        sigma = 1.0 / (1.0 + jnp.exp(-pre))
        slope_ref[...] = sigma * (1.0 + pre * (1.0 - sigma))

    def hop(h):
        pl.when(h == hops - 1)(slopes)
        for c in range(CHUNKS):
            for d, came, further in ((0, z >= h + 1, z < z_count - 1), (1, z + h + 1 < z_count, z > 0)):
                @pl.when(came)
                def _():
                    line_wait(d, h, c).wait_recv()

                    @pl.when(further & (h + 1 < hops))
                    def _():
                        line_copy(d * hops + h, d, h + 1, c).start()

            def both(d):
                zs = z - (1 - 2 * d) * (h + 1)

                @pl.when((zs >= 0) & (zs < z_count))
                def _():
                    spread(d * hops + h, zs, c)

            each(2, both)

    each(hops, hop)

    contract_last = (((1,), (1,)), ((), ()))
    logits = jnp.zeros((block, slots * block), f32)

    def lane_cut(f, c):
        return pl.ds(pl.multiple_of(f * part + chunks[c][0], 128), chunks[c][1])

    for c, (offset, size) in enumerate(chunks):
        all_but_one(
            stage.at[:, pl.ds(0, PLANE - 1), :, :, lanes(c)], pull_s.at[0], pull_r.at[c]
        ).wait_recv()

        def quarter_logits(f, carry):
            return carry + lax.dot_general(
                q_ref[:, lane_cut(f, c)], cols[f, :, :, lanes(c)].reshape(slots * block, size),
                contract_last, preferred_element_type=f32,
            )

        logits = lax.fori_loop(0, 4, quarter_logits, logits)
    weights32 = soft(logits * INVERSE_TEMP, valid) - target[...]
    weights = weights32.astype(bf16)
    weights_t = jnp.transpose(weights32).astype(bf16)
    def push_copy(zt, g, c):
        return remote(
            terms.at[g % 4, :, own_rows(zt, g // 4), lanes(c)], tin.at[zt, me, :, :, lanes(c)],
            push_s.at[0], push_r.at[zt, c], member(g),
        )

    def push(zt, c):
        peers(lambda g: push_copy(zt, g, c).start())
        tin[zt, me, :, :, lanes(c)] = terms[quarter, :, own_rows(zt, x), lanes(c)]

    bits = max(1, (z_count - 1).bit_length())
    orders = [sorted(range(z_count), key=lambda t: (-abs(t - own), -abs(2 * t - z_count + 1))) for own in range(z_count)]

    def target_at(i):
        code = sum(
            ((orders[own][at] - own) % z_count) << (bits * (at * z_count + own))
            for at in range(z_count - 1) for own in range(z_count)
        )
        moved = lax.shift_right_logical(jnp.int32(code), (bits * (i * z_count + z)).astype(jnp.int32))
        return (z + moved % (1 << bits)) % z_count

    for c, (offset, size) in enumerate(chunks):
        def quarter_terms(f):
            sums = jnp.dot(weights_t, q_ref[:, lane_cut(f, c)], preferred_element_type=f32)
            terms[f, :, :, lanes(c)] = (
                (sums * INVERSE_TEMP).astype(bf16).reshape(slots, block, size)
            )

        each(4, quarter_terms)
        push(target_at(z * 0), c)

    def quarter_sums(f):
        sums = jnp.dot(weights, cols[f].reshape(slots * block, part), preferred_element_type=f32)
        sums = sums * INVERSE_TEMP
        span = pl.ds(pl.multiple_of(f * part, 128), part)
        qg_ref[:, span] = sums.astype(bf16)
        topbuf[dp, :, span] = sums[0:1]

    each(4, quarter_sums)
    qg_copy = pltpu.make_async_copy(qg_ref, qg_hbm, store_s.at[0])
    qg_copy.start()

    def top_copy(j):
        return remote(topbuf.at[dp], topbuf.at[dp], top_s.at[0], top_r.at[0], (section, j))

    @pl.when(section == 1)
    def _():
        others(dp_count, dp, lambda j: top_copy(j).start())

    def cot_copy(j):
        return remote(cbuf.at[dp], cbuf.at[dp], cot_s.at[0], cot_r.at[0], (1 - section, j))

    def layer(own):
        inner = (cot[...] * slope_ref[...]).astype(bf16)
        loads[2].wait()
        back = lax.dot_general(inner, w_ref[...], contract_last, preferred_element_type=f32)
        updated = own + back
        gi_ref[...] = updated
        inner_ref[...] = inner
        return updated

    def last_section():
        all_but_one(topbuf.at[pl.ds(0, dp_count - 1)], top_s.at[0], top_r.at[0]).wait_recv()
        own = jnp.zeros((micro, col), f32)
        for j in range(dp_count):
            cot[j:j + 1, :] = topbuf[j]
        for j in range(dp_count):
            own = jnp.where(dp == j, cot[:, j * col:(j + 1) * col], own)
        updated = layer(own)
        cbuf[dp, :, :col] = updated
        each(dp_count, lambda j: cot_copy(j).start())

    def summed(zt, c):
        all_but_one(
            tin.at[zt, pl.ds(0, PLANE - 1), :, :, lanes(c)], push_s.at[0], push_r.at[zt, c]
        ).wait_recv()
        size = chunks[c][1]
        return jnp.dot(
            sel_t[...], tin[zt, :, :, :, lanes(c)].reshape(total, size),
            preferred_element_type=f32,
        ).reshape(rows, block_total, size)

    def sum_copy(d, h, c, step):
        return remote(
            sum_out.at[d, h, :, :, lanes(c)], sum_in.at[d, h, :, :, lanes(c)],
            sum_s.at[d, h, c], sum_r.at[d, h, c], (section, dp + step * GROUP),
        )

    def fin_copy(i, c):
        return remote(
            fin.at[pl.ds((i % 2) * stripe, stripe), :, lanes(c)],
            final_in.at[quarter, :, :, lanes(c)],
            fin_s.at[0], fin_r.at[c], (i // 2, z * GROUP + x * 2 + i % 2),
        )

    def own_sum(value, c):
        zero = jnp.zeros_like(value)

        @pl.when(z > 0)
        def _():
            sum_copy(0, 0, c, -1).wait_recv()

        @pl.when(z < z_count - 1)
        def _():
            sum_copy(1, 0, c, 1).wait_recv()

        below = jnp.where(z > 0, sum_in[0, 0, :, :, lanes(c)].astype(f32), zero)
        above = jnp.where(z < z_count - 1, sum_in[1, 0, :, :, lanes(c)].astype(f32), zero)
        fin[:, :, lanes(c)] = (value + below + above).astype(bf16)
        others(4, quarter, lambda i: fin_copy(i, c).start())
        final_in[quarter, :, :, lanes(c)] = fin[pl.ds(core * stripe, stripe), :, lanes(c)]

    def turn(i):
        zt = target_at(i)
        d = 1 - (zt - z - 1 + z_count) // z_count
        step = 1 - 2 * d
        h = (zt - z) * step
        for c in range(CHUNKS):
            value = summed(zt, c)
            push(target_at(i + 1), c)
            sum_out[d, h - 1, :, :, lanes(c)] = value.astype(bf16)

            @pl.when(z != d * (z_count - 1))
            def _():
                sum_copy(d, h, c, -step).wait_recv()
                both = value + sum_in[d, h, :, :, lanes(c)].astype(f32)
                sum_out[d, h - 1, :, :, lanes(c)] = both.astype(bf16)

            sum_copy(d, h - 1, c, step).start()

        pl.when((section == 1) & (i == 0))(last_section)

    each(z_count - 1, turn)
    for c in range(CHUNKS):
        own_sum(summed(z, c), c)

    @pl.when(section == 0)
    def _():
        remote(cbuf, cbuf, cot_s.at[0], cot_r.at[0], (1 - section, dp)).wait_recv()
        cot[...] = jnp.concatenate([cbuf[j][:, :col] for j in range(dp_count)], axis=1)
        layer(cbuf[dp][:, :col])

    qg_copy.wait()
    cand_copy.wait_send()
    half_copy.wait_send()

    def line_sent(h):
        for c in range(CHUNKS):
            for d, begun, further in ((0, z >= h, z < z_count - 1), (1, z + h < z_count, z > 0)):
                @pl.when(begun & further)
                def _():
                    line_copy(own_slot, d, h, c).wait_send()

            for d, held in ((0, z + h + 1 < z_count), (1, z >= h + 1)):
                @pl.when(held)
                def _():
                    sum_copy(d, h, c, 1 - 2 * d).wait_send()

    each(hops, line_sent)
    seven = pl.ds(0, PLANE - 1)
    all_but_one(stage.at[:, seven], pull_s.at[0], pull_r.at[0]).wait_send()
    all_but_one(tin.at[:, seven], push_s.at[0], pull_r.at[0]).wait_send()
    fifteen = pl.ds(0, dp_count - 1)
    all_but_one(prebuf.at[fifteen], pre_s.at[0], pre_r.at[0]).wait_send()

    @pl.when(section == 1)
    def _():
        all_but_one(topbuf.at[fifteen], top_s.at[0], top_r.at[0]).wait_send()
        all_but_one(cbuf, cot_s.at[0], cot_r.at[0]).wait_send()

    rows_out = []
    for c in range(CHUNKS):
        all_but_one(
            final_in.at[pl.ds(0, 3), :, :, lanes(c)], fin_s.at[0], fin_r.at[c]
        ).wait_recv()
        for f in range(4):
            rows_out.append(pltpu.make_async_copy(
                final_in.at[f, :, :, lanes(c)],
                pg_hbm.at[:, :, pl.ds(f * part + chunks[c][0], chunks[c][1])],
                store_s.at[1 + c * 4 + f],
            ))
            rows_out[-1].start()
    for copy in rows_out:
        copy.wait()
    all_but_one(final_in.at[pl.ds(0, 3)], fin_s.at[0], fin_r.at[0]).wait_send()


def finish_kernel(
    qg_in, pg_in, gi_in, inner_ref, inp_ref, qg_out, pg_out, gi_ref, wg_out,
    qg, pg, wg, in_s, out_s,
):
    part = inner_ref.shape[1] // 4
    takes, gives = [], []
    for f in range(4):
        cut = pl.ds(f * part, part)
        for i, (source, ref, dest) in enumerate(((qg_in, qg, qg_out), (pg_in, pg, pg_out))):
            at = (slice(None),) * (len(ref.shape) - 1) + (cut,)
            takes.append(pltpu.make_async_copy(source.at[at], ref.at[at], in_s.at[2 * f + i]))
            gives.append(pltpu.make_async_copy(ref.at[at], dest.at[at], out_s.at[4 + 2 * f + i]))
    for take in takes:
        take.start()
    gi_ref[...] = gi_in[...]
    outer = []
    for f in range(4):
        cut = pl.ds(f * part, part)
        wg[:, cut] = lax.dot_general(
            inp_ref[...], inner_ref[:, cut],
            (((0,), (0,)), ((), ())), preferred_element_type=jnp.float32,
        ).astype(wg.dtype)
        outer.append(pltpu.make_async_copy(wg.at[:, cut], wg_out.at[:, cut], out_s.at[f]))
        outer[-1].start()
    for take, give in zip(takes, gives):
        take.wait()
        give.start()
    for give in gives + outer:
        give.wait()


def plane_body(queries, passages, candidates, counts, teacher, section_weights, section_inputs, pre_acts):
    dp_count = lax.axis_size("dp")
    z_count = dp_count // GROUP
    stripe, block_total, width = passages.shape
    block = queries.shape[0]
    slots = candidates.shape[1]
    part = width // 4
    rows = 2 * stripe
    micro, col = section_inputs.shape[1:]
    wide = -(-col // 128) * 128
    f32, bf16, i32 = jnp.float32, jnp.bfloat16, jnp.int32
    table = candidates.T
    vmem, dma = pltpu.VMEM, pltpu.SemaphoreType.DMA
    hop = z_count - 1
    scratch = [
        vmem(passages.shape, bf16),
        vmem(queries.shape, bf16),
        vmem(teacher.shape, f32),
        vmem(section_weights.shape[1:], bf16),
        vmem(queries.shape, bf16),
        vmem((micro, width), f32),
        dma((7,)), dma((1 + 4 * CHUNKS,)),
        vmem(table.shape, i32),
        vmem((2 * hop + 1, rows, block_total, part), bf16),
        vmem((PLANE * slots * rows, rows * block_total), bf16),
        vmem((rows * block_total, PLANE * slots * rows), bf16),
        vmem((z_count, PLANE, slots, rows, part), bf16),
        vmem((4, slots, block, part), bf16),
        vmem((block, slots * block), f32),
        vmem((4, slots, block, part), bf16),
        vmem((z_count, PLANE, slots, rows, part), bf16),
        vmem((2, hop, rows, block_total, part), bf16),
        vmem((2, hop, rows, block_total, part), bf16),
        vmem((rows, block_total, part), bf16),
        vmem((4, stripe, block_total, part), bf16),
        vmem((dp_count, micro, wide), bf16),
        vmem((dp_count, 1, width), f32),
        vmem((dp_count, micro, wide), f32),
        vmem((micro, width), f32),
        dma((1,)), dma((1,)), dma((1,)), dma((1,)),
        dma((2, hop, CHUNKS)), dma((2, hop, CHUNKS)),
        dma((1,)), dma((CHUNKS,)),
        dma((1,)), dma((z_count, CHUNKS)),
        dma((2, hop, CHUNKS)), dma((2, hop, CHUNKS)),
        dma((1,)), dma((CHUNKS,)),
        dma((1,)), dma((1,)),
        dma((1,)), dma((1,)),
        dma((1,)), dma((1,)),
    ]
    here, there = pl.BlockSpec(memory_space=vmem), pl.BlockSpec(memory_space=pl.ANY)
    query_grads, passage_grads, grad_inputs, inner = pl.pallas_call(
        relay_kernel,
        out_shape=(
            jax.ShapeDtypeStruct(queries.shape, bf16),
            jax.ShapeDtypeStruct(passages.shape, bf16),
            jax.ShapeDtypeStruct((micro, col), f32),
            jax.ShapeDtypeStruct((micro, width), bf16),
        ),
        in_specs=[there, there, here, here, there, there, here],
        out_specs=(there, there, here, here),
        scratch_shapes=scratch,
        compiler_params=pltpu.CompilerParams(
            collective_id=0, has_side_effects=True, vmem_limit_bytes=56 * 1024 * 1024
        ),
    )(queries, passages, table, counts[None], teacher, section_weights[0], pre_acts[0])
    query_grads, passage_grads, grad_inputs, weight_grads = pl.pallas_call(
        finish_kernel,
        out_shape=(
            jax.ShapeDtypeStruct(queries.shape, bf16),
            jax.ShapeDtypeStruct(passages.shape, bf16),
            jax.ShapeDtypeStruct((micro, col), f32),
            jax.ShapeDtypeStruct(section_weights.shape[1:], bf16),
        ),
        in_specs=[there, there, here, here, here],
        out_specs=(there, there, here, there),
        scratch_shapes=[
            vmem(queries.shape, bf16),
            vmem(passages.shape, bf16),
            vmem(section_weights.shape[1:], bf16),
            dma((8,)), dma((12,)),
        ],
        compiler_params=pltpu.CompilerParams(vmem_limit_bytes=60 * 1024 * 1024),
    )(query_grads, passage_grads, grad_inputs, inner, section_inputs[0])
    return query_grads, passage_grads, grad_inputs[None], weight_grads[None]


def body(queries, passages, candidates, counts, teacher, section_weights, section_inputs, pre_acts):
    sections, dp_count = lax.axis_size("section"), lax.axis_size("dp")
    stripe, block_total, width = passages.shape
    by_planes = (
        sections == 2
        and dp_count == 16
        and stripe == 8
        and block_total == 16
        and width % 512 == 0
        and candidates.shape[0] == dp_count
        and candidates.shape[1] * dp_count * stripe == teacher.shape[1]
        and section_inputs.shape[1] == dp_count
    )
    chosen = plane_body if by_planes else general_body
    return chosen(
        queries, passages, candidates, counts, teacher, section_weights, section_inputs, pre_acts
    )


def solution(mesh):
    placed = (
        P(("section", "dp"), None),
        P("dp", None, None),
        P("section", None),
        P("section"),
        P(("section", "dp"), None),
        P("section", "dp", None),
        P("section", None, "dp"),
        P("section", None, "dp"),
    )
    return jax.shard_map(
        body,
        mesh=mesh,
        in_specs=placed,
        out_specs=(
            P(("section", "dp"), None),
            P("dp", None, None),
            P("section", None, "dp"),
            P("section", "dp", None),
        ),
        check_vma=False,
    )
```

```python
import functools

import jax
import jax.numpy as jnp
from jax import lax
from jax.experimental import pallas as pl
from jax.experimental.pallas import tpu as pltpu
from jax.sharding import PartitionSpec as P

INVERSE_TEMP = 20.0


def passed_along(value, axis, steps):
    count = lax.axis_size(axis)
    initial, last = (max(0, -steps), min(count, count - steps))
    return lax.ppermute(value, axis, [(source, source + steps) for source in range(initial, last)])


def soft_weights(logits, valid):
    masked = jnp.where(valid, logits, -1e30)
    highest = jnp.max(masked, axis=-1, keepdims=True)
    expons = jnp.where(valid, jnp.exp(masked - highest), 0.0)
    return expons / jnp.sum(expons, axis=-1, keepdims=True)


def general_body(queries, passages, candidates, counts, teacher, section_weights, section_inputs, pre_acts):
    dp_count = lax.axis_size("dp")
    dp_index = lax.axis_index("dp")
    stripe, block_total, width = passages.shape
    row_block_count = stripe * dp_count
    blocks_here = candidates.shape[0] // dp_count
    slot_count = candidates.shape[1]
    requests = blocks_here * slot_count
    all_slots = candidates.reshape(-1)
    outgoing = jnp.take(passages, all_slots, axis=1)
    pulled_rows = lax.all_to_all(outgoing, "dp", split_axis=1, concat_axis=0, tiled=True)
    pulled_rows = pulled_rows.reshape(row_block_count, blocks_here, slot_count, width)
    own_counts = lax.dynamic_slice_in_dim(counts, dp_index * blocks_here, blocks_here)
    slot_valid = jnp.arange(slot_count, dtype=jnp.int32)[None, :] < own_counts[:, None]
    column_valid = jnp.repeat(slot_valid, row_block_count, axis=1)[:, None, :]
    query_row_items = queries.reshape(blocks_here, row_block_count, width)
    logits = (
        jnp.einsum(
            "ixp,wifp->ixfw", query_row_items, pulled_rows, preferred_element_type=jnp.float32
        )
        * INVERSE_TEMP
    )
    logits = logits.reshape(blocks_here, row_block_count, slot_count * row_block_count)
    target_logits = soft_weights(
        teacher.reshape(blocks_here, row_block_count, slot_count * row_block_count), column_valid
    )
    weight_matrices = (soft_weights(logits, column_valid) - target_logits).astype(jnp.bfloat16)
    weight_matrices = weight_matrices.reshape(
        blocks_here, row_block_count, slot_count, row_block_count
    )
    query_sums = (
        jnp.einsum(
            "geal,lgay->gey", weight_matrices, pulled_rows, preferred_element_type=jnp.float32
        )
        * INVERSE_TEMP
    )
    passage_sums = (
        jnp.einsum(
            "fnyw,fnj->wfyj", weight_matrices, query_row_items, preferred_element_type=jnp.float32
        )
        * INVERSE_TEMP
    )
    block_terms = passage_sums.reshape(row_block_count, requests, width).astype(jnp.bfloat16)
    micro_count = section_inputs.shape[1] // dp_count
    col_width = width // dp_count
    micro_cols = jnp.transpose(
        query_sums[0, :micro_count].reshape(micro_count, dp_count, col_width), (1, 0, 2)
    )
    incoming_piece = lax.all_to_all(block_terms, "dp", split_axis=0, concat_axis=1, tiled=True)
    entry = lax.all_to_all(micro_cols, "dp", split_axis=0, concat_axis=1, tiled=True)
    onehot = (all_slots[:, None] == jnp.arange(block_total, dtype=jnp.int32)[None, :]).astype(
        jnp.float32
    )
    dense = jnp.einsum(
        "sjd,jn->snd",
        incoming_piece.astype(jnp.float32),
        onehot,
        precision=lax.Precision.HIGHEST,
        preferred_element_type=jnp.float32,
    )
    passage_out = lax.psum(dense, "section").astype(jnp.bfloat16)
    weight_rows = section_weights[0]
    input_cols = section_inputs[0]
    pre = pre_acts[0].astype(jnp.float32)
    sigma = jax.nn.sigmoid(pre)
    slope = sigma * (1.0 + pre * (1.0 - sigma))
    carry = entry.reshape(dp_count * micro_count, col_width)
    section_count = lax.axis_size("section")
    section_index = lax.axis_index("section")
    grad_cols = jnp.zeros_like(carry)
    grad_weight = jnp.zeros((col_width, width), jnp.float32)
    for section_turn in range(section_count):
        active_flag = section_count - 1 - section_turn
        inner = (carry * slope).astype(jnp.bfloat16)
        piece = lax.all_gather(inner, "dp", axis=1, tiled=True)
        back_sum = jnp.einsum("mj,ij->mi", piece, weight_rows, preferred_element_type=jnp.float32)
        weight_part = jnp.einsum("mi,mj->ij", input_cols, piece, preferred_element_type=jnp.float32)
        back_sum, layer_weight = (back_sum, weight_part)
        updated = carry + back_sum
        is_active = section_index == active_flag
        grad_cols = jnp.where(is_active, updated, grad_cols)
        grad_weight = jnp.where(is_active, layer_weight, grad_weight)
        if section_turn + 1 < section_count:
            carry = passed_along(updated, "section", -1)
    return (
        query_sums.reshape(blocks_here * row_block_count, width).astype(jnp.bfloat16),
        passage_out,
        grad_cols[None],
        grad_weight[None].astype(jnp.bfloat16),
    )


PLANE = 8
GROUP = 4


def chunks_of(width, count):
    lanes, edges = width // 128, [0]
    for i in range(count):
        edges.append(edges[-1] + -(-(lanes - edges[-1]) // (count - i)))
    return [(128 * a, 128 * (b - a)) for a, b in zip(edges, edges[1:])]


CHUNKS = 2


def cells(width, ref, index):
    return ref.at[:, :, pl.ds(pl.multiple_of(index * width, width), width)]


def relay_kernel(
    q_hbm, p_hbm, cand_ref, count_ref, teacher_hbm, w_hbm, pre_ref,
    qg_hbm, pg_hbm, gi_ref, inner_ref,
    p_ref, q_ref, teacher_ref, w_ref, qg_ref, slope_ref, load_s, store_s,
    candx, line_in, sel, sel_t, stage, cols, target, terms, tin,
    sum_out, sum_in, fin, final_in, prebuf, topbuf, cbuf, cot,
    cand_s, cand_r, half_s, half_r, line_s, line_r, pull_s, pull_r, push_s, push_r,
    sum_s, sum_r, fin_s, fin_r, pre_s, pre_r, top_s, top_r, cot_s, cot_r,
):
    dp_count = lax.axis_size("dp")
    section = lax.axis_index("section")
    dp = lax.axis_index("dp")
    z = dp // GROUP
    x = (dp // 2) % 2
    core = dp % 2
    me = x * 4 + section * 2 + core
    quarter = section * 2 + core
    z_count = dp_count // GROUP
    stripe, block_total, width = p_ref.shape
    part = width // 4
    rows = 2 * stripe
    block = q_ref.shape[0]
    slots = teacher_ref.shape[1] // block
    micro, col = pre_ref.shape
    f32, bf16 = jnp.float32, jnp.bfloat16
    chunks = chunks_of(part, CHUNKS)
    hops = z_count - 1
    own_slot = 2 * hops
    shard = line_in.at[own_slot]

    def lanes(c):
        return pl.ds(*chunks[c])

    def remote(source, dest, send, recv, device):
        return pltpu.make_async_remote_copy(
            src_ref=source, dst_ref=dest, send_sem=send, recv_sem=recv,
            device_id=device, device_id_type=pl.DeviceIdType.MESH,
        )

    def member(g):
        return ((g // 2) % 2, z * GROUP + (g // 4) * 2 + g % 2)

    def others(count, own, act):
        def step(i, carry):
            act((own + i) % count)
            return carry
        lax.fori_loop(1, count, step, 0)

    def peers(act):
        def step(j, carry):
            i = (j * 5) % PLANE
            act(
                (x + i // 4) % 2 * 4
                + (section + (i // 2) % 2) % 2 * 2
                + (core + i % 2) % 2
            )
            return carry
        lax.fori_loop(1, PLANE, step, 0)

    def each(count, act):
        def step(i, carry):
            act(i)
            return carry
        lax.fori_loop(0, count, step, 0)

    loads = [
        pltpu.make_async_copy(source, dest, load_s.at[i])
        for i, (source, dest) in enumerate(
            ((q_hbm, q_ref), (teacher_hbm, teacher_ref), (w_hbm, w_ref))
        )
    ]
    rows_in = [
        pltpu.make_async_copy(
            p_hbm.at[:, :, pl.ds(f * part, part)], p_ref.at[:, :, pl.ds(f * part, part)],
            load_s.at[len(loads) + f],
        )
        for f in range(4)
    ]
    for load in rows_in + loads:
        load.start()

    barrier = pltpu.get_barrier_semaphore()
    everyone = 2 * dp_count

    def greet(i):
        pl.semaphore_signal(
            barrier, inc=1, device_id=(i // dp_count, i % dp_count),
            device_id_type=pl.DeviceIdType.MESH,
        )

    others(everyone, section * dp_count + dp, greet)
    pl.semaphore_wait(barrier, everyone - 1)

    cand_copy = remote(cand_ref, candx, cand_s.at[0], cand_r.at[0], (1 - section, dp))
    cand_copy.start()
    partner = dp + 1 - 2 * core
    for load in rows_in:
        load.wait()
    half_copy = remote(
        cells(part, p_ref, section * 2 + 1 - core), shard.at[pl.ds(core * stripe, stripe)],
        half_s.at[0], half_r.at[0], (section, partner),
    )
    half_copy.start()
    shard[pl.ds(core * stripe, stripe)] = p_ref[
        :, :, pl.ds(pl.multiple_of(quarter * part, part), part)
    ]
    half_wait = remote(
        cells(part, p_ref, quarter), shard.at[pl.ds((1 - core) * stripe, stripe)],
        half_s.at[0], half_r.at[0], (section, partner),
    )
    half_wait.wait_recv()

    def line_copy(source, d, h, c):
        return remote(
            line_in.at[source, :, :, lanes(c)], line_in.at[d * hops + h, :, :, lanes(c)],
            line_s.at[d, h, c], line_r.at[d, h, c], (section, dp + (1 - 2 * d) * GROUP),
        )

    def line_wait(d, h, c):
        return remote(
            line_in.at[own_slot, :, :, lanes(c)], line_in.at[d * hops + h, :, :, lanes(c)],
            line_s.at[d, h, c], line_r.at[d, h, c], (section, dp - (1 - 2 * d) * GROUP),
        )

    for d, further in enumerate((z < z_count - 1, z > 0)):
        @pl.when(further)
        def _():
            for c in range(CHUNKS):
                line_copy(own_slot, d, 0, c).start()

    cand_copy.wait_recv()
    total = PLANE * slots * rows
    listed_shape = (total, dp_count)
    at_row = lax.broadcasted_iota(jnp.int32, listed_shape, 0)
    lane = lax.broadcasted_iota(jnp.int32, listed_shape, 1)
    g_of = at_row // (slots * rows)
    slot_of = (at_row // rows) % slots
    here = (g_of // 2) % 2 == section
    listed = jnp.zeros(listed_shape, f32)
    for slot in range(slots):
        mine = cand_ref[slot:slot + 1, :].astype(f32)
        away = candx[slot:slot + 1, :].astype(f32)
        listed = jnp.where(slot_of == slot, jnp.where(here, mine, away), listed)
    picked_lane = lane == z * GROUP + (g_of // 4) * 2 + g_of % 2
    wanted = jnp.sum(jnp.where(picked_lane, listed, 0.0), axis=1, keepdims=True)
    shape = (total, rows * block_total)
    row_of = lax.broadcasted_iota(jnp.int32, shape, 0) % rows
    place = lax.broadcasted_iota(jnp.int32, shape, 1)
    hit = (place // block_total == row_of) & ((place % block_total).astype(f32) == wanted)
    onehot = jnp.where(hit, 1.0, 0.0)
    sel[...] = onehot.astype(bf16)
    sel_t[...] = jnp.transpose(onehot).astype(bf16)

    def own_rows(zs, at_x):
        return pl.ds(pl.multiple_of(zs * GROUP * stripe + at_x * rows, rows), rows)

    def pull_copy(zs, g, c):
        return remote(
            stage.at[zs, g, :, :, lanes(c)], cols.at[quarter, :, own_rows(zs, x), lanes(c)],
            pull_s.at[0], pull_r.at[c], member(g),
        )

    def spread(slot, zs, c):
        size = chunks[c][1]
        picked = jnp.dot(
            sel[...], line_in[slot, :, :, lanes(c)].reshape(rows * block_total, size),
            preferred_element_type=f32,
        )
        stage[zs, :, :, :, lanes(c)] = picked.astype(bf16).reshape(PLANE, slots, rows, size)
        peers(lambda g: pull_copy(zs, g, c).start())
        cols[quarter, :, own_rows(zs, x), lanes(c)] = stage[zs, me, :, :, lanes(c)]

    for c in range(CHUNKS):
        spread(own_slot, z, c)

    prebuf[dp, :, :col] = pre_ref[...]

    def pre_copy(j):
        return remote(prebuf.at[dp], prebuf.at[dp], pre_s.at[0], pre_r.at[0], (section, j))

    others(dp_count, dp, lambda j: pre_copy(j).start())

    def soft(values, valid):
        masked = jnp.where(valid, values, -1e30)
        highest = jnp.max(masked, axis=-1, keepdims=True)
        expons = jnp.where(valid, jnp.exp(masked - highest), 0.0)
        return expons / jnp.sum(expons, axis=-1, keepdims=True)

    own_row = count_ref[...].astype(f32)
    own_lane = lax.broadcasted_iota(jnp.int32, own_row.shape, 1)
    how_many = jnp.sum(jnp.where(own_lane == dp, own_row, 0.0), axis=1, keepdims=True)
    slot_lane = lax.broadcasted_iota(jnp.int32, teacher_ref.shape, 1) // block
    valid = slot_lane.astype(f32) < how_many
    loads[1].wait()
    target[...] = soft(teacher_ref[...], valid)
    loads[0].wait()

    beside = (section, dp + 1 - 2 * core)

    def all_but_one(ref, send, recv):
        return remote(ref, ref, send, recv, beside)

    def slopes():
        all_but_one(prebuf.at[pl.ds(0, dp_count - 1)], pre_s.at[0], pre_r.at[0]).wait_recv()
        pre = jnp.concatenate([prebuf[j].astype(f32)[:, :col] for j in range(dp_count)], axis=1)
        sigma = 1.0 / (1.0 + jnp.exp(-pre))
        slope_ref[...] = sigma * (1.0 + pre * (1.0 - sigma))

    def hop(h):
        pl.when(h == hops - 1)(slopes)
        for c in range(CHUNKS):
            for d, came, further in ((0, z >= h + 1, z < z_count - 1), (1, z + h + 1 < z_count, z > 0)):
                @pl.when(came)
                def _():
                    line_wait(d, h, c).wait_recv()

                    @pl.when(further & (h + 1 < hops))
                    def _():
                        line_copy(d * hops + h, d, h + 1, c).start()

            def both(d):
                zs = z - (1 - 2 * d) * (h + 1)

                @pl.when((zs >= 0) & (zs < z_count))
                def _():
                    spread(d * hops + h, zs, c)

            each(2, both)

    each(hops, hop)

    contract_last = (((1,), (1,)), ((), ()))
    logits = jnp.zeros((block, slots * block), f32)

    def lane_cut(f, c):
        return pl.ds(pl.multiple_of(f * part + chunks[c][0], 128), chunks[c][1])

    for c, (offset, size) in enumerate(chunks):
        all_but_one(
            stage.at[:, pl.ds(0, PLANE - 1), :, :, lanes(c)], pull_s.at[0], pull_r.at[c]
        ).wait_recv()

        def quarter_logits(f, carry):
            return carry + lax.dot_general(
                q_ref[:, lane_cut(f, c)], cols[f, :, :, lanes(c)].reshape(slots * block, size),
                contract_last, preferred_element_type=f32,
            )

        logits = lax.fori_loop(0, 4, quarter_logits, logits)
    weights32 = soft(logits * INVERSE_TEMP, valid) - target[...]
    weights = weights32.astype(bf16)
    weights_t = jnp.transpose(weights32).astype(bf16)
    def push_copy(zt, g, c):
        return remote(
            terms.at[g % 4, :, own_rows(zt, g // 4), lanes(c)], tin.at[zt, me, :, :, lanes(c)],
            push_s.at[0], push_r.at[zt, c], member(g),
        )

    def push(zt, c):
        peers(lambda g: push_copy(zt, g, c).start())
        tin[zt, me, :, :, lanes(c)] = terms[quarter, :, own_rows(zt, x), lanes(c)]

    bits = max(1, (z_count - 1).bit_length())
    orders = [sorted(range(z_count), key=lambda t: (-abs(t - own), -abs(2 * t - z_count + 1))) for own in range(z_count)]

    def target_at(i):
        code = sum(
            ((orders[own][at] - own) % z_count) << (bits * (at * z_count + own))
            for at in range(z_count - 1) for own in range(z_count)
        )
        moved = lax.shift_right_logical(jnp.int32(code), (bits * (i * z_count + z)).astype(jnp.int32))
        return (z + moved % (1 << bits)) % z_count

    for c, (offset, size) in enumerate(chunks):
        def quarter_terms(f):
            sums = jnp.dot(weights_t, q_ref[:, lane_cut(f, c)], preferred_element_type=f32)
            terms[f, :, :, lanes(c)] = (
                (sums * INVERSE_TEMP).astype(bf16).reshape(slots, block, size)
            )

        each(4, quarter_terms)
        push(target_at(z * 0), c)

    def quarter_sums(f):
        sums = jnp.dot(weights, cols[f].reshape(slots * block, part), preferred_element_type=f32)
        sums = sums * INVERSE_TEMP
        span = pl.ds(pl.multiple_of(f * part, 128), part)
        qg_ref[:, span] = sums.astype(bf16)
        topbuf[dp, :, span] = sums[0:1]

    each(4, quarter_sums)
    qg_copy = pltpu.make_async_copy(qg_ref, qg_hbm, store_s.at[0])
    qg_copy.start()

    def top_copy(j):
        return remote(topbuf.at[dp], topbuf.at[dp], top_s.at[0], top_r.at[0], (section, j))

    @pl.when(section == 1)
    def _():
        others(dp_count, dp, lambda j: top_copy(j).start())

    def cot_copy(j):
        return remote(cbuf.at[dp], cbuf.at[dp], cot_s.at[0], cot_r.at[0], (1 - section, j))

    def layer(own):
        inner = (cot[...] * slope_ref[...]).astype(bf16)
        loads[2].wait()
        back = lax.dot_general(inner, w_ref[...], contract_last, preferred_element_type=f32)
        updated = own + back
        gi_ref[...] = updated
        inner_ref[...] = inner
        return updated

    def last_section():
        all_but_one(topbuf.at[pl.ds(0, dp_count - 1)], top_s.at[0], top_r.at[0]).wait_recv()
        own = jnp.zeros((micro, col), f32)
        for j in range(dp_count):
            cot[j:j + 1, :] = topbuf[j]
        for j in range(dp_count):
            own = jnp.where(dp == j, cot[:, j * col:(j + 1) * col], own)
        updated = layer(own)
        cbuf[dp, :, :col] = updated
        each(dp_count, lambda j: cot_copy(j).start())

    def summed(zt, c):
        all_but_one(
            tin.at[zt, pl.ds(0, PLANE - 1), :, :, lanes(c)], push_s.at[0], push_r.at[zt, c]
        ).wait_recv()
        size = chunks[c][1]
        return jnp.dot(
            sel_t[...], tin[zt, :, :, :, lanes(c)].reshape(total, size),
            preferred_element_type=f32,
        ).reshape(rows, block_total, size)

    def sum_copy(d, h, c, step):
        return remote(
            sum_out.at[d, h, :, :, lanes(c)], sum_in.at[d, h, :, :, lanes(c)],
            sum_s.at[d, h, c], sum_r.at[d, h, c], (section, dp + step * GROUP),
        )

    def fin_copy(i, c):
        return remote(
            fin.at[pl.ds((i % 2) * stripe, stripe), :, lanes(c)],
            final_in.at[quarter, :, :, lanes(c)],
            fin_s.at[0], fin_r.at[c], (i // 2, z * GROUP + x * 2 + i % 2),
        )

    def own_sum(value, c):
        zero = jnp.zeros_like(value)

        @pl.when(z > 0)
        def _():
            sum_copy(0, 0, c, -1).wait_recv()

        @pl.when(z < z_count - 1)
        def _():
            sum_copy(1, 0, c, 1).wait_recv()

        below = jnp.where(z > 0, sum_in[0, 0, :, :, lanes(c)].astype(f32), zero)
        above = jnp.where(z < z_count - 1, sum_in[1, 0, :, :, lanes(c)].astype(f32), zero)
        fin[:, :, lanes(c)] = (value + below + above).astype(bf16)
        others(4, quarter, lambda i: fin_copy(i, c).start())
        final_in[quarter, :, :, lanes(c)] = fin[pl.ds(core * stripe, stripe), :, lanes(c)]

    def turn(i):
        zt = target_at(i)
        d = 1 - (zt - z - 1 + z_count) // z_count
        step = 1 - 2 * d
        h = (zt - z) * step
        for c in range(CHUNKS):
            value = summed(zt, c)
            push(target_at(i + 1), c)
            sum_out[d, h - 1, :, :, lanes(c)] = value.astype(bf16)

            @pl.when(z != d * (z_count - 1))
            def _():
                sum_copy(d, h, c, -step).wait_recv()
                both = value + sum_in[d, h, :, :, lanes(c)].astype(f32)
                sum_out[d, h - 1, :, :, lanes(c)] = both.astype(bf16)

            sum_copy(d, h - 1, c, step).start()

        pl.when((section == 1) & (i == 0))(last_section)

    each(z_count - 1, turn)
    for c in range(CHUNKS):
        own_sum(summed(z, c), c)

    @pl.when(section == 0)
    def _():
        remote(cbuf, cbuf, cot_s.at[0], cot_r.at[0], (1 - section, dp)).wait_recv()
        cot[...] = jnp.concatenate([cbuf[j][:, :col] for j in range(dp_count)], axis=1)
        layer(cbuf[dp][:, :col])

    qg_copy.wait()
    cand_copy.wait_send()
    half_copy.wait_send()

    def line_sent(h):
        for c in range(CHUNKS):
            for d, begun, further in ((0, z >= h, z < z_count - 1), (1, z + h < z_count, z > 0)):
                @pl.when(begun & further)
                def _():
                    line_copy(own_slot, d, h, c).wait_send()

            for d, held in ((0, z + h + 1 < z_count), (1, z >= h + 1)):
                @pl.when(held)
                def _():
                    sum_copy(d, h, c, 1 - 2 * d).wait_send()

    each(hops, line_sent)
    seven = pl.ds(0, PLANE - 1)
    all_but_one(stage.at[:, seven], pull_s.at[0], pull_r.at[0]).wait_send()
    all_but_one(tin.at[:, seven], push_s.at[0], pull_r.at[0]).wait_send()
    fifteen = pl.ds(0, dp_count - 1)
    all_but_one(prebuf.at[fifteen], pre_s.at[0], pre_r.at[0]).wait_send()

    @pl.when(section == 1)
    def _():
        all_but_one(topbuf.at[fifteen], top_s.at[0], top_r.at[0]).wait_send()
        all_but_one(cbuf, cot_s.at[0], cot_r.at[0]).wait_send()

    rows_out = []
    for c in range(CHUNKS):
        all_but_one(
            final_in.at[pl.ds(0, 3), :, :, lanes(c)], fin_s.at[0], fin_r.at[c]
        ).wait_recv()
        for f in range(4):
            rows_out.append(pltpu.make_async_copy(
                final_in.at[f, :, :, lanes(c)],
                pg_hbm.at[:, :, pl.ds(f * part + chunks[c][0], chunks[c][1])],
                store_s.at[1 + c * 4 + f],
            ))
            rows_out[-1].start()
    for copy in rows_out:
        copy.wait()
    all_but_one(final_in.at[pl.ds(0, 3)], fin_s.at[0], fin_r.at[0]).wait_send()


def finish_kernel(
    qg_in, pg_in, gi_in, inner_ref, inp_ref, qg_out, pg_out, gi_ref, wg_out,
    qg, pg, wg, in_s, out_s,
):
    part = inner_ref.shape[1] // 4
    takes, gives = [], []
    for f in range(4):
        cut = pl.ds(f * part, part)
        for i, (source, ref, dest) in enumerate(((qg_in, qg, qg_out), (pg_in, pg, pg_out))):
            at = (slice(None),) * (len(ref.shape) - 1) + (cut,)
            takes.append(pltpu.make_async_copy(source.at[at], ref.at[at], in_s.at[2 * f + i]))
            gives.append(pltpu.make_async_copy(ref.at[at], dest.at[at], out_s.at[4 + 2 * f + i]))
    for take in takes:
        take.start()
    gi_ref[...] = gi_in[...]
    outer = []
    for f in range(4):
        cut = pl.ds(f * part, part)
        wg[:, cut] = lax.dot_general(
            inp_ref[...], inner_ref[:, cut],
            (((0,), (0,)), ((), ())), preferred_element_type=jnp.float32,
        ).astype(wg.dtype)
        outer.append(pltpu.make_async_copy(wg.at[:, cut], wg_out.at[:, cut], out_s.at[f]))
        outer[-1].start()
    for take, give in zip(takes, gives):
        take.wait()
        give.start()
    for give in gives + outer:
        give.wait()


def plane_body(queries, passages, candidates, counts, teacher, section_weights, section_inputs, pre_acts):
    dp_count = lax.axis_size("dp")
    z_count = dp_count // GROUP
    stripe, block_total, width = passages.shape
    block = queries.shape[0]
    slots = candidates.shape[1]
    part = width // 4
    rows = 2 * stripe
    micro, col = section_inputs.shape[1:]
    wide = -(-col // 128) * 128
    f32, bf16, i32 = jnp.float32, jnp.bfloat16, jnp.int32
    table = candidates.T
    vmem, dma = pltpu.VMEM, pltpu.SemaphoreType.DMA
    hop = z_count - 1
    scratch = [
        vmem(passages.shape, bf16),
        vmem(queries.shape, bf16),
        vmem(teacher.shape, f32),
        vmem(section_weights.shape[1:], bf16),
        vmem(queries.shape, bf16),
        vmem((micro, width), f32),
        dma((7,)), dma((1 + 4 * CHUNKS,)),
        vmem(table.shape, i32),
        vmem((2 * hop + 1, rows, block_total, part), bf16),
        vmem((PLANE * slots * rows, rows * block_total), bf16),
        vmem((rows * block_total, PLANE * slots * rows), bf16),
        vmem((z_count, PLANE, slots, rows, part), bf16),
        vmem((4, slots, block, part), bf16),
        vmem((block, slots * block), f32),
        vmem((4, slots, block, part), bf16),
        vmem((z_count, PLANE, slots, rows, part), bf16),
        vmem((2, hop, rows, block_total, part), bf16),
        vmem((2, hop, rows, block_total, part), bf16),
        vmem((rows, block_total, part), bf16),
        vmem((4, stripe, block_total, part), bf16),
        vmem((dp_count, micro, wide), bf16),
        vmem((dp_count, 1, width), f32),
        vmem((dp_count, micro, wide), f32),
        vmem((micro, width), f32),
        dma((1,)), dma((1,)), dma((1,)), dma((1,)),
        dma((2, hop, CHUNKS)), dma((2, hop, CHUNKS)),
        dma((1,)), dma((CHUNKS,)),
        dma((1,)), dma((z_count, CHUNKS)),
        dma((2, hop, CHUNKS)), dma((2, hop, CHUNKS)),
        dma((1,)), dma((CHUNKS,)),
        dma((1,)), dma((1,)),
        dma((1,)), dma((1,)),
        dma((1,)), dma((1,)),
    ]
    here, there = pl.BlockSpec(memory_space=vmem), pl.BlockSpec(memory_space=pl.ANY)
    query_grads, passage_grads, grad_inputs, inner = pl.pallas_call(
        relay_kernel,
        out_shape=(
            jax.ShapeDtypeStruct(queries.shape, bf16),
            jax.ShapeDtypeStruct(passages.shape, bf16),
            jax.ShapeDtypeStruct((micro, col), f32),
            jax.ShapeDtypeStruct((micro, width), bf16),
        ),
        in_specs=[there, there, here, here, there, there, here],
        out_specs=(there, there, here, here),
        scratch_shapes=scratch,
        compiler_params=pltpu.CompilerParams(
            collective_id=0, has_side_effects=True, vmem_limit_bytes=56 * 1024 * 1024
        ),
    )(queries, passages, table, counts[None], teacher, section_weights[0], pre_acts[0])
    query_grads, passage_grads, grad_inputs, weight_grads = pl.pallas_call(
        finish_kernel,
        out_shape=(
            jax.ShapeDtypeStruct(queries.shape, bf16),
            jax.ShapeDtypeStruct(passages.shape, bf16),
            jax.ShapeDtypeStruct((micro, col), f32),
            jax.ShapeDtypeStruct(section_weights.shape[1:], bf16),
        ),
        in_specs=[there, there, here, here, here],
        out_specs=(there, there, here, there),
        scratch_shapes=[
            vmem(queries.shape, bf16),
            vmem(passages.shape, bf16),
            vmem(section_weights.shape[1:], bf16),
            dma((8,)), dma((12,)),
        ],
        compiler_params=pltpu.CompilerParams(vmem_limit_bytes=60 * 1024 * 1024),
    )(query_grads, passage_grads, grad_inputs, inner, section_inputs[0])
    return query_grads, passage_grads, grad_inputs[None], weight_grads[None]


def body(queries, passages, candidates, counts, teacher, section_weights, section_inputs, pre_acts):
    sections, dp_count = lax.axis_size("section"), lax.axis_size("dp")
    stripe, block_total, width = passages.shape
    by_planes = (
        sections == 2
        and dp_count == 16
        and stripe == 8
        and block_total == 16
        and width % 512 == 0
        and candidates.shape[0] == dp_count
        and candidates.shape[1] * dp_count * stripe == teacher.shape[1]
        and section_inputs.shape[1] == dp_count
    )
    chosen = plane_body if by_planes else general_body
    return chosen(
        queries, passages, candidates, counts, teacher, section_weights, section_inputs, pre_acts
    )


def solution(mesh):
    placed = (
        P(("section", "dp"), None),
        P("dp", None, None),
        P("section", None),
        P("section"),
        P(("section", "dp"), None),
        P("section", "dp", None),
        P("section", None, "dp"),
        P("section", None, "dp"),
    )
    return jax.shard_map(
        body,
        mesh=mesh,
        in_specs=placed,
        out_specs=(
            P(("section", "dp"), None),
            P("dp", None, None),
            P("section", None, "dp"),
            P("section", "dp", None),
        ),
        check_vma=False,
    )
```
